512 devices in a mesh: wide: 64 (over z, x, core), narrow: 8 (over y).
Axes of the slice: x: 4, y: 8, z: 8, core: 2. Of those that a mesh axis runs over, the one named last changes fastest.
Arguments:
- right_side: float32 [256, 512, 128], P('wide', 'narrow'), may hold values from -24 to 24
- alpha_coef: float32 [256, 512, 128], P('wide', 'narrow'), may hold values from 0.1 to 2
- beta_x: float32 [256, 512, 128], P('wide', 'narrow'), may hold values from 0.25 to 4
- beta_y: float32 [256, 512, 128], P('wide', 'narrow'), may hold values from 0.25 to 4
- beta_z: float32 [256, 512, 128], P('wide', 'narrow'), may hold values from 0.25 to 4
Outputs:
- solution_field: float32 [256, 512, 128], P('wide', 'narrow')
The draws below stay inside these ranges and needn't reach their ends.
All inputs are finite; a program needn't handle non-finite values.
Results may differ from the reference program's by a relative error of at most 0.00002.
Values sent between devices are 32-bit elements; how exact they have to be, the bound alone decides.
No kernel may reach another device: no remote copies, remote signals or barrier semaphores. Data moves between devices by JAX's collectives and lax.ppermute only.
A program may use at most 64 MiB of HBM per device.

```python
import math
import jax
import jax.numpy as jnp

NZ = 128
NX = 256
NY = 512


def draw_right_side(key, part):
    key = jax.random.fold_in(key, 11)
    values = 4.0 * jax.random.normal(key, (NX, NY, NZ), jnp.float32)
    return jnp.clip(values, -24.0, 24.0)


def steps_of(own_key, dims, cuts, low, high):
    def one(dim, parts):
        heights = jax.random.uniform(jax.random.fold_in(jax.random.fold_in(own_key, 6), dim), (parts,), jnp.float32, low / len(cuts), high / len(cuts))
        return jnp.repeat(jnp.exp(heights), dims[dim] // parts).reshape((-1,) + (1,) * (len(dims) - dim - 1))

    level = one(*cuts[0])
    for cut in cuts[1:]:
        level = level * one(*cut)
    return level


def setup_inputs(seed: int = 0) -> dict:
    keys = jax.random.split(jax.random.key(seed), 6)
    right_side = draw_right_side(jax.random.fold_in(keys[5], 71), 0)
    alpha_coef = jnp.clip(jnp.exp(math.log(2.0) - 2.9957323 * jax.random.uniform(keys[1], (NX, NY, NZ), jnp.float32) ** steps_of(keys[1], (NX, NY, NZ), ((0, 64), (1, 8)), -0.2, 0.2)), 0.1, 2.0)
    beta_x = jnp.clip(jnp.exp(math.log(4.0) - 2.7725887 * jax.random.uniform(keys[2], (NX, NY, NZ), jnp.float32) ** steps_of(keys[2], (NX, NY, NZ), ((0, 64), (1, 8)), -0.2, 0.2)), 0.25, 4.0)
    beta_y = jnp.clip(jnp.exp(math.log(4.0) - 2.7725887 * jax.random.uniform(keys[3], (NX, NY, NZ), jnp.float32) ** steps_of(keys[3], (NX, NY, NZ), ((0, 64), (1, 8)), -0.2, 0.2)), 0.25, 4.0)
    beta_z = jnp.clip(jnp.exp(math.log(4.0) - 2.7725887 * jax.random.uniform(keys[4], (NX, NY, NZ), jnp.float32) ** steps_of(keys[4], (NX, NY, NZ), ((0, 64), (1, 8)), -0.2, 0.2)), 0.25, 4.0)
    return {"right_side": right_side, "alpha_coef": alpha_coef, "beta_x": beta_x, "beta_y": beta_y, "beta_z": beta_z}


spectrum_low = 0.25
spectrum_high = 2.0


def average_cells(values):
    a, b, c = values.shape
    return values.reshape(a // 2, 2, b // 2, 2, c // 2, 2).mean(axis=(1, 3, 5))


def average_yz(values):
    a, b, c = values.shape
    return values.reshape(a, b // 2, 2, c // 2, 2).mean(axis=(2, 4))


def average_xz(values):
    a, b, c = values.shape
    return values.reshape(a // 2, 2, b, c // 2, 2).mean(axis=(1, 4))


def average_xy(values):
    a, b, c = values.shape
    return values.reshape(a // 2, 2, b // 2, 2, c).mean(axis=(1, 3))


def coarsen(raw):
    alpha, bxl, bxt, byl, byt, bzl = raw
    return (average_cells(alpha), average_yz(bxl[0::2]), average_yz(bxt),
            average_xz(byl[:, 0::2]), average_xz(byt), average_xy(bzl[:, :, 0::2]))


def make_coef(raw, scale):
    alpha, bxl, bxt, byl, byt, bzl = raw
    bxh = jnp.concatenate([bxl[1:], bxt], 0)
    byh = jnp.concatenate([byl[:, 1:], byt], 1)
    bzh = jnp.concatenate([bzl[:, :, 1:], jnp.zeros_like(bzl[:, :, :1])], 2)
    total = bxl + bxh + byl + byh + bzl + bzh
    inverse = 1.0 / (alpha + scale * total)
    return (alpha, bxl, bxh, byl, byh, bzl, bzh, scale, inverse)


def operate(field, near, coef):
    alpha, bxl, bxh, byl, byh, bzl, bzh, scale, inverse = coef
    below_x, above_x, below_y, above_y = near
    below_z = jnp.concatenate([jnp.zeros_like(field[:, :, :1]), field[:, :, :-1]], 2)
    above_z = jnp.concatenate([field[:, :, 1:], jnp.zeros_like(field[:, :, :1])], 2)
    flux = bxl * (field - below_x) + bxh * (field - above_x) + byl * (field - below_y) \
        + byh * (field - above_y) + bzl * (field - below_z) + bzh * (field - above_z)
    return alpha * field + scale * flux


def chebyshev(start, rhs, coef, degree, near_fn, from_zero):
    inverse = coef[8]
    theta = (spectrum_high + spectrum_low) / 2.0
    delta = (spectrum_high - spectrum_low) / 2.0
    sigma = theta / delta
    if from_zero:
        resid = rhs
    else:
        resid = rhs - operate(start, near_fn(start), coef)
    previous = start
    current = start + (1.0 / theta) * inverse * resid
    rho_prev = 1.0 / sigma
    for step in range(1, degree):
        resid = rhs - operate(current, near_fn(current), coef)
        rho_now = 1.0 / (2.0 * sigma - rho_prev)
        upcoming = current + (rho_now * rho_prev) * (current - previous) + (2.0 * rho_now / delta) * inverse * resid
        previous, current = current, upcoming
        rho_prev = rho_now
    return current


def whole_near(field):
    padded = jnp.pad(field, ((1, 1), (1, 1), (0, 0)))
    return (padded[:-2, 1:-1], padded[2:, 1:-1], padded[1:-1, :-2], padded[1:-1, 2:])


def expand(values):
    return jnp.repeat(jnp.repeat(jnp.repeat(values, 2, axis=0), 2, axis=1), 2, axis=2)


def reference(right_side, alpha_coef, beta_x, beta_y, beta_z):
    bxl = jnp.concatenate([jnp.zeros_like(beta_x[:1]), beta_x[1:]], 0)
    byl = jnp.concatenate([jnp.zeros_like(beta_y[:, :1]), beta_y[:, 1:]], 1)
    bzl = jnp.concatenate([jnp.zeros_like(beta_z[:, :, :1]), beta_z[:, :, 1:]], 2)
    bxt = jnp.zeros_like(beta_x[:1])
    byt = jnp.zeros_like(beta_y[:, :1])
    raw0 = (alpha_coef, bxl, bxt, byl, byt, bzl)
    coef0 = make_coef(raw0, 1.0)
    level0 = chebyshev(jnp.zeros_like(right_side), right_side, coef0, 3, whole_near, True)
    rhs1 = average_cells(right_side - operate(level0, whole_near(level0), coef0))
    raw1 = coarsen(raw0)
    coef1 = make_coef(raw1, 0.25)
    level1 = chebyshev(jnp.zeros_like(rhs1), rhs1, coef1, 3, whole_near, True)
    rhs2 = average_cells(rhs1 - operate(level1, whole_near(level1), coef1))
    raw2 = coarsen(raw1)
    coef2 = make_coef(raw2, 0.0625)
    coarse_error = chebyshev(jnp.zeros_like(rhs2), rhs2, coef2, 4, whole_near, True)
    level1 = chebyshev(level1 + expand(coarse_error), rhs1, coef1, 2, whole_near, False)
    level0 = chebyshev(level0 + expand(level1), right_side, coef0, 2, whole_near, False)
    return level0
```

```python
import functools

import jax
import jax.numpy as jnp
from jax import lax
from jax.experimental import pallas as pl
from jax.experimental.pallas import tpu as pltpu
from jax.sharding import PartitionSpec as P

F32 = jnp.float32
THETA = (2.0 + 0.25) / 2.0
DELTA = (2.0 - 0.25) / 2.0
SIGMA = THETA / DELTA
RHO = [1.0 / SIGMA]
for _step in range(3):
    RHO.append(1.0 / (2.0 * SIGMA - RHO[-1]))
MOMENTUM = [0.0] + [RHO[k] * RHO[k - 1] for k in range(1, 4)]
GAIN = [1.0 / THETA] + [2.0 * RHO[k] / DELTA for k in range(1, 4)]

PX, PY, PZ = 4, 64, 128
HY = 32
EY = PY + 2 * HY
PAD = 8
B, ALPHA, BX, BY, BZ = range(5)
ANY = pl.BlockSpec(memory_space=pl.ANY)
VMEM = pl.BlockSpec(memory_space=pltpu.VMEM)


def shape(*dims):
    return jax.ShapeDtypeStruct(dims, F32)


def params(mib=40):
    return pltpu.CompilerParams(vmem_limit_bytes=mib * 1024 * 1024)


def parity():
    return lax.rem(lax.axis_index("wide"), 2)


def lanes(rows):
    return lax.broadcasted_iota(jnp.int32, (rows, PZ), 1)


def moved(v, shift):
    return pltpu.roll(v, shift % PZ, 1)


def defect(x_ref, w_ref, q, wq, r0, n, reach):
    rows = pl.ds(PAD + r0, n)
    here = pl.ds(r0, n)
    x = x_ref[q, rows, :]
    total = w_ref[6, wq, here, :] - x
    total += w_ref[0, wq, here, :] * x_ref[q - 1, rows, :]
    total += w_ref[1, wq, here, :] * x_ref[q + 1, rows, :]
    total += w_ref[2, wq, here, :] * x_ref[q, pl.ds(PAD + r0 - 1, n), :]
    total += w_ref[3, wq, here, :] * x_ref[q, pl.ds(PAD + r0 + 1, n), :]
    total += w_ref[4, wq, here, :] * moved(x, reach)
    total += w_ref[5, wq, here, :] * moved(x, -reach)
    return x, total


def sweep(x_ref, prev_ref, w_ref, lo, hi, rows, reach, k, store, chunk, woff=0):
    def body(q, carry):
        for r0 in range(rows[0], rows[1], chunk):
            n = min(chunk, rows[1] - r0)
            x, z = defect(x_ref, w_ref, q, q + woff, r0, n, reach)
            new = x + GAIN[k] * z
            if k > 0:
                gap = x if prev_ref is None else x - prev_ref[q, pl.ds(PAD + r0, n), :]
                new += MOMENTUM[k] * gap
            store(q, r0, n, new)
        return carry

    lax.fori_loop(lo, hi, body, 0)


def into(ref):
    def store(q, r0, n, v):
        ref[q, pl.ds(PAD + r0, n), :] = v

    return store


def scaled(raw, b, x_ref, w_ref, lo, hi, rows, reach, scale, chunk, woff=0, d_ref=None, doff=0):
    alpha, bxl, byl, bzl = raw

    def body(q, carry):
        for r0 in range(0, rows, chunk):
            n = min(chunk, rows - r0)
            here = pl.ds(r0, n)
            x0, x1 = bxl(q, r0, n), bxl(q + 1, r0, n)
            y0, y1 = byl(q, r0, n), byl(q, r0 + 1, n)
            z0 = bzl(q, r0, n)
            z1 = moved(z0, -reach)
            d = alpha(q, r0, n) + scale * (x0 + x1 + y0 + y1 + z0 + z1)
            inside = d > 0.0
            inv = jnp.where(inside, 1.0 / jnp.where(inside, d, 1.0), 0.0)
            si = scale * inv
            wq = q + woff
            for a, f in enumerate((x0, x1, y0, y1, z0, z1)):
                w_ref[a, wq, here, :] = si * f
            c0 = inv * b(q, r0, n)
            w_ref[6, wq, here, :] = c0
            x_ref[q, pl.ds(PAD + r0, n), :] = c0 * (1.0 / THETA)
            if d_ref is not None:
                d_ref[q + doff, here, :] = d
        return carry

    lax.fori_loop(lo, hi, body, 0)


def clear_pads(ref, rows):
    ref[:, :PAD, :] = jnp.zeros((ref.shape[0], PAD, PZ), F32)
    ref[:, PAD + rows :, :] = jnp.zeros((ref.shape[0], PAD, PZ), F32)


def pair_lanes(v, reach):
    low = (lanes(v.shape[0]) & reach) == 0
    return v + jnp.where(low, moved(v, -reach), moved(v, reach))


def low_lanes(v, reach):
    low = (lanes(v.shape[0]) & reach) == 0
    return jnp.where(low, v, moved(v, reach))


def pair_rows(t_ref, rows):
    return t_ref[pl.ds(0, rows, 2), :] + t_ref[pl.ds(1, rows, 2), :]


def pack2(v0, v1):
    return jnp.where((lanes(v0.shape[0]) & 1) == 0, v0, v1)


def unpack2(v):
    even = (lanes(v.shape[0]) & 1) == 0
    return jnp.where(even, v, moved(v, 1)), jnp.where(even, moved(v, -1), v)


def pack4(items):
    place = lanes(items[0].shape[0]) & 3
    out = items[0]
    for i, item in enumerate(items[1:], 1):
        out = jnp.where(place == i, item, out)
    return out


def unpack4(v, i):
    place = lanes(v.shape[0]) & 3
    out = v
    for m in range(4):
        if m != i:
            out = jnp.where(place == m, moved(v, m - i), out)
    return out


def pack_kernel(b, al, bx, by, bz, a_out, lo_out, hi_out, xs_out):
    wide, narrow = lax.axis_index("wide"), lax.axis_index("narrow")
    par = lax.rem(wide, 2)
    row = lax.broadcasted_iota(jnp.int32, (PY, PZ), 0)
    first_row = jnp.logical_and(row == 0, jnp.broadcast_to(narrow, (PY, PZ)) == 0)
    first_x = jnp.broadcast_to(wide, (PY, PZ)) == 0
    first_z = lanes(PY) == 0
    for p in range(PX):
        vx = bx[p]
        if p == 0:
            vx = jnp.where(first_x, 0.0, vx)
        vy = jnp.where(first_row, 0.0, by[p])
        vz = jnp.where(first_z, 0.0, bz[p])
        for i, v in enumerate((b[p], al[p], vx, vy, vz)):
            a_out[i, p] = v
            lo_out[i, p] = v[:HY]
            hi_out[i, p] = v[PY - HY :]
            if p < 3:

                @pl.when(par == 0)
                def _():
                    xs_out[3 * i + p] = v

            if p > 0:

                @pl.when(par == 1)
                def _():
                    xs_out[3 * i + p - 1] = v

        if p == 3:
            xs_out[15] = vx


def corner_kernel(lo, hi, sw_out, xs_out):
    par = parity()
    for i in range(5):
        for p in range(PX):
            sw_out[i, p, :HY] = lo[i, p]
            sw_out[i, p, HY:] = hi[i, p]
            if p < 3:
                xs_out[3 * i + p, :HY] = lo[i, par + p]
                xs_out[3 * i + p, HY:] = hi[i, par + p]
    xs_out[15, :HY] = lo[BX, 3]
    xs_out[15, HY:] = hi[BX, 3]


def coarse_kernel(a, lo, hi, out, t):
    def line(i, planes):
        for ref, r0, n in ((lo, 0, HY), (a, HY, PY), (hi, HY + PY, HY)):
            v = ref[i, planes[0]]
            if len(planes) > 1:
                v = v + ref[i, planes[1]]
            t[pl.ds(r0, n), :] = v

    half = EY // 2
    got = []
    for c in range(2):
        both = (2 * c, 2 * c + 1)
        line(ALPHA, both)
        al = pair_lanes(pair_rows(t, half), 1) * 0.125
        line(BX, both[:1])
        bx = pair_lanes(pair_rows(t, half), 1) * 0.25
        line(BY, both)
        by = pair_lanes(t[pl.ds(0, half, 2), :], 1) * 0.25
        line(BZ, both)
        bz = low_lanes(pair_rows(t, half), 1) * 0.25
        got.append((al, bx, by, bz))
    for i in range(4):
        out[i] = pack2(got[0][i], got[1][i])


Q0 = 3


def fine_kernel(a, lo, hi, sw, xs, csw, cxs, send, xsend, pre, w_out, s, w, d, x, y, t, sems, out_sem):
    par = parity()
    copies = []

    def copy(src, dst):
        c = pltpu.make_async_copy(src, dst, sems.at[len(copies)])
        c.start()
        copies.append(c)

    own = pl.ds(PAD + HY, PY)
    low = pl.ds(PAD, HY)
    high = pl.ds(PAD + HY + PY, HY)
    block = pl.ds(Q0, PX)
    near = 7 * (1 - par)
    far = 7 * par
    extra = pl.ds(10 + par, 1)
    other = pl.ds(11 - par, 1)
    copy(a, s.at[:, block, own])
    copy(lo, s.at[:, block, low])
    copy(hi, s.at[:, block, high])
    copy(sw.at[:, pl.ds(par, 3)], s.at[:, pl.ds(near, 3), own])
    copy(sw.at[BX, pl.ds(3, 1)], s.at[BX, extra, own])
    copy(csw.at[:, pl.ds(par, 3), pl.ds(0, HY)], s.at[:, pl.ds(near, 3), low])
    copy(csw.at[:, pl.ds(par, 3), pl.ds(HY, HY)], s.at[:, pl.ds(near, 3), high])
    copy(csw.at[BX, pl.ds(3, 1), pl.ds(0, HY)], s.at[BX, extra, low])
    copy(csw.at[BX, pl.ds(3, 1), pl.ds(HY, HY)], s.at[BX, extra, high])
    for i in range(5):
        three = pl.ds(3 * i, 3)
        copy(xs.at[three], s.at[i, pl.ds(far, 3), own])
        copy(cxs.at[three, pl.ds(0, HY)], s.at[i, pl.ds(far, 3), low])
        copy(cxs.at[three, pl.ds(HY, HY)], s.at[i, pl.ds(far, 3), high])
    last = pl.ds(15, 1)
    copy(xs.at[last], s.at[BX, other, own])
    copy(cxs.at[last, pl.ds(0, HY)], s.at[BX, other, low])
    copy(cxs.at[last, pl.ds(HY, HY)], s.at[BX, other, high])
    for i in range(5):
        s[i, :, :PAD, :] = jnp.zeros((12, PAD, PZ), F32)
        s[i, :, PAD + EY :, :] = jnp.zeros((12, PAD, PZ), F32)
    clear_pads(x, EY)
    clear_pads(y, EY)
    for c in copies:
        c.wait()

    def raw(i):
        return lambda q, r0, n: s[i, q, pl.ds(PAD + r0, n), :]

    chunk = 32
    scaled((raw(ALPHA), raw(BX), raw(BY), raw(BZ)), raw(B), x, w, 0, 10, EY, 1, 1.0, chunk, d_ref=d)
    keep = pltpu.make_async_copy(w.at[:, pl.ds(2, 6), pl.ds(HY - 8, PY + 16)], w_out, out_sem)
    keep.start()
    rows = (0, EY)
    sweep(x, None, w, 1, 9, rows, 1, 1, into(y), chunk)
    sweep(y, x, w, 2, 8, rows, 1, 2, into(x), chunk)
    half = EY // 2
    got = []
    for c in range(2):
        for r0 in range(0, EY, chunk):
            v = 0.0
            for q in (Q0 + 2 * c, Q0 + 2 * c + 1):
                _, z = defect(x, w, q, q, r0, chunk, 1)
                v = v + d[q, pl.ds(r0, chunk), :] * z
            t[pl.ds(r0, chunk), :] = v
        got.append(pair_lanes(pair_rows(t, half), 1) * 0.125)
    mid = pl.ds(PAD + HY - 8, PY + 16)
    send[pl.ds(0, half), :] = pack2(got[0], got[1])
    send[pl.ds(half, PY + 16), :] = x[Q0 + 2 - par, mid, :]
    xsend[...] = x[Q0 + 1 + par, mid, :]
    for p in range(6):
        pre[p] = x[Q0 - 1 + p, mid, :]
    keep.wait()


R1 = EY // 2
R2 = EY // 4
C0 = 8


def middle_kernel(own, other, mine, its, rown, rother, rmine, rits, up, down, pre, w_out, coarse_out, rhs_out,
                  s, w, d, x, y, t, u, out_sem):
    par = parity()

    def place(i, e, v):
        v0, v1 = unpack2(v)
        s[i, 2 * e, pl.ds(PAD, R1), :] = v0
        s[i, 2 * e + 1, pl.ds(PAD, R1), :] = v1

    for i in range(5):
        s[i, :, :PAD, :] = jnp.zeros((21, PAD, PZ), F32)
        s[i, :, PAD + R1 :, :] = jnp.zeros((21, PAD, PZ), F32)
        s[i, 20, :, :] = jnp.zeros((R1 + 2 * PAD, PZ), F32)
    clear_pads(x, R1)
    clear_pads(y, R1)
    place(0, 4 + par, own[pl.ds(0, R1), :])
    place(0, 5 - par, other[pl.ds(0, R1), :])
    for i in range(4):
        place(i + 1, 4 + par, rown[i])
        place(i + 1, 5 - par, rother[i])
    for k in range(4):
        lower, upper = 3 - k, 6 + k
        e = jnp.where(par == 0, lower, upper)
        f = jnp.where(par == 0, upper, lower)
        place(0, e, mine[pl.ds(k * R1, R1), :])
        place(0, f, its[pl.ds(k * R1, R1), :])
        for i in range(4):
            place(i + 1, e, rmine[4 * k + i])
            place(i + 1, f, rits[4 * k + i])

    def raw(i):
        return lambda q, r0, n: s[i, q, pl.ds(PAD + r0, n), :]

    chunk = 32
    scaled((raw(1), raw(2), raw(3), raw(4)), raw(0), x, w, 0, 20, R1, 2, 0.25, chunk, d_ref=d)
    keep = pltpu.make_async_copy(w.at[:, pl.ds(C0 - 2, 8)], w_out, out_sem)
    keep.start()
    rows = (0, R1)
    sweep(x, None, w, 2, 18, rows, 2, 1, into(y), chunk)
    sweep(y, x, w, 3, 17, rows, 2, 2, into(x), chunk)
    for p in range(10):
        pre[p] = x[C0 - 3 + p, pl.ds(PAD, R1), :]

    def residual(c, carry):
        for r0 in range(0, R1, chunk):
            v = 0.0
            for k in range(2):
                q = 4 + 2 * c + k
                _, z = defect(x, w, q, q, r0, chunk, 2)
                v = v + d[q, pl.ds(r0, chunk), :] * z
            t[pl.ds(r0, chunk), :] = v
        rhs_out[c] = pair_lanes(pair_rows(t, R2), 2) * 0.125
        return carry

    lax.fori_loop(0, 6, residual, 0)

    def coarsen(c, carry):
        body = pl.ds(PAD, R1)

        def line(i, both):
            v = s[i, 2 * c, body, :]
            if both:
                v = v + s[i, 2 * c + 1, body, :]
            t[...] = v

        line(1, True)
        coarse_out[0, c] = pair_lanes(pair_rows(t, R2), 2) * 0.125
        line(2, False)
        coarse_out[1, c] = pair_lanes(pair_rows(t, R2), 2) * 0.25
        line(3, True)
        coarse_out[2, c] = pair_lanes(t[pl.ds(0, R2, 2), :], 2) * 0.25
        line(4, True)
        coarse_out[3, c] = low_lanes(pair_rows(t, R2), 2) * 0.25
        return carry

    lax.fori_loop(0, 10, coarsen, 0)

    def first(plane):
        c = plane + 4
        byl = coarse_out[2, c]
        u[...] = jnp.zeros(u.shape, F32)
        u[pl.ds(0, R2), :] = byl
        bzl = coarse_out[3, c]
        total = coarse_out[1, c] + coarse_out[1, c + 1] + byl + u[pl.ds(1, R2), :] + bzl + moved(bzl, -4)
        dd = coarse_out[0, c] + 0.0625 * total
        inside = dd > 0.0
        inv = jnp.where(inside, 1.0 / jnp.where(inside, dd, 1.0), 0.0)
        return inv * rhs_out[plane + 2] * (1.0 / THETA)

    up[...] = pack4([rhs_out[1 + 2], rhs_out[0 + 2], first(-1)])
    down[...] = pack4([rhs_out[0 + 2], rhs_out[1 + 2], first(2), coarse_out[1, 2 + 4]])
    keep.wait()


M0 = 5


def last_kernel(below, above, coarse, rhs, pre1_in, w1_in, pre0_in, sw, xs, w0_in, out,
                s, w2, x2, y2, pre1, w1, x1, y1, pre0, w0, x0, y0, t, sems):
    par = parity()
    copies = {}

    def copy(name, src, dst):
        c = pltpu.make_async_copy(src, dst, sems.at[len(copies)])
        c.start()
        copies[name] = c

    copy("pre1", pre1_in, pre1)
    copy("w1", w1_in, w1)
    copy("pre0", pre0_in, pre0.at[pl.ds(1, 6)])
    mid = PY + 16
    copy("sw", sw.at[pl.ds(R1, mid)], pre0.at[7 - 7 * par])
    copy("xs", xs.at[pl.ds(2 * R1, mid)], pre0.at[7 * par])
    copy("w0", w0_in, w0)

    body = pl.ds(PAD, R2)
    for i in range(5):
        clear_pads(s.at[i], R2)
    clear_pads(x2, R2)
    clear_pads(y2, R2)
    for c in range(10):
        for i in range(4):
            s[i + 1, c + 1, body, :] = coarse[i, c]
    lo, hi = below[...], above[...]
    s[0, 2, body, :] = unpack4(lo, 0)
    s[0, 1, body, :] = unpack4(lo, 1)
    for c in range(6):
        s[0, c + 3, body, :] = rhs[c]
    s[0, 9, body, :] = unpack4(hi, 0)
    s[0, 10, body, :] = unpack4(hi, 1)
    s[2, 11, body, :] = unpack4(hi, 3)

    def raw(i):
        return lambda q, r0, n: s[i, q, pl.ds(PAD + r0, n), :]

    scaled((raw(1), raw(2), raw(3), raw(4)), raw(0), x2, w2, 1, 11, R2, 4, 0.0625, R2)
    x2[0, body, :] = unpack4(lo, 2)
    x2[11, body, :] = unpack4(hi, 2)
    rows = (0, R2)
    sweep(x2, None, w2, 1, 11, rows, 4, 1, into(y2), R2)
    sweep(y2, x2, w2, 2, 10, rows, 4, 2, into(x2), R2)
    sweep(x2, y2, w2, 3, 9, rows, 4, 3, into(y2), R2)

    copies["pre1"].wait()
    clear_pads(x1, R1)
    clear_pads(y1, R1)
    for q in range(10):
        c = (q - 3) // 2 + M0
        v = y2[c, body, :]
        t[pl.ds(0, R2, 2), :] = v
        t[pl.ds(1, R2, 2), :] = v
        x1[q, pl.ds(PAD, R1), :] = pre1[q] + t[...]
    copies["w1"].wait()
    rows = (0, R1)
    sweep(x1, None, w1, 1, 9, rows, 2, 0, into(y1), 32, woff=-1)
    sweep(y1, x1, w1, 2, 8, rows, 2, 1, into(x1), 32, woff=-1)

    copies["pre0"].wait()
    copies["sw"].wait()
    copies["xs"].wait()
    clear_pads(x0, mid)
    clear_pads(y0, mid)
    for q in range(8):
        c = (q - 2) // 2 + 3 + 2 * par
        v = x1[c, pl.ds(PAD + 12, mid // 2), :]
        t0 = x0.at[q]
        t0[pl.ds(PAD, mid // 2, 2), :] = v
        t0[pl.ds(PAD + 1, mid // 2, 2), :] = v
        x0[q, pl.ds(PAD, mid), :] += pre0[q]
    copies["w0"].wait()
    sweep(x0, None, w0, 1, 7, (0, mid), 1, 0, into(y0), 40, woff=-1)

    def finish(q, r0, n, v):
        out[q - 2, pl.ds(r0 - 8, n), :] = v

    sweep(y0, x0, w0, 2, 6, (8, 8 + PY), 1, 1, finish, 32, woff=-1)


def swap(v, axis="wide"):
    count = lax.axis_size(axis)
    return lax.ppermute(v, axis, [(i, i ^ 1) for i in range(count)])


def across(v, chips):
    count = lax.axis_size("wide")
    step = 2 * chips - 1
    pairs = [(i, i + step) for i in range(1, count, 2) if i + step < count]
    pairs += [(i, i - step) for i in range(0, count, 2) if i - step >= 0]
    return lax.ppermute(v, "wide", pairs)


def shifted(v, axis, step):
    count = lax.axis_size(axis)
    return lax.ppermute(v, axis, [(i, i + step) for i in range(count) if 0 <= i + step < count])


def shards(right_side, alpha_coef, beta_x, beta_y, beta_z):
    a, ylo, yhi, xs = pl.pallas_call(
        pack_kernel,
        out_shape=(shape(5, PX, PY, PZ), shape(5, PX, HY, PZ), shape(5, PX, HY, PZ), shape(16, PY, PZ)),
        in_specs=[VMEM] * 5,
        out_specs=(VMEM,) * 4,
        compiler_params=params(),
        name="pack",
    )(right_side, alpha_coef, beta_x, beta_y, beta_z)
    lo = shifted(yhi, "narrow", 1)
    hi = shifted(ylo, "narrow", -1)
    xs = across(xs, 1)
    sw = swap(a)
    csw, cxs = pl.pallas_call(
        corner_kernel,
        out_shape=(shape(5, PX, 2 * HY, PZ), shape(16, 2 * HY, PZ)),
        in_specs=[VMEM] * 2,
        out_specs=(VMEM,) * 2,
        compiler_params=params(),
        name="corners",
    )(lo, hi)
    cxs = across(cxs, 1)
    csw = swap(csw)
    raw1 = pl.pallas_call(
        coarse_kernel,
        out_shape=shape(4, R1, PZ),
        in_specs=[VMEM] * 3,
        out_specs=VMEM,
        scratch_shapes=[pltpu.VMEM((EY, PZ), F32)],
        compiler_params=params(),
        name="coarse_coefficients",
    )(a, lo, hi)
    raw1_other = swap(raw1)
    pair = jnp.concatenate([raw1, raw1_other], 0)
    raw1_mine = jnp.concatenate([across(pair, 1), across(pair, 2)], 0)
    raw1_its = swap(raw1_mine)

    mid = PY + 16
    send, xsend, pre0, w0 = pl.pallas_call(
        fine_kernel,
        out_shape=(shape(R1 + mid, PZ), shape(mid, PZ), shape(6, mid, PZ), shape(7, 6, mid, PZ)),
        in_specs=[ANY] * 7,
        out_specs=(VMEM, VMEM, VMEM, ANY),
        scratch_shapes=[
            pltpu.VMEM((5, 12, EY + 2 * PAD, PZ), F32),
            pltpu.VMEM((7, 10, EY, PZ), F32),
            pltpu.VMEM((10, EY, PZ), F32),
            pltpu.VMEM((10, EY + 2 * PAD, PZ), F32),
            pltpu.VMEM((10, EY + 2 * PAD, PZ), F32),
            pltpu.VMEM((EY, PZ), F32),
            pltpu.SemaphoreType.DMA((27,)),
            pltpu.SemaphoreType.DMA,
        ],
        compiler_params=params(),
        name="level0_pre",
    )(a, lo, hi, sw, xs, csw, cxs)

    other = swap(send)
    pair = jnp.concatenate([send[:R1], other[:R1], xsend], 0)
    one = across(pair, 1)
    two = across(pair[: 2 * R1], 2)
    mine = jnp.concatenate([one[: 2 * R1], two], 0)
    its = swap(mine)

    up, down, pre1, w1, coarse, rhs = pl.pallas_call(
        middle_kernel,
        out_shape=(
            shape(R2, PZ), shape(R2, PZ), shape(10, R1, PZ), shape(7, 8, R1, PZ), shape(4, 10, R2, PZ),
            shape(6, R2, PZ),
        ),
        in_specs=[VMEM] * 8,
        out_specs=(VMEM, VMEM, VMEM, ANY, VMEM, VMEM),
        scratch_shapes=[
            pltpu.VMEM((5, 21, R1 + 2 * PAD, PZ), F32),
            pltpu.VMEM((7, 20, R1, PZ), F32),
            pltpu.VMEM((20, R1, PZ), F32),
            pltpu.VMEM((20, R1 + 2 * PAD, PZ), F32),
            pltpu.VMEM((20, R1 + 2 * PAD, PZ), F32),
            pltpu.VMEM((R1, PZ), F32),
            pltpu.VMEM((R2 + PAD, PZ), F32),
            pltpu.SemaphoreType.DMA,
        ],
        compiler_params=params(),
        name="level1_pre",
    )(send, other, mine, its, raw1, raw1_other, raw1_mine, raw1_its)

    below = shifted(up, "wide", 4)
    above = shifted(down, "wide", -4)
    return pl.pallas_call(
        last_kernel,
        out_shape=shape(PX, PY, PZ),
        in_specs=[VMEM] * 4 + [ANY] * 6,
        out_specs=VMEM,
        scratch_shapes=[
            pltpu.VMEM((5, 12, R2 + 2 * PAD, PZ), F32),
            pltpu.VMEM((7, 12, R2, PZ), F32),
            pltpu.VMEM((12, R2 + 2 * PAD, PZ), F32),
            pltpu.VMEM((12, R2 + 2 * PAD, PZ), F32),
            pltpu.VMEM((10, R1, PZ), F32),
            pltpu.VMEM((7, 8, R1, PZ), F32),
            pltpu.VMEM((10, R1 + 2 * PAD, PZ), F32),
            pltpu.VMEM((10, R1 + 2 * PAD, PZ), F32),
            pltpu.VMEM((8, mid, PZ), F32),
            pltpu.VMEM((7, 6, mid, PZ), F32),
            pltpu.VMEM((8, mid + 2 * PAD, PZ), F32),
            pltpu.VMEM((8, mid + 2 * PAD, PZ), F32),
            pltpu.VMEM((R1, PZ), F32),
            pltpu.SemaphoreType.DMA((6,)),
        ],
        compiler_params=params(),
        name="coarse_and_post",
    )(below, above, coarse, rhs, pre1, w1, pre0, other, one, w0)


def solution(mesh):
    spec = P("wide", "narrow", None)
    return jax.shard_map(shards, mesh=mesh, in_specs=(spec,) * 5, out_specs=spec, check_vma=False)
```

```python
import jax
import jax.numpy as jnp
from jax import lax
from jax.experimental import pallas as pl
from jax.experimental.pallas import tpu as pltpu
from jax.sharding import PartitionSpec as P

F32 = jnp.float32
THETA = (2.0 + 0.25) / 2.0
DELTA = (2.0 - 0.25) / 2.0
SIGMA = THETA / DELTA
RHO = [1.0 / SIGMA]
for _step in range(3):
    RHO.append(1.0 / (2.0 * SIGMA - RHO[-1]))
MOMENTUM = [0.0] + [RHO[k] * RHO[k - 1] for k in range(1, 4)]
GAIN = [1.0 / THETA] + [2.0 * RHO[k] / DELTA for k in range(1, 4)]

PX, PY, PZ = 4, 64, 128
HY = 8
EY = PY + 2 * HY
H1 = PY // 2
G1 = 16
R1 = H1 + 2 * G1
R2 = R1 // 2
RAW = 5 * PX * EY
SIDE = 5 * PX * HY
PAD = 8
B, ALPHA, BX, BY, BZ = range(5)
ANY = pl.BlockSpec(memory_space=pl.ANY)
VMEM = pl.BlockSpec(memory_space=pltpu.VMEM)
HBM = pl.BlockSpec(memory_space=pltpu.HBM)


def shape(*dims):
    return jax.ShapeDtypeStruct(dims, F32)


def scratch(*dims):
    return pltpu.VMEM(dims, F32)


def call(kernel, name, out_shape, out_specs, in_specs, scratch_shapes, flops, mib=24, aliases=None):
    return pl.pallas_call(
        kernel,
        out_shape=out_shape,
        in_specs=in_specs,
        out_specs=out_specs,
        scratch_shapes=scratch_shapes,
        compiler_params=pltpu.CompilerParams(vmem_limit_bytes=mib * 1024 * 1024),
        cost_estimate=pl.CostEstimate(flops=flops, bytes_accessed=0, transcendentals=0),
        input_output_aliases=aliases or {},
        name=name,
    )


def parity():
    return lax.rem(lax.axis_index("wide"), 2)


def lanes(rows):
    return lax.broadcasted_iota(jnp.int32, (rows, PZ), 1)


def moved(v, shift):
    return pltpu.roll(v, shift % PZ, 1)


def planes(lo, hi, each, unroll):
    steps = (hi - lo) // unroll

    def body(i, carry):
        for k in range(unroll):
            each(lo + i * unroll + k)
        return carry

    if steps > 1:
        lax.fori_loop(0, steps, body, 0)
    else:
        steps = 0
    for q in range(lo + steps * unroll, hi):
        each(q)


def defect(x_ref, c_ref, w_ref, q, r0, n, reach, cq, cr, wq, wr):
    rows = pl.ds(PAD + r0, n)
    here = pl.ds(wr + r0, n)
    x = x_ref[q, rows, :]
    total = c_ref[cq, pl.ds(cr + r0, n), :] - x
    total += w_ref[0, wq, here, :] * x_ref[q - 1, rows, :]
    total += w_ref[1, wq, here, :] * x_ref[q + 1, rows, :]
    total += w_ref[2, wq, here, :] * x_ref[q, pl.ds(PAD + r0 - 1, n), :]
    total += w_ref[3, wq, here, :] * x_ref[q, pl.ds(PAD + r0 + 1, n), :]
    total += w_ref[4, wq, here, :] * moved(x, reach)
    total += w_ref[5, wq, here, :] * moved(x, -reach)
    return x, total


def sweep(x_ref, prev_ref, c_ref, w_ref, lo, hi, rows, reach, k, store, chunk, woff=0, coff=0, wr=0, cr=0, unroll=8):
    def each(q):
        for r0 in range(rows[0], rows[1], chunk):
            n = min(chunk, rows[1] - r0)
            x, z = defect(x_ref, c_ref, w_ref, q, r0, n, reach, q + coff, cr, q + woff, wr)
            new = x + GAIN[k] * z
            if k > 0:
                gap = x if prev_ref is None else x - prev_ref[q, pl.ds(PAD + r0, n), :]
                new += MOMENTUM[k] * gap
            store(q, r0, n, new)

    planes(lo, hi, each, unroll)


def into(ref):
    def store(q, r0, n, v):
        ref[q, pl.ds(PAD + r0, n), :] = v

    return store


def inverse(d):
    inside = d > 0.0
    return jnp.where(inside, 1.0 / jnp.where(inside, d, 1.0), 0.0)


def faces(alpha, x0, x1, y0, y1, z0, reach, scale):
    z1 = moved(z0, -reach)
    d = alpha + scale * (x0 + x1 + y0 + y1 + z0 + z1)
    inv = inverse(d)
    si = scale * inv
    return d, inv, [si * f for f in (x0, x1, y0, y1, z0, z1)]


def next_rows(load, r0, n, rows):
    if r0 + n < rows:
        return load(r0 + 1, n)
    return pltpu.roll(load(r0, n), n - 1, 0)


def clear_pads(ref, rows):
    ref[:, :PAD, :] = jnp.zeros((ref.shape[0], PAD, PZ), F32)
    ref[:, PAD + rows :, :] = jnp.zeros((ref.shape[0], PAD, PZ), F32)


def pair_lanes(v, reach):
    low = (lanes(v.shape[0]) & reach) == 0
    return v + jnp.where(low, moved(v, -reach), moved(v, reach))


def low_lanes(v, reach):
    low = (lanes(v.shape[0]) & reach) == 0
    return jnp.where(low, v, moved(v, reach))


def pack2(v0, v1):
    return jnp.where((lanes(v0.shape[0]) & 1) == 0, v0, v1)


def unpack2(v):
    even = (lanes(v.shape[0]) & 1) == 0
    return jnp.where(even, v, moved(v, 1)), jnp.where(even, moved(v, -1), v)


def pack4(items):
    place = lanes(items[0].shape[0]) & 3
    out = items[0]
    for i, item in enumerate(items[1:], 1):
        out = jnp.where(place == i, item, out)
    return out


def unpack4(v, i):
    place = lanes(v.shape[0]) & 3
    out = v
    for m in range(4):
        if m != i:
            out = jnp.where(place == m, moved(v, m - i), out)
    return out


def coarser(load, rows, reach):
    def cell(i):
        return load(i, 0, 0) + load(i, 0, 1) + load(i, 1, 0) + load(i, 1, 1)

    al = pair_lanes(cell(0), reach) * 0.125
    bx = pair_lanes(load(1, 0, 0) + load(1, 0, 1), reach) * 0.25
    by = pair_lanes(load(2, 0, 0) + load(2, 1, 0), reach) * 0.25
    bz = low_lanes(cell(3), reach) * 0.25
    return al, bx, by, bz


def pack_kernel(b, al, bx, by, bz, a, lo_out, hi_out, xs_out, raw, sems):
    wide, narrow = lax.axis_index("wide"), lax.axis_index("narrow")
    par = lax.rem(wide, 2)
    copies = [pltpu.make_async_copy(ref, a.at[i], sems.at[i]) for i, ref in enumerate((b, al, bx, by, bz))]
    for c in copies:
        c.start()
    for c in copies:
        c.wait()
    row = lax.broadcasted_iota(jnp.int32, (PAD, PZ), 0)
    first_row = jnp.logical_and(row == 0, jnp.broadcast_to(narrow, (PAD, PZ)) == 0)
    a[BX, 0] = jnp.where(jnp.broadcast_to(wide, (PY, PZ)) == 0, 0.0, a[BX, 0])
    first_z = lanes(PY) == 0
    for p in range(PX):
        a[BY, p, :PAD] = jnp.where(first_row, 0.0, a[BY, p, :PAD])
        a[BZ, p] = jnp.where(first_z, 0.0, a[BZ, p])
    got = []
    for c in range(2):

        def load(i, k, row):
            return a[i + 1, 2 * c + k, pl.ds(row, H1, 2), :]

        got.append(coarser(load, H1, 1))
    for i in range(4):
        v = pack2(got[0][i], got[1][i])
        raw[i] = v
        lo_out[pl.ds(SIDE + G1 * i, G1), :] = v[:G1]
        hi_out[pl.ds(SIDE + G1 * i, G1), :] = v[H1 - G1 :]
    for i in range(5):
        for p in range(PX):
            here = pl.ds((PX * i + p) * HY, HY)
            lo_out[here, :] = a[i, p, :HY]
            hi_out[here, :] = a[i, p, PY - HY :]
        for p in range(3):
            xs_out[3 * i + p] = a[i, par + p]
    xs_out[15] = a[BX, 3]


def corner_kernel(a, raw, lo, hi, _, sw, xs):
    par = parity()
    for i in range(5):
        for p in range(PX):
            k = PX * i + p
            sw[pl.ds(k * EY, HY), :] = lo[pl.ds(k * HY, HY), :]
            sw[pl.ds(k * EY + HY, PY), :] = a[i, p]
            sw[pl.ds(k * EY + HY + PY, HY), :] = hi[pl.ds(k * HY, HY), :]
        for p in range(3):
            here = pl.ds(pl.multiple_of((PX * i + p + par) * HY, HY), HY)
            xs[3 * i + p, :HY] = lo[here, :]
            xs[3 * i + p, HY:] = hi[here, :]
    here = pl.ds((PX * BX + 3) * HY, HY)
    xs[15, :HY] = lo[here, :]
    xs[15, HY:] = hi[here, :]
    for i in range(4):
        here = pl.ds(SIDE + G1 * i, G1)
        base = RAW + R1 * i
        sw[pl.ds(base, G1), :] = lo[here, :]
        sw[pl.ds(base + G1, H1), :] = raw[i]
        sw[pl.ds(base + G1 + H1, G1), :] = hi[here, :]


Q0 = 3


def fine_kernel(own, sw, xs, cxs, rhs, rhs_lo, rhs_hi, edge, xedge, pre, w, cc, sx, sf, d, x, y, z, t):
    par = parity()
    near = 7 * (1 - par)
    far = 7 * par

    def plane(ref, k, r0=0, n=EY):
        return ref[pl.ds(pl.multiple_of(k * EY + r0, 8) if (r0 % 8 == 0) else k * EY + r0, n), :]

    for p in range(PX):
        sx[Q0 + p] = plane(own, PX * BX + p)
    for k in range(3):
        sx[near + k] = plane(sw, PX * BX + par + k)
    sx[10 + par] = plane(sw, PX * BX + 3)

    def joined(dst, i):
        dst[:HY] = cxs[i, :HY]
        dst[HY : HY + PY] = xs[i]
        dst[HY + PY :] = cxs[i, HY:]

    for k in range(3):
        joined(sx.at[far + k], 3 * BX + k)
    joined(sx.at[11 - par], 15)
    for j, i in enumerate((B, ALPHA, BY, BZ)):
        for k in range(3):
            joined(sf.at[3 * j + k], 3 * i + k)
    clear_pads(x, EY)
    clear_pads(y, EY)
    chunk = 40

    def prepare(q, get):
        for r0 in range(0, EY, chunk):
            here = pl.ds(r0, chunk)

            def load(i):
                return lambda r, n: get(i, r, n)

            dd, inv, w6 = faces(
                load(ALPHA)(r0, chunk), sx[q, here, :], sx[q + 1, here, :], load(BY)(r0, chunk),
                next_rows(load(BY), r0, chunk, EY), load(BZ)(r0, chunk), 1, 1.0,
            )
            for a, f in enumerate(w6):
                w[a, q, here, :] = f
            c0 = inv * load(B)(r0, chunk)
            cc[q, here, :] = c0
            x[q, pl.ds(PAD + r0, chunk), :] = c0 * (1.0 / THETA)
            d[q, here, :] = dd

    for p in range(PX):
        prepare(Q0 + p, lambda i, r, n: plane(own, PX * i + p, r, n))
    for k in range(3):
        prepare(near + k, lambda i, r, n: plane(sw, PX * i + par + k, r, n))
    slot = {B: 0, ALPHA: 1, BY: 2, BZ: 3}
    for k in range(3):
        prepare(far + k, lambda i, r, n: sf[3 * slot[i] + k, pl.ds(r, n), :])

    rows = (0, EY)
    sweep(x, None, cc, w, 1, 9, rows, 1, 1, into(y), chunk)
    sweep(y, x, cc, w, 2, 8, rows, 1, 2, into(z), chunk)
    got = []
    for c in range(2):
        for r0 in range(0, EY, chunk):
            v = 0.0
            for q in (Q0 + 2 * c, Q0 + 2 * c + 1):
                _, zz = defect(z, cc, w, q, r0, chunk, 1, q, 0, q, 0)
                v = v + d[q, pl.ds(r0, chunk), :] * zz
            t[c, pl.ds(r0, chunk), :] = v
        got.append(pair_lanes(t[c, pl.ds(HY, H1, 2), :] + t[c, pl.ds(HY + 1, H1, 2), :], 1) * 0.125)
    v = pack2(got[0], got[1])
    rhs[...] = v
    rhs_lo[...] = v[:G1]
    rhs_hi[...] = v[H1 - G1 :]
    mid = pl.ds(PAD, EY)
    edge[...] = z[Q0 + 2 - par, mid, :]
    xedge[...] = z[Q0 + 1 + par, mid, :]
    for p in range(6):
        pre[p] = z[Q0 - 1 + p, mid, :]


def extend_kernel(lo, rhs, hi, edge, _, send):
    send[:G1] = lo[...]
    send[pl.ds(G1, H1), :] = rhs[...]
    send[pl.ds(G1 + H1, G1), :] = hi[...]
    send[pl.ds(R1, EY), :] = edge[...]


C0 = 8
M0 = 5


def place_coefficients(s, i, e, v):
    v0, v1 = unpack2(v)
    s[i, 2 * e, pl.ds(PAD, R1), :] = v0
    s[i, 2 * e + 1, pl.ds(PAD, R1), :] = v1


def middle_faces(s, w1, inv1, d1, q):
    for r0 in range(0, R1, 32):
        here, up, out = pl.ds(PAD + r0, 32), pl.ds(PAD + r0 + 1, 32), pl.ds(r0, 32)
        dd, inv, w6 = faces(
            s[0, q, here, :], s[1, q, here, :], s[1, q + 1, here, :], s[2, q, here, :], s[2, q, up, :],
            s[3, q, here, :], 2, 0.25,
        )
        for a, f in enumerate(w6):
            w1[a, q, out, :] = f
        inv1[q, out, :] = inv
        d1[q, out, :] = dd


def sides(par, k):
    lower, upper = 3 - k, 6 + k
    return jnp.where(par == 0, lower, upper), jnp.where(par == 0, upper, lower)


def near_coefficients_kernel(own, other, one, two, s, w1, inv1, d1):
    par = parity()
    for i in range(4):
        s[i, 20, :, :] = jnp.zeros((R1 + 2 * PAD, PZ), F32)
        s[i, :, PAD + R1 :, :] = jnp.zeros((21, PAD, PZ), F32)
        place_coefficients(s, i, 4 + par, own[i])
        place_coefficients(s, i, 5 - par, other[i])
        for k in range(4):
            ref = one if k < 2 else two
            place_coefficients(s, i, sides(par, k)[0], ref[4 * (k % 2) + i])
    for k in range(11):
        middle_faces(s, w1, inv1, d1, 8 * par + k)


def level2_load(s, c):
    def load(i, k, row):
        return s[i, 2 * c + k, pl.ds(PAD + row, R2, 2), :]

    return load


def coarse_coefficients_kernel(s, w2, inv2, last, s2):
    def coarsen(c):
        for i, v in enumerate(coarser(level2_load(s, c), R2, 2)):
            s2[i, c, pl.ds(0, R2), :] = v

    s2[2, :, R2:, :] = jnp.zeros((10, PAD, PZ), F32)
    planes(0, 10, coarsen, 10)
    body = pl.ds(0, R2)

    def scale(c):
        _, inv, w6 = faces(
            s2[0, c, body, :], s2[1, c, body, :], s2[1, c + 1, body, :], s2[2, c, body, :], s2[2, c, pl.ds(1, R2), :],
            s2[3, c, body, :], 4, 0.0625,
        )
        for a, f in enumerate(w6):
            w2[a, c + 1] = f
        inv2[c + 1] = inv

    planes(0, 9, scale, 9)
    for i in range(4):
        last[i] = s2[i, 9]


def join_kernel(one, two, raw_one, raw_two, out):
    out[pl.ds(0, 2 * R1), :] = one[pl.ds(0, 2 * R1), :]
    out[pl.ds(2 * R1, 2 * R1), :] = two[...]
    for k in range(8):
        out[pl.ds((4 + k) * R1, R1), :] = raw_one[k]
        out[pl.ds((12 + k) * R1, R1), :] = raw_two[k]


def middle_kernel(own, other, one, two, its, s_in, w_in, inv_in, d_in, edge, cc, pre, rhs, s, w, inv, d, x, y, z, t, u):
    par = parity()
    clear_pads(x, R1)
    clear_pads(y, R1)
    for k in range(4):
        e = sides(par, k)[1]
        for i in range(4):
            place_coefficients(s, i, e, its[pl.ds((4 + 4 * k + i) * R1, R1), :])
    for k in range(9):
        middle_faces(s, w, inv, d, 11 - 11 * par + k)

    def place(e, v):
        for k, b in enumerate(unpack2(v)):
            q = 2 * e + k
            c0 = inv[q] * b
            cc[q] = c0
            x[q, pl.ds(PAD, R1), :] = c0 * (1.0 / THETA)

    place(4 + par, own[pl.ds(0, R1), :])
    place(5 - par, other[pl.ds(0, R1), :])
    for k in range(4):
        e, f = sides(par, k)
        ref = one if k < 2 else two
        place(e, ref[pl.ds((k % 2) * R1, R1), :])
        place(f, its[pl.ds(k * R1, R1), :])

    rows = (0, R1)
    sweep(x, None, cc, w, 2, 18, rows, 2, 1, into(y), 32)
    sweep(y, x, cc, w, 3, 17, rows, 2, 2, into(z), 32)

    def residual(c):
        for r0 in range(0, R1, 32):
            v = 0.0
            for k in range(2):
                q = 4 + 2 * c + k
                _, zz = defect(z, cc, w, q, r0, 32, 2, q, 0, q, 0)
                v = v + d[q, pl.ds(r0, 32), :] * zz
            t[c, pl.ds(r0, 32), :] = v
        rhs[c] = pair_lanes(t[c, pl.ds(0, R2, 2), :] + t[c, pl.ds(1, R2, 2), :], 2) * 0.125

    planes(0, 6, residual, 6)

    def first(k, plane):
        load = level2_load(s, plane + 4)
        al, bx, by, bz = coarser(load, R2, 2)
        after = level2_load(s, plane + 5)
        bx1 = pair_lanes(after(1, 0, 0) + after(1, 0, 1), 2) * 0.25
        u[k, pl.ds(0, R2), :] = by
        u[k, pl.ds(R2, PAD), :] = jnp.zeros((PAD, PZ), F32)
        _, inv2, _ = faces(al, bx, bx1, by, u[k, pl.ds(1, R2), :], bz, 4, 0.0625)
        return inv2 * rhs[plane + 2] * (1.0 / THETA), bx

    up = pack4([rhs[1 + 2], rhs[0 + 2], first(0, -1)[0]])
    down = pack4([rhs[0 + 2], rhs[1 + 2], *first(1, 2)])
    edge[...] = jnp.where(jnp.broadcast_to(par, up.shape) == 0, down, up)
    for p in range(10):
        pre[p] = z[C0 - 3 + p, pl.ds(PAD, R1), :]


def last_kernel(mine, its, rhs, w2, inv2, last, pre1, w1, c1, pre0, sw, xs, w0, c0, out,
                wx, c2, x2, y2, z2, x1, y1, z1, x0, y0):
    par = parity()
    body = pl.ds(PAD, R2)
    upper = jnp.broadcast_to(par, mine.shape) == 1
    lo, hi = jnp.where(upper, its[...], mine[...]), jnp.where(upper, mine[...], its[...])
    clear_pads(x2, R2)
    clear_pads(y2, R2)
    clear_pads(z2, R2)
    _, inv, w6 = faces(
        last[0, :R2], last[1, :R2], unpack4(hi, 3), last[2, :R2], last[2, pl.ds(1, R2), :], last[3, :R2], 4, 0.0625
    )
    for a, f in enumerate(w6):
        wx[a, 0] = f

    def start(j, b, dinv):
        v = dinv * b
        c2[j] = v
        x2[j, body, :] = v * (1.0 / THETA)

    start(1, unpack4(lo, 1), inv2[1])
    start(2, unpack4(lo, 0), inv2[2])
    for c in range(6):
        start(c + 3, rhs[c], inv2[c + 3])
    start(9, unpack4(hi, 0), inv2[9])
    start(10, unpack4(hi, 1), inv)
    x2[0, body, :] = unpack4(lo, 2)
    x2[11, body, :] = unpack4(hi, 2)
    rows = (0, R2)
    sweep(x2, None, c2, w2, 1, 10, rows, 4, 1, into(y2), R2, unroll=9)
    sweep(x2, None, c2, wx, 10, 11, rows, 4, 1, into(y2), R2, woff=-10)
    sweep(y2, x2, c2, w2, 2, 10, rows, 4, 2, into(z2), R2, unroll=8)
    sweep(z2, y2, c2, w2, 3, 9, rows, 4, 3, into(x2), R2, unroll=6)

    clear_pads(x1, R1)
    clear_pads(y1, R1)
    for q in range(10):
        v = x2[(q - 3) // 2 + M0, body, :]
        z1[q, pl.ds(PAD, R2, 2), :] = v
        z1[q, pl.ds(PAD + 1, R2, 2), :] = v
        x1[q, pl.ds(PAD, R1), :] = pre1[q] + z1[q, pl.ds(PAD, R1), :]
    rows = (0, R1)
    off = C0 - 3
    sweep(x1, None, c1, w1, 1, 9, rows, 2, 0, into(y1), 32, woff=off, coff=off)
    sweep(y1, x1, c1, w1, 2, 8, rows, 2, 1, into(z1), 32, woff=off, coff=off, unroll=6)

    clear_pads(x0, EY)
    clear_pads(y0, EY)
    near, far = 7 - 7 * par, 7 * par
    body = pl.ds(PAD, EY)
    for q in range(8):
        v = z1[(q - 2) // 2 + 3 + 2 * par, pl.ds(PAD + 12, EY // 2), :]
        x0[q, pl.ds(PAD, EY // 2, 2), :] = v
        x0[q, pl.ds(PAD + 1, EY // 2, 2), :] = v
        if 0 < q < 7:
            x0[q, body, :] += pre0[q - 1]
    x0[near, body, :] += sw[pl.ds(R1, EY), :]
    x0[far, body, :] += xs[pl.ds(2 * R1, EY), :]
    off = Q0 - 2
    sweep(x0, None, c0, w0, 1, 7, (0, EY), 1, 0, into(y0), 40, woff=off, coff=off, unroll=6)

    def finish(q, r0, n, v):
        out[q - 2, pl.ds(r0 - 8, n), :] = v

    sweep(y0, x0, c0, w0, 2, 6, (8, 8 + PY), 1, 1, finish, 32, woff=off, coff=off, unroll=4)


def swap(v):
    return lax.ppermute(v, "wide", [(i, i ^ 1) for i in range(lax.axis_size("wide"))])


def across(v, chips):
    count = lax.axis_size("wide")
    step = 2 * chips - 1
    pairs = [(i, i + step) for i in range(1, count, 2) if i + step < count]
    pairs += [(i, i - step) for i in range(0, count, 2) if i - step >= 0]
    return lax.ppermute(v, "wide", pairs)


def shifted(v, axis, step):
    count = lax.axis_size(axis)
    return lax.ppermute(v, axis, [(i, i + step) for i in range(count) if 0 <= i + step < count])


def shards(right_side, alpha_coef, beta_x, beta_y, beta_z):
    a, ylo, yhi, xs, raw = call(
        pack_kernel, "pack",
        (shape(5, PX, PY, PZ), shape(SIDE + 4 * G1, PZ), shape(SIDE + 4 * G1, PZ), shape(16, PY, PZ),
         shape(4, H1, PZ)),
        (VMEM,) * 5, [ANY] * 5, [pltpu.SemaphoreType.DMA((5,))], 1000,
    )(*[pltpu.with_memory_space_constraint(v, pltpu.HBM) for v in (right_side, alpha_coef, beta_x, beta_y, beta_z)])
    lo = shifted(yhi, "narrow", 1)
    hi = shifted(ylo, "narrow", -1)
    xs = across(xs, 1)
    own, cxs = call(
        corner_kernel, "corners", (shape(RAW + 4 * R1, PZ), shape(16, 2 * HY, PZ)), (VMEM,) * 2,
        [VMEM] * 4 + [ANY], [], 1000,
    )(a, raw, lo, hi, xs)
    sw = swap(own)
    cxs = across(cxs, 1)

    raw_own, raw_other = own[RAW:].reshape(4, R1, PZ), sw[RAW:].reshape(4, R1, PZ)
    raw1 = jnp.concatenate([raw_own, raw_other], 0)
    raw1_one, raw1_two = across(raw1, 1), across(raw1, 2)

    rhs, rhs_lo, rhs_hi, edge0, xedge0, pre0, w0, c0 = call(
        fine_kernel, "level0_pre",
        (shape(H1, PZ), shape(G1, PZ), shape(G1, PZ), shape(EY, PZ), shape(EY, PZ), shape(6, EY, PZ),
         shape(6, 10, EY, PZ), shape(10, EY, PZ)),
        (VMEM,) * 8, [VMEM] * 4,
        [scratch(12, EY, PZ), scratch(12, EY, PZ), scratch(10, EY, PZ)] + [scratch(10, EY + 2 * PAD, PZ)] * 3
        + [scratch(2, EY, PZ)],
        20000000000,
    )(own, sw, xs, cxs)
    rhs_below = shifted(rhs_hi, "narrow", 1)
    rhs_above = shifted(rhs_lo, "narrow", -1)
    s1, w1, inv1, d1 = call(
        near_coefficients_kernel, "near_coefficients",
        (shape(4, 21, R1 + 2 * PAD, PZ), shape(6, 20, R1, PZ), shape(20, R1, PZ), shape(20, R1, PZ)),
        (VMEM,) * 4, [VMEM] * 4, [], 20000000000,
    )(raw_own, raw_other, raw1_one, raw1_two)
    send = call(extend_kernel, "extend", shape(R1 + EY, PZ), VMEM, [VMEM] * 4 + [ANY], [], 1000)(
        rhs_below, rhs, rhs_above, edge0, d1
    )

    other = swap(send)
    pair = jnp.concatenate([send[:R1], other[:R1], xedge0], 0)
    one = across(pair, 1)
    two = across(pair[: 2 * R1], 2)
    mine = call(join_kernel, "join", shape(20 * R1, PZ), VMEM, [VMEM] * 4, [], 1000)(
        one, two, raw1_one, raw1_two
    )
    its = swap(mine)

    edge, c1, pre1, rhs2, s1, w1, _, _ = call(
        middle_kernel, "level1_pre",
        (shape(R2, PZ), shape(20, R1, PZ), shape(10, R1, PZ), shape(6, R2, PZ),
         shape(4, 21, R1 + 2 * PAD, PZ), shape(6, 20, R1, PZ), shape(20, R1, PZ), shape(20, R1, PZ)),
        (VMEM,) * 8, [VMEM] * 9,
        [scratch(20, R1 + 2 * PAD, PZ)] * 3 + [scratch(6, R1, PZ), scratch(2, R2 + PAD, PZ)],
        4000000, aliases={5: 4, 6: 5, 7: 6, 8: 7},
    )(send, other, one, two, its, s1, w1, inv1, d1)

    w2, inv2, last2 = call(
        coarse_coefficients_kernel, "level2_coefficients",
        (shape(6, 12, R2, PZ), shape(12, R2, PZ), shape(4, R2 + PAD, PZ)),
        (VMEM,) * 3, [VMEM], [scratch(4, 10, R2 + PAD, PZ)], 4000000,
    )(s1)
    mine2 = across(edge, 2)
    its2 = swap(mine2)
    return call(
        last_kernel, "coarse_and_post", shape(PX, PY, PZ), VMEM, [VMEM] * 14,
        [scratch(6, 1, R2, PZ), scratch(12, R2, PZ)] + [scratch(12, R2 + 2 * PAD, PZ)] * 3
        + [scratch(10, R1 + 2 * PAD, PZ)] * 3 + [scratch(8, EY + 2 * PAD, PZ)] * 2,
        4000000,
    )(mine2, its2, rhs2, w2, inv2, last2, pre1, w1, c1, pre0, other, one, w0, c0)


def solution(mesh):
    spec = P("wide", "narrow", None)
    return jax.shard_map(shards, mesh=mesh, in_specs=(spec,) * 5, out_specs=spec, check_vma=False)
```

```python
import jax
import jax.numpy as jnp
from jax import lax
from jax.experimental import pallas as pl
from jax.experimental.pallas import tpu as pltpu
from jax.sharding import PartitionSpec as P

F32 = jnp.float32
THETA = (2.0 + 0.25) / 2.0
DELTA = (2.0 - 0.25) / 2.0
SIGMA = THETA / DELTA
RHO = [1.0 / SIGMA]
for _step in range(3):
    RHO.append(1.0 / (2.0 * SIGMA - RHO[-1]))
MOMENTUM = [0.0] + [RHO[k] * RHO[k - 1] for k in range(1, 4)]
GAIN = [1.0 / THETA] + [2.0 * RHO[k] / DELTA for k in range(1, 4)]

PX, PY, PZ = 4, 64, 128
HY = 8
EY = PY + 2 * HY
H1 = PY // 2
G1 = 16
R1 = H1 + 2 * G1
R2 = R1 // 2
RAW = 5 * PX * EY
SIDE = 5 * PX * HY
PAD = 8
SMALL, LARGE = 1000, 2 * 10**10
B, ALPHA, BX, BY, BZ = range(5)
ANY = pl.BlockSpec(memory_space=pl.ANY)
VMEM = pl.BlockSpec(memory_space=pltpu.VMEM)
HBM = pl.BlockSpec(memory_space=pltpu.HBM)


def shape(*dims):
    return jax.ShapeDtypeStruct(dims, F32)


def scratch(*dims):
    return pltpu.VMEM(dims, F32)


def call(kernel, name, out_shape, out_specs, in_specs, scratch_shapes, flops, mib=24, aliases=None):
    return pl.pallas_call(
        kernel,
        out_shape=out_shape,
        in_specs=in_specs,
        out_specs=out_specs,
        scratch_shapes=scratch_shapes,
        compiler_params=pltpu.CompilerParams(vmem_limit_bytes=mib * 1024 * 1024),
        cost_estimate=pl.CostEstimate(flops=flops, bytes_accessed=0, transcendentals=0),
        input_output_aliases=aliases or {},
        name=name,
    )


def parity():
    return lax.rem(lax.axis_index("wide"), 2)


def lanes(rows):
    return lax.broadcasted_iota(jnp.int32, (rows, PZ), 1)


def moved(v, shift):
    return pltpu.roll(v, shift % PZ, 1)


def planes(lo, hi, each, unroll):
    if not unroll:
        each(lo)
        return
    steps = (hi - lo) // unroll

    def body(i, carry):
        for k in range(unroll):
            each(lo + i * unroll + k)
        return carry

    if steps > 1:
        lax.fori_loop(0, steps, body, 0)
    else:
        steps = 0
    for q in range(lo + steps * unroll, hi):
        each(q)


def defect(x_ref, c_ref, w_ref, q, r0, n, reach, cq, cr, wq, wr):
    rows = pl.ds(PAD + r0, n)
    here = pl.ds(wr + r0, n)
    x = x_ref[q, rows, :]
    total = c_ref[cq, pl.ds(cr + r0, n), :] - x
    total += w_ref[0, wq, here, :] * x_ref[q - 1, rows, :]
    total += w_ref[1, wq, here, :] * x_ref[q + 1, rows, :]
    total += w_ref[2, wq, here, :] * x_ref[q, pl.ds(PAD + r0 - 1, n), :]
    total += w_ref[3, wq, here, :] * x_ref[q, pl.ds(PAD + r0 + 1, n), :]
    total += w_ref[4, wq, here, :] * moved(x, reach)
    total += w_ref[5, wq, here, :] * moved(x, -reach)
    return x, total


def sweep(x_ref, prev_ref, c_ref, w_ref, lo, hi, rows, reach, k, store, chunk, woff=0, coff=0, wr=0, cr=0, unroll=8):
    def each(q):
        for r0 in range(rows[0], rows[1], chunk):
            n = min(chunk, rows[1] - r0)
            x, z = defect(x_ref, c_ref, w_ref, q, r0, n, reach, q + coff, cr, q + woff, wr)
            new = x + GAIN[k] * z
            if k > 0:
                gap = x if prev_ref is None else x - prev_ref[q, pl.ds(PAD + r0, n), :]
                new += MOMENTUM[k] * gap
            store(q, r0, n, new)

    planes(lo, hi, each, unroll)


def into(ref):
    def store(q, r0, n, v):
        ref[q, pl.ds(PAD + r0, n), :] = v

    return store


def inverse(d):
    inside = d > 0.0
    return jnp.where(inside, 1.0 / jnp.where(inside, d, 1.0), 0.0)


def faces(alpha, x0, x1, y0, y1, z0, reach, scale):
    z1 = moved(z0, -reach)
    d = alpha + scale * (x0 + x1 + y0 + y1 + z0 + z1)
    inv = inverse(d)
    si = scale * inv
    return d, inv, [si * f for f in (x0, x1, y0, y1, z0, z1)]


def next_rows(load, r0, n, rows):
    if r0 + n < rows:
        return load(r0 + 1, n)
    return pltpu.roll(load(r0, n), n - 1, 0)


def clear_pads(ref, rows):
    ref[:, :PAD, :] = jnp.zeros((ref.shape[0], PAD, PZ), F32)
    ref[:, PAD + rows :, :] = jnp.zeros((ref.shape[0], PAD, PZ), F32)


def pair_lanes(v, reach):
    low = (lanes(v.shape[0]) & reach) == 0
    return v + jnp.where(low, moved(v, -reach), moved(v, reach))


def low_lanes(v, reach):
    low = (lanes(v.shape[0]) & reach) == 0
    return jnp.where(low, v, moved(v, reach))


def pack2(v0, v1):
    return jnp.where((lanes(v0.shape[0]) & 1) == 0, v0, v1)


def unpack2(v):
    even = (lanes(v.shape[0]) & 1) == 0
    return jnp.where(even, v, moved(v, 1)), jnp.where(even, moved(v, -1), v)


def pack4(items):
    place = lanes(items[0].shape[0]) & 3
    out = items[0]
    for i, item in enumerate(items[1:], 1):
        out = jnp.where(place == i, item, out)
    return out


def unpack4(v, i):
    place = lanes(v.shape[0]) & 3
    out = v
    for m in range(4):
        if m != i:
            out = jnp.where(place == m, moved(v, m - i), out)
    return out


def coarser(load, rows, reach):
    def cell(i):
        return load(i, 0, 0) + load(i, 0, 1) + load(i, 1, 0) + load(i, 1, 1)

    al = pair_lanes(cell(0), reach) * 0.125
    bx = pair_lanes(load(1, 0, 0) + load(1, 0, 1), reach) * 0.25
    by = pair_lanes(load(2, 0, 0) + load(2, 1, 0), reach) * 0.25
    bz = low_lanes(cell(3), reach) * 0.25
    return al, bx, by, bz


def pack_kernel(b, al, bx, by, bz, a, lo_out, hi_out, raw, sems):
    wide, narrow = lax.axis_index("wide"), lax.axis_index("narrow")
    copies = [pltpu.make_async_copy(ref, a.at[i], sems.at[i]) for i, ref in enumerate((b, al, bx, by, bz))]
    for c in copies:
        c.start()
    for c in copies:
        c.wait()
    row = lax.broadcasted_iota(jnp.int32, (PAD, PZ), 0)
    first_row = jnp.logical_and(row == 0, jnp.broadcast_to(narrow, (PAD, PZ)) == 0)
    a[BX, 0] = jnp.where(jnp.broadcast_to(wide, (PY, PZ)) == 0, 0.0, a[BX, 0])
    first_z = lanes(PY) == 0
    for p in range(PX):
        a[BY, p, :PAD] = jnp.where(first_row, 0.0, a[BY, p, :PAD])
        a[BZ, p] = jnp.where(first_z, 0.0, a[BZ, p])
    got = []
    for c in range(2):

        def load(i, k, row):
            return a[i + 1, 2 * c + k, pl.ds(row, H1, 2), :]

        got.append(coarser(load, H1, 1))
    for i in range(4):
        v = pack2(got[0][i], got[1][i])
        raw[i] = v
        lo_out[pl.ds(SIDE + G1 * i, G1), :] = v[:G1]
        hi_out[pl.ds(SIDE + G1 * i, G1), :] = v[H1 - G1 :]
    for i in range(5):
        for p in range(PX):
            here = pl.ds((PX * i + p) * HY, HY)
            lo_out[here, :] = a[i, p, :HY]
            hi_out[here, :] = a[i, p, PY - HY :]


def plane(ref, k, r0=0, n=EY):
    start = k * EY + r0
    return ref[pl.ds(pl.multiple_of(start, 8) if r0 % 8 == 0 else start, n), :]


def corner_kernel(a, raw, lo, hi, sw, xs, x):
    par = parity()
    for i in range(5):
        for p in range(PX):
            k = PX * i + p
            sw[pl.ds(k * EY, HY), :] = lo[pl.ds(k * HY, HY), :]
            sw[pl.ds(k * EY + HY, PY), :] = a[i, p]
            sw[pl.ds(k * EY + HY + PY, HY), :] = hi[pl.ds(k * HY, HY), :]
    for i in range(4):
        here = pl.ds(SIDE + G1 * i, G1)
        base = RAW + R1 * i
        sw[pl.ds(base, G1), :] = lo[here, :]
        sw[pl.ds(base + G1, H1), :] = raw[i]
        sw[pl.ds(base + G1 + H1, G1), :] = hi[here, :]
    for i in range(5):
        xs[pl.ds(i * EY, EY), :] = plane(sw, PX * i + 3 * par)
    clear_pads(x, EY)
    body = pl.ds(PAD, EY)

    def prepared(p):
        by = plane(sw, PX * BY + p)
        _, inv, w = faces(
            plane(sw, PX * ALPHA + p), plane(sw, PX * BX + p), plane(sw, PX * BX + p + 1), by,
            pltpu.roll(by, EY - 1, 0), plane(sw, PX * BZ + p), 1, 1.0,
        )
        return w, inv * plane(sw, PX * B + p)

    for p in range(3):
        x[p, body, :] = prepared(p)[1] * (1.0 / THETA)
    second = 1 + par
    w, c0 = prepared(second)
    lower = jnp.broadcast_to(par, c0.shape) == 0
    v = x[second, body, :]
    z = c0 - v + w[0] * x[second - 1, body, :] + jnp.where(lower, w[1] * x[2, body, :], 0.0)
    z += w[2] * x[second, pl.ds(PAD - 1, EY), :] + w[3] * x[second, pl.ds(PAD + 1, EY), :]
    z += w[4] * moved(v, 1) + w[5] * moved(v, -1)
    xs[pl.ds(5 * EY, EY), :] = v
    xs[pl.ds(6 * EY, EY), :] = v + GAIN[1] * z + MOMENTUM[1] * v
    xs[pl.ds(7 * EY, EY), :] = jnp.where(lower, plane(sw, PX * BX + second), w[1])


Q0 = 3


def fine_kernel(own, sw, xs, rhs, rhs_lo, rhs_hi, edge, xedge, pre, w, cc, sx, d, x, y, z, t):
    par = parity()
    near = 7 * (1 - par)
    far = 2 + 5 * par
    for p in range(PX):
        sx[Q0 + p] = plane(own, PX * BX + p)
    for k in range(3):
        sx[near + k] = plane(sw, PX * BX + par + k)
    sx[10 + par] = plane(sw, PX * BX + 3)
    sx[far] = plane(xs, BX)
    sx[11 - 3 * par] = plane(xs, 7)
    clear_pads(x, EY)
    clear_pads(y, EY)
    chunk = 40

    def prepare(q, get):
        for r0 in range(0, EY, chunk):
            here = pl.ds(r0, chunk)

            def load(i):
                return lambda r, n: get(i, r, n)

            dd, inv, w6 = faces(
                load(ALPHA)(r0, chunk), sx[q, here, :], sx[q + 1, here, :], load(BY)(r0, chunk),
                next_rows(load(BY), r0, chunk, EY), load(BZ)(r0, chunk), 1, 1.0,
            )
            for a, f in enumerate(w6):
                w[a, q, here, :] = f
            c0 = inv * load(B)(r0, chunk)
            cc[q, here, :] = c0
            x[q, pl.ds(PAD + r0, chunk), :] = c0 * (1.0 / THETA)
            d[q, here, :] = dd

    for p in range(PX):
        prepare(Q0 + p, lambda i, r, n: plane(own, PX * i + p, r, n))
    for k in range(3):
        prepare(near + k, lambda i, r, n: plane(sw, PX * i + par + k, r, n))
    prepare(far, lambda i, r, n: plane(xs, i, r, n))
    beyond = 1 + 7 * par
    body = pl.ds(PAD, EY)
    x[beyond, body, :] = plane(xs, 5)
    missing = GAIN[1] * plane(xs, 7) * x[2, body, :]
    y[beyond, body, :] = plane(xs, 6) + jnp.where(jnp.broadcast_to(par, missing.shape) == 0, missing, 0.0)

    rows = (0, EY)
    sweep(x, None, cc, w, 2, 8, rows, 1, 1, into(y), chunk)
    sweep(x, None, cc, w, 8 - 7 * par, 9 - 7 * par, rows, 1, 1, into(y), chunk, unroll=0)
    sweep(y, x, cc, w, 2, 8, rows, 1, 2, into(z), chunk)
    got = []
    for c in range(2):
        for r0 in range(0, EY, chunk):
            v = 0.0
            for q in (Q0 + 2 * c, Q0 + 2 * c + 1):
                _, zz = defect(z, cc, w, q, r0, chunk, 1, q, 0, q, 0)
                v = v + d[q, pl.ds(r0, chunk), :] * zz
            t[c, pl.ds(r0, chunk), :] = v
        got.append(pair_lanes(t[c, pl.ds(HY, H1, 2), :] + t[c, pl.ds(HY + 1, H1, 2), :], 1) * 0.125)
    v = pack2(got[0], got[1])
    rhs[...] = v
    rhs_lo[...] = v[:G1]
    rhs_hi[...] = v[H1 - G1 :]
    mid = pl.ds(PAD, EY)
    edge[...] = z[Q0 + 2 - par, mid, :]
    xedge[...] = z[Q0 + 1 + par, mid, :]
    for p in range(6):
        pre[p] = z[Q0 - 1 + p, mid, :]


C0 = 5
N1 = 14
M0 = 5
S_SHAPE = (4, N1, R1 + 2 * PAD, PZ)
O_EDGE = R1
O_ONE = O_EDGE + EY
O_BESIDE = O_ONE + R1
O_TWO = O_BESIDE + R1
O_RAW = O_TWO + 2 * R1
O_END = O_RAW + 8 * R1


def place_coefficients(s, i, e, v):
    v0, v1 = unpack2(v)
    s[i, 1 + 2 * e, pl.ds(PAD, R1), :] = v0
    s[i, 2 + 2 * e, pl.ds(PAD, R1), :] = v1


def middle_faces(s, w1, inv1, d1, q):
    for r0 in range(0, R1, 32):
        here, up, out = pl.ds(PAD + r0, 32), pl.ds(PAD + r0 + 1, 32), pl.ds(r0, 32)
        dd, inv, w6 = faces(
            s[0, q, here, :], s[1, q, here, :], s[1, q + 1, here, :], s[2, q, here, :], s[2, q, up, :],
            s[3, q, here, :], 2, 0.25,
        )
        for a, f in enumerate(w6):
            w1[a, q, out, :] = f
        inv1[q, out, :] = inv
        d1[q, out, :] = dd


def sides(par, k):
    lower, upper = 1 - k, 4 + k
    return jnp.where(par == 0, lower, upper), jnp.where(par == 0, upper, lower)


def level2_load(s, plane):
    def load(i, k, row):
        return s[i, 2 * plane + C0 + k, pl.ds(PAD + row, R2, 2), :]

    return load


def near_coefficients_kernel(own, other, beside, s, w1, inv1, d1, coarse):
    par = parity()
    for i in range(4):
        s[i, :, PAD + R1 :, :] = jnp.zeros((N1, PAD, PZ), F32)
        rows = pl.ds(R1 * i, R1)
        place_coefficients(s, i, 2 + par, own[rows, :])
        place_coefficients(s, i, 3 - par, other[rows, :])
        place_coefficients(s, i, sides(par, 0)[0], beside[pl.ds(R1 * (4 + i), R1), :])
        place_coefficients(s, i, sides(par, 1)[0], beside[rows, :])
    for k in range(7):
        middle_faces(s, w1, inv1, d1, 1 + 4 * par + k)
    for k in range(2):
        coarse[pl.ds(R2 * k, R2), :] = pack4(coarser(level2_load(s, k), R2, 2))


def extend_kernel(lo, rhs, hi, xedge, s, inv, coarse, send, send2):
    par = parity()
    send[:G1] = lo[...]
    send[pl.ds(G1, H1), :] = rhs[...]
    send[pl.ds(G1 + H1, G1), :] = hi[...]
    send[pl.ds(R1, EY), :] = xedge[...]
    v = send[:R1]
    odd = jnp.broadcast_to(par, v.shape)
    v0, v1 = unpack2(v)
    q = C0 + 3 * par
    x1 = inv[q] * jnp.where(odd == 0, v0, v1) * (1.0 / THETA)
    send2[:R1] = pack2(x1, s[1, q, pl.ds(PAD, R1), :])
    send2[R1:] = coarse[...]


def join_kernel(own, edge, one, beside, two, raw_beside, out):
    out[:R1] = own[:R1]
    out[pl.ds(O_EDGE, EY), :] = edge[...]
    out[pl.ds(O_ONE, R1), :] = one[:R1]
    out[pl.ds(O_BESIDE, R1), :] = beside[:R1]
    out[pl.ds(O_TWO, 2 * R1), :] = two[...]
    out[pl.ds(O_RAW, 4 * R1), :] = raw_beside[pl.ds(4 * R1, 4 * R1), :]
    out[pl.ds(O_RAW + 4 * R1, 4 * R1), :] = raw_beside[pl.ds(0, 4 * R1), :]


def both_sides(par, mine, its):
    upper = jnp.broadcast_to(par, mine.shape) == 1
    return jnp.where(upper, its, mine), jnp.where(upper, mine, its)


def middle_kernel(own, one, beside, two, its, s_in, w_in, inv_in, d_in, edge, cc, pre, rhs, s, w, inv, d,
                  x, y, z, t, u):
    par = parity()
    clear_pads(x, R1)
    clear_pads(y, R1)
    body = pl.ds(PAD, R1)
    lower, upper = both_sides(par, two[:R1], its[pl.ds(O_TWO, R1), :])
    x[0, body, :] = unpack2(lower)[0]
    x1, bx = unpack2(upper)
    x[N1 - 1, body, :] = x1
    s[1, N1 - 1, body, :] = bx
    for k in range(2):
        e = sides(par, k)[1]
        for i in range(4):
            place_coefficients(s, i, e, its[pl.ds(O_RAW + (4 * k + i) * R1, R1), :])
    for k in range(5):
        middle_faces(s, w, inv, d, jnp.where(par == 0, 8 + k, 1 + k if k < 4 else 12))

    def place(e, v):
        for k, b in enumerate(unpack2(v)):
            q = 1 + 2 * e + k
            c0 = inv[q] * b
            cc[q] = c0
            x[q, body, :] = c0 * (1.0 / THETA)

    place(2 + par, own[:R1])
    place(3 - par, its[:R1])
    for k, ref, row in ((0, one, O_ONE), (1, beside, O_BESIDE)):
        e, f = sides(par, k)
        place(e, ref[:R1])
        place(f, its[pl.ds(row, R1), :])

    rows = (0, R1)
    sweep(x, None, cc, w, 1, 13, rows, 2, 1, into(y), 32, unroll=12)
    sweep(y, x, cc, w, 2, 12, rows, 2, 2, into(z), 32, unroll=10)

    for c in range(4):
        for r0 in range(0, R1, 32):
            v = 0.0
            for k in range(2):
                q = C0 - 2 + 2 * c + k
                _, zz = defect(z, cc, w, q, r0, 32, 2, q, 0, q, 0)
                v = v + d[q, pl.ds(r0, 32), :] * zz
            t[c, pl.ds(r0, 32), :] = v
        rhs[c] = pair_lanes(t[c, pl.ds(0, R2, 2), :] + t[c, pl.ds(1, R2, 2), :], 2) * 0.125

    def first(k, plane):
        al, bx, by, bz = coarser(level2_load(s, plane), R2, 2)
        after = level2_load(s, plane + 1)
        bx1 = pair_lanes(after(1, 0, 0) + after(1, 0, 1), 2) * 0.25
        u[k, pl.ds(0, R2), :] = by
        u[k, pl.ds(R2, PAD), :] = jnp.zeros((PAD, PZ), F32)
        _, inv2, _ = faces(al, bx, bx1, by, u[k, pl.ds(1, R2), :], bz, 4, 0.0625)
        return inv2 * rhs[plane + 1] * (1.0 / THETA), bx

    below, above = first(0, -1), first(1, 2)
    up = pack4([rhs[3], rhs[2], rhs[1], below[0]])
    down = pack4([rhs[0], rhs[1], rhs[2], above[0]])
    wide = jnp.broadcast_to(lax.axis_index("wide"), up.shape)
    ends = (lanes(R2) & 3) == 0
    down = jnp.where(wide == 0, jnp.where(ends, rhs[1], 0.0), down)
    up = jnp.where(wide == lax.axis_size("wide") - 1, jnp.where(ends, rhs[2], 0.0), up)
    edge[:R2] = jnp.where(jnp.broadcast_to(par, up.shape) == 0, down, up)
    edge[R2:] = above[1]
    for p in range(10):
        pre[p] = z[C0 - 3 + p, body, :]


def coarse_coefficients_kernel(s, two, its, w2, inv2, last, s2):
    par = parity()
    for c in range(2, 8):
        for i, v in enumerate(coarser(level2_load(s, c - 4), R2, 2)):
            s2[i, c, pl.ds(0, R2), :] = v
    for k in range(2):
        rows = pl.ds(R1 + R2 * k, R2)
        lower, upper = both_sides(par, two[rows, :], its[pl.ds(O_TWO + R1 + R2 * k, R2), :])
        for i in range(4):
            s2[i, k, pl.ds(0, R2), :] = unpack4(lower, i)
            s2[i, 8 + k, pl.ds(0, R2), :] = unpack4(upper, i)
    s2[2, :, R2:, :] = jnp.zeros((10, PAD, PZ), F32)
    body = pl.ds(0, R2)
    for c in range(9):
        _, inv, w6 = faces(
            s2[0, c, body, :], s2[1, c, body, :], s2[1, c + 1, body, :], s2[2, c, body, :], s2[2, c, pl.ds(1, R2), :],
            s2[3, c, body, :], 4, 0.0625,
        )
        for a, f in enumerate(w6):
            w2[a, c + 1] = f
        inv2[c + 1] = inv
    for i in range(4):
        last[i] = s2[i, 9]


def last_kernel(two2, its2, rhs, w2, inv2, last, pre1, w1, c1, pre0, sw, xs, w0, c0, out,
                wx, c2, x2, y2, z2, x1, y1, z1, x0, y0):
    par = parity()
    body = pl.ds(PAD, R2)
    lo, hi = both_sides(par, two2[:R2], its2[:R2])
    _, beyond = both_sides(par, two2[R2:], its2[R2:])
    clear_pads(x2, R2)
    clear_pads(y2, R2)
    clear_pads(z2, R2)
    _, inv, w6 = faces(
        last[0, :R2], last[1, :R2], beyond, last[2, :R2], last[2, pl.ds(1, R2), :], last[3, :R2], 4, 0.0625
    )
    for a, f in enumerate(w6):
        wx[a, 0] = f

    def start(j, b, dinv):
        v = dinv * b
        c2[j] = v
        x2[j, body, :] = v * (1.0 / THETA)

    for k in range(3):
        start(3 - k, unpack4(lo, k), inv2[3 - k])
        start(8 + k, unpack4(hi, k), inv2[8 + k] if k < 2 else inv)
    for c in range(4):
        start(c + 4, rhs[c], inv2[c + 4])
    x2[0, body, :] = unpack4(lo, 3)
    x2[11, body, :] = unpack4(hi, 3)
    rows = (0, R2)
    sweep(x2, None, c2, w2, 1, 10, rows, 4, 1, into(y2), R2, unroll=9)
    sweep(x2, None, c2, wx, 10, 11, rows, 4, 1, into(y2), R2, woff=-10)
    sweep(y2, x2, c2, w2, 2, 10, rows, 4, 2, into(z2), R2, unroll=8)
    sweep(z2, y2, c2, w2, 3, 9, rows, 4, 3, into(x2), R2, unroll=6)

    clear_pads(x1, R1)
    clear_pads(y1, R1)
    for q in range(10):
        v = x2[(q - 3) // 2 + M0, body, :]
        z1[q, pl.ds(PAD, R2, 2), :] = v
        z1[q, pl.ds(PAD + 1, R2, 2), :] = v
        x1[q, pl.ds(PAD, R1), :] = pre1[q] + z1[q, pl.ds(PAD, R1), :]
    rows = (0, R1)
    off = C0 - 3
    sweep(x1, None, c1, w1, 1, 9, rows, 2, 0, into(y1), 32, woff=off, coff=off)
    sweep(y1, x1, c1, w1, 2, 8, rows, 2, 1, into(z1), 32, woff=off, coff=off, unroll=6)

    clear_pads(x0, EY)
    clear_pads(y0, EY)
    near, far = 7 - 7 * par, 7 * par
    body = pl.ds(PAD, EY)
    for q in range(8):
        v = z1[(q - 2) // 2 + 3 + 2 * par, pl.ds(PAD + 12, EY // 2), :]
        x0[q, pl.ds(PAD, EY // 2, 2), :] = v
        x0[q, pl.ds(PAD + 1, EY // 2, 2), :] = v
        if 0 < q < 7:
            x0[q, body, :] += pre0[q - 1]
    x0[near, body, :] += sw[pl.ds(O_EDGE, EY), :]
    x0[far, body, :] += xs[pl.ds(R1, EY), :]
    off = Q0 - 2
    sweep(x0, None, c0, w0, 1, 7, (0, EY), 1, 0, into(y0), 40, woff=off, coff=off, unroll=6)

    def finish(q, r0, n, v):
        out[q - 2, pl.ds(r0 - 8, n), :] = v

    sweep(y0, x0, c0, w0, 2, 6, (8, 8 + PY), 1, 1, finish, 32, woff=off, coff=off, unroll=4)


def swap(v):
    return lax.ppermute(v, "wide", [(i, i ^ 1) for i in range(lax.axis_size("wide"))])


def across(v, chips, ends=()):
    count = lax.axis_size("wide")
    step = 2 * chips - 1
    pairs = [(i, i + step) for i in range(1, count, 2) if i + step < count]
    pairs += [(i, i - step) for i in range(0, count, 2) if i - step >= 0]
    return lax.ppermute(v, "wide", pairs + list(ends))


def from_beside(v):
    count = lax.axis_size("wide")
    pairs = [(i, i + 2) for i in range(0, count - 2, 2)] + [(i, i - 2) for i in range(3, count, 2)]
    return lax.ppermute(v, "wide", pairs)


def shifted(v, axis, step):
    count = lax.axis_size(axis)
    return lax.ppermute(v, axis, [(i, i + step) for i in range(count) if 0 <= i + step < count])


def shards(right_side, alpha_coef, beta_x, beta_y, beta_z):
    a, ylo, yhi, raw = call(
        pack_kernel, "pack",
        (shape(5, PX, PY, PZ), shape(SIDE + 4 * G1, PZ), shape(SIDE + 4 * G1, PZ), shape(4, H1, PZ)),
        (VMEM,) * 4, [ANY] * 5, [pltpu.SemaphoreType.DMA((5,))], SMALL,
    )(*[pltpu.with_memory_space_constraint(v, pltpu.HBM) for v in (right_side, alpha_coef, beta_x, beta_y, beta_z)])
    lo = shifted(yhi, "narrow", 1)
    hi = shifted(ylo, "narrow", -1)
    own, xs = call(
        corner_kernel, "corners", (shape(RAW + 4 * R1, PZ), shape(8 * EY, PZ)), (VMEM,) * 2, [VMEM] * 4,
        [scratch(3, EY + 2 * PAD, PZ)], SMALL,
    )(a, raw, lo, hi)
    xs = across(xs, 1)
    sw = swap(own)
    raw_beside = from_beside(jnp.concatenate([own[RAW:], sw[RAW:]], 0))

    rhs, rhs_lo, rhs_hi, edge0, xedge0, pre0, w0, c0 = call(
        fine_kernel, "level0_pre",
        (shape(H1, PZ), shape(G1, PZ), shape(G1, PZ), shape(EY, PZ), shape(EY, PZ), shape(6, EY, PZ),
         shape(6, 10, EY, PZ), shape(10, EY, PZ)),
        (VMEM,) * 8, [VMEM] * 3,
        [scratch(12, EY, PZ), scratch(10, EY, PZ)] + [scratch(10, EY + 2 * PAD, PZ)] * 3 + [scratch(2, EY, PZ)],
        LARGE,
    )(own, sw, xs)
    rhs_below = shifted(rhs_hi, "narrow", 1)
    rhs_above = shifted(rhs_lo, "narrow", -1)
    w1_shapes = (shape(*S_SHAPE), shape(6, N1, R1, PZ), shape(N1, R1, PZ), shape(N1, R1, PZ))
    s1, w1, inv1, d1, coarse = call(
        near_coefficients_kernel, "near_coefficients", w1_shapes + (shape(R1, PZ),),
        (VMEM,) * 5, [VMEM] * 3, [], LARGE,
    )(own[RAW:], sw[RAW:], raw_beside)
    send, send2 = call(
        extend_kernel, "extend", (shape(R1 + EY, PZ), shape(2 * R1, PZ)), (VMEM,) * 2, [VMEM] * 7, [], SMALL
    )(rhs_below, rhs, rhs_above, xedge0, s1, inv1, coarse)

    one = across(send, 1)
    beside = from_beside(send[:R1])
    two = across(send2, 2)
    mine = call(join_kernel, "join", shape(O_END, PZ), VMEM, [VMEM] * 6, [], SMALL)(
        send, edge0, one, beside, two, raw_beside
    )
    its = swap(mine)

    edge, c1, pre1, rhs2, s1, w1, _, _ = call(
        middle_kernel, "level1_pre",
        (shape(2 * R2, PZ), shape(N1, R1, PZ), shape(10, R1, PZ), shape(4, R2, PZ)) + w1_shapes,
        (VMEM,) * 8, [VMEM] * 9,
        [scratch(N1, R1 + 2 * PAD, PZ)] * 3 + [scratch(4, R1, PZ), scratch(2, R2 + PAD, PZ)],
        LARGE, aliases={5: 4, 6: 5, 7: 6, 8: 7},
    )(send, one, beside, two, its, s1, w1, inv1, d1)

    w2, inv2, last2 = call(
        coarse_coefficients_kernel, "level2_coefficients",
        (shape(6, 12, R2, PZ), shape(12, R2, PZ), shape(4, R2 + PAD, PZ)),
        (VMEM,) * 3, [VMEM] * 3, [scratch(4, 10, R2 + PAD, PZ)], LARGE,
    )(s1, two, its)
    count = lax.axis_size("wide")
    two2 = across(edge, 2, ((0, 2), (count - 1, count - 3)))
    its2 = swap(two2)
    return call(
        last_kernel, "coarse_and_post", shape(PX, PY, PZ), VMEM, [VMEM] * 14,
        [scratch(6, 1, R2, PZ), scratch(12, R2, PZ)] + [scratch(12, R2 + 2 * PAD, PZ)] * 3
        + [scratch(10, R1 + 2 * PAD, PZ)] * 3 + [scratch(8, EY + 2 * PAD, PZ)] * 2,
        LARGE,
    )(two2, its2, rhs2, w2, inv2, last2, pre1, w1, c1, pre0, its, one, w0, c0)


def solution(mesh):
    spec = P("wide", "narrow", None)
    return jax.shard_map(shards, mesh=mesh, in_specs=(spec,) * 5, out_specs=spec, check_vma=False)
```

```python
import jax
import jax.numpy as jnp
from jax import lax
from jax.experimental import pallas as pl
from jax.experimental.pallas import tpu as pltpu
from jax.sharding import PartitionSpec as P

F32 = jnp.float32
THETA = (2.0 + 0.25) / 2.0
DELTA = (2.0 - 0.25) / 2.0
SIGMA = THETA / DELTA
RHO = [1.0 / SIGMA]
for _step in range(3):
    RHO.append(1.0 / (2.0 * SIGMA - RHO[-1]))
MOMENTUM = [0.0] + [RHO[k] * RHO[k - 1] for k in range(1, 4)]
GAIN = [1.0 / THETA] + [2.0 * RHO[k] / DELTA for k in range(1, 4)]

PX, PY, PZ = 4, 64, 128
HY = 8
EY = PY + 2 * HY
H1 = PY // 2
G1 = 16
R1 = H1 + 2 * G1
R2 = R1 // 2
RAW = 5 * PX * EY
SRAW = 8 * EY
SIDE = 5 * PX * HY
PAD = 8
SMALL, LARGE = 1000, 2 * 10**10
B, ALPHA, BX, BY, BZ = range(5)
ANY = pl.BlockSpec(memory_space=pl.ANY)
VMEM = pl.BlockSpec(memory_space=pltpu.VMEM)
HBM = pl.BlockSpec(memory_space=pltpu.HBM)


def shape(*dims):
    return jax.ShapeDtypeStruct(dims, F32)


def scratch(*dims):
    return pltpu.VMEM(dims, F32)


def call(kernel, name, out_shape, out_specs, in_specs, scratch_shapes, flops, mib=24, aliases=None):
    return pl.pallas_call(
        kernel,
        out_shape=out_shape,
        in_specs=in_specs,
        out_specs=out_specs,
        scratch_shapes=scratch_shapes,
        compiler_params=pltpu.CompilerParams(vmem_limit_bytes=mib * 1024 * 1024),
        cost_estimate=pl.CostEstimate(flops=flops, bytes_accessed=0, transcendentals=0),
        input_output_aliases=aliases or {},
        name=name,
    )


def parity():
    return lax.rem(lax.axis_index("wide"), 2)


def lanes(rows):
    return lax.broadcasted_iota(jnp.int32, (rows, PZ), 1)


def moved(v, shift):
    return pltpu.roll(v, shift % PZ, 1)


def planes(lo, hi, each, unroll):
    if not unroll:
        each(lo)
        return
    steps = (hi - lo) // unroll

    def body(i, carry):
        for k in range(unroll):
            each(lo + i * unroll + k)
        return carry

    if steps > 1:
        lax.fori_loop(0, steps, body, 0)
    else:
        steps = 0
    for q in range(lo + steps * unroll, hi):
        each(q)


def defect(x_ref, c_ref, w_ref, q, r0, n, reach, cq, cr, wq, wr):
    rows = pl.ds(PAD + r0, n)
    here = pl.ds(wr + r0, n)
    x = x_ref[q, rows, :]
    total = c_ref[cq, pl.ds(cr + r0, n), :] - x
    total += w_ref[0, wq, here, :] * x_ref[q - 1, rows, :]
    total += w_ref[1, wq, here, :] * x_ref[q + 1, rows, :]
    total += w_ref[2, wq, here, :] * x_ref[q, pl.ds(PAD + r0 - 1, n), :]
    total += w_ref[3, wq, here, :] * x_ref[q, pl.ds(PAD + r0 + 1, n), :]
    total += w_ref[4, wq, here, :] * moved(x, reach)
    total += w_ref[5, wq, here, :] * moved(x, -reach)
    return x, total


def sweep(x_ref, prev_ref, c_ref, w_ref, lo, hi, rows, reach, k, store, chunk, woff=0, coff=0, wr=0, cr=0, unroll=8):
    def each(q):
        for r0 in range(rows[0], rows[1], chunk):
            n = min(chunk, rows[1] - r0)
            x, z = defect(x_ref, c_ref, w_ref, q, r0, n, reach, q + coff, cr, q + woff, wr)
            new = x + GAIN[k] * z
            if k > 0:
                gap = x if prev_ref is None else x - prev_ref[q, pl.ds(PAD + r0, n), :]
                new += MOMENTUM[k] * gap
            store(q, r0, n, new)

    planes(lo, hi, each, unroll)


def into(ref):
    def store(q, r0, n, v):
        ref[q, pl.ds(PAD + r0, n), :] = v

    return store


def inverse(d):
    inside = d > 0.0
    return jnp.where(inside, 1.0 / jnp.where(inside, d, 1.0), 0.0)


def faces(alpha, x0, x1, y0, y1, z0, reach, scale):
    z1 = moved(z0, -reach)
    d = alpha + scale * (x0 + x1 + y0 + y1 + z0 + z1)
    inv = inverse(d)
    si = scale * inv
    return d, inv, [si * f for f in (x0, x1, y0, y1, z0, z1)]


def next_rows(load, r0, n, rows):
    if r0 + n < rows:
        return load(r0 + 1, n)
    return pltpu.roll(load(r0, n), n - 1, 0)


def clear_pads(ref, rows):
    ref[:, :PAD, :] = jnp.zeros((ref.shape[0], PAD, PZ), F32)
    ref[:, PAD + rows :, :] = jnp.zeros((ref.shape[0], PAD, PZ), F32)


def pair_lanes(v, reach):
    low = (lanes(v.shape[0]) & reach) == 0
    return v + jnp.where(low, moved(v, -reach), moved(v, reach))


def low_lanes(v, reach):
    low = (lanes(v.shape[0]) & reach) == 0
    return jnp.where(low, v, moved(v, reach))


def pack2(v0, v1):
    return jnp.where((lanes(v0.shape[0]) & 1) == 0, v0, v1)


def unpack2(v):
    even = (lanes(v.shape[0]) & 1) == 0
    return jnp.where(even, v, moved(v, 1)), jnp.where(even, moved(v, -1), v)


def pack4(items):
    place = lanes(items[0].shape[0]) & 3
    out = items[0]
    for i, item in enumerate(items[1:], 1):
        out = jnp.where(place == i, item, out)
    return out


def unpack4(v, i):
    place = lanes(v.shape[0]) & 3
    out = v
    for m in range(4):
        if m != i:
            out = jnp.where(place == m, moved(v, m - i), out)
    return out


def coarser(load, rows, reach):
    def cell(i):
        return load(i, 0, 0) + load(i, 0, 1) + load(i, 1, 0) + load(i, 1, 1)

    al = pair_lanes(cell(0), reach) * 0.125
    bx = pair_lanes(load(1, 0, 0) + load(1, 0, 1), reach) * 0.25
    by = pair_lanes(load(2, 0, 0) + load(2, 1, 0), reach) * 0.25
    bz = low_lanes(cell(3), reach) * 0.25
    return al, bx, by, bz


def pack_kernel(b, al, bx, by, bz, a, lo_out, hi_out, raw, sems):
    wide, narrow = lax.axis_index("wide"), lax.axis_index("narrow")
    copies = [pltpu.make_async_copy(ref, a.at[i], sems.at[i]) for i, ref in enumerate((b, al, bx, by, bz))]
    for c in copies:
        c.start()
    for c in copies:
        c.wait()
    row = lax.broadcasted_iota(jnp.int32, (PAD, PZ), 0)
    first_row = jnp.logical_and(row == 0, jnp.broadcast_to(narrow, (PAD, PZ)) == 0)
    a[BX, 0] = jnp.where(jnp.broadcast_to(wide, (PY, PZ)) == 0, 0.0, a[BX, 0])
    first_z = lanes(PY) == 0
    for p in range(PX):
        a[BY, p, :PAD] = jnp.where(first_row, 0.0, a[BY, p, :PAD])
        a[BZ, p] = jnp.where(first_z, 0.0, a[BZ, p])
    got = []
    for c in range(2):

        def load(i, k, row):
            return a[i + 1, 2 * c + k, pl.ds(row, H1, 2), :]

        got.append(coarser(load, H1, 1))
    for i in range(4):
        v = pack2(got[0][i], got[1][i])
        raw[i] = v
        lo_out[pl.ds(SIDE + G1 * i, G1), :] = v[:G1]
        hi_out[pl.ds(SIDE + G1 * i, G1), :] = v[H1 - G1 :]
    for i in range(5):
        for p in range(PX):
            here = pl.ds((PX * i + p) * HY, HY)
            lo_out[here, :] = a[i, p, :HY]
            hi_out[here, :] = a[i, p, PY - HY :]


def plane(ref, k, r0=0, n=EY):
    start = k * EY + r0
    return ref[pl.ds(pl.multiple_of(start, 8) if r0 % 8 == 0 else start, n), :]


def corner_kernel(a, raw, lo, hi, own, sw, xs, x, v):
    par = parity()
    for i in range(5):
        for p in range(PX):
            k = PX * i + p
            own[pl.ds(k * EY, HY), :] = lo[pl.ds(k * HY, HY), :]
            own[pl.ds(k * EY + HY, PY), :] = a[i, p]
            own[pl.ds(k * EY + HY + PY, HY), :] = hi[pl.ds(k * HY, HY), :]
    for i in range(4):
        here = pl.ds(SIDE + G1 * i, G1)
        for ref, base in ((own, RAW + R1 * i), (sw, SRAW + R1 * i)):
            ref[pl.ds(base, G1), :] = lo[here, :]
            ref[pl.ds(base + G1, H1), :] = raw[i]
            ref[pl.ds(base + G1 + H1, G1), :] = hi[here, :]
    xs[pl.ds(SRAW, R1), :] = own[pl.ds(RAW + R1, R1), :]
    for i in range(5):
        here = pl.ds(i * EY, EY)
        xs[here, :] = plane(own, PX * i + 3 * par)
        sw[here, :] = plane(own, PX * i + 3 - 3 * par)
    clear_pads(x, EY)
    body = pl.ds(PAD, EY)
    kept = []
    for p in range(3):
        by = plane(own, PX * BY + p)
        _, inv, w = faces(
            plane(own, PX * ALPHA + p), plane(own, PX * BX + p), plane(own, PX * BX + p + 1), by,
            pltpu.roll(by, EY - 1, 0), plane(own, PX * BZ + p), 1, 1.0,
        )
        c0 = inv * plane(own, PX * B + p)
        x[p, body, :] = c0 * (1.0 / THETA)
        kept.append((w, c0))
    for up in range(2):
        second = 1 + up
        w, c0 = kept[second]
        here = x[second, body, :]
        z = c0 - here + w[0] * x[second - 1, body, :]
        if not up:
            z += w[1] * x[2, body, :]
        z += w[2] * x[second, pl.ds(PAD - 1, EY), :] + w[3] * x[second, pl.ds(PAD + 1, EY), :]
        z += w[4] * moved(here, 1) + w[5] * moved(here, -1)
        v[up, pl.ds(0, EY), :] = here
        v[up, pl.ds(EY, EY), :] = here + GAIN[1] * z + MOMENTUM[1] * here
        v[up, pl.ds(2 * EY, EY), :] = w[1] if up else plane(own, PX * BX + second)
    xs[pl.ds(5 * EY, 3 * EY), :] = v[par]
    sw[pl.ds(5 * EY, 3 * EY), :] = v[1 - par]


Q0 = 3


def fine_kernel(own, sw, xs, _, rhs, rhs_lo, rhs_hi, edge, xedge, pre, w, cc, sx, d, x, y, z, t):
    par = parity()
    sides2 = ((xs, par), (sw, 1 - par))
    for p in range(PX):
        sx[Q0 + p] = plane(own, PX * BX + p)
    for ref, above in sides2:
        sx[2 + 5 * above] = plane(ref, BX)
        sx[9 - above] = plane(ref, 7)
    clear_pads(x, EY)
    clear_pads(y, EY)
    chunk = 40

    def prepare(q, get):
        for r0 in range(0, EY, chunk):
            here = pl.ds(r0, chunk)

            def load(i):
                return lambda r, n: get(i, r, n)

            dd, inv, w6 = faces(
                load(ALPHA)(r0, chunk), sx[q, here, :], sx[q + 1, here, :], load(BY)(r0, chunk),
                next_rows(load(BY), r0, chunk, EY), load(BZ)(r0, chunk), 1, 1.0,
            )
            for a, f in enumerate(w6):
                w[a, q, here, :] = f
            c0 = inv * load(B)(r0, chunk)
            cc[q, here, :] = c0
            x[q, pl.ds(PAD + r0, chunk), :] = c0 * (1.0 / THETA)
            d[q, here, :] = dd

    for p in range(PX):
        prepare(Q0 + p, lambda i, r, n: plane(own, PX * i + p, r, n))
    body = pl.ds(PAD, EY)
    for ref, above in sides2:
        q = 2 + 5 * above
        prepare(q, lambda i, r, n: plane(ref, i, r, n))
        x[1 + 7 * above, body, :] = plane(ref, 5)
        missing = GAIN[1] * plane(ref, 7) * x[q, body, :]
        below = jnp.broadcast_to(above, missing.shape) == 0
        y[1 + 7 * above, body, :] = plane(ref, 6) + jnp.where(below, missing, 0.0)

    rows = (0, EY)
    sweep(x, None, cc, w, 2, 8, rows, 1, 1, into(y), chunk)
    sweep(y, x, cc, w, 2, 8, rows, 1, 2, into(z), chunk)
    got = []
    for c in range(2):
        for r0 in range(0, EY, chunk):
            v = 0.0
            for q in (Q0 + 2 * c, Q0 + 2 * c + 1):
                _, zz = defect(z, cc, w, q, r0, chunk, 1, q, 0, q, 0)
                v = v + d[q, pl.ds(r0, chunk), :] * zz
            t[c, pl.ds(r0, chunk), :] = v
        got.append(pair_lanes(t[c, pl.ds(HY, H1, 2), :] + t[c, pl.ds(HY + 1, H1, 2), :], 1) * 0.125)
    v = pack2(got[0], got[1])
    rhs[...] = v
    rhs_lo[...] = v[:G1]
    rhs_hi[...] = v[H1 - G1 :]
    mid = pl.ds(PAD, EY)
    edge[...] = z[Q0 + 2 - par, mid, :]
    xedge[...] = z[Q0 + 1 + par, mid, :]
    for p in range(6):
        pre[p] = z[Q0 - 1 + p, mid, :]


C0 = 5
N1 = 14
M0 = 5
S_SHAPE = (4, N1, R1 + 2 * PAD, PZ)
O_EDGE = R1
O_ONE = O_EDGE + EY
O_BESIDE = O_ONE + R1
O_TWO = O_BESIDE + R1
O_RAW = O_TWO + 2 * R1
O_END = O_RAW + 8 * R1


def place_coefficients(s, i, e, v):
    v0, v1 = unpack2(v)
    s[i, 1 + 2 * e, pl.ds(PAD, R1), :] = v0
    s[i, 2 + 2 * e, pl.ds(PAD, R1), :] = v1


def middle_faces(s, w1, inv1, d1, q):
    for r0 in range(0, R1, 32):
        here, up, out = pl.ds(PAD + r0, 32), pl.ds(PAD + r0 + 1, 32), pl.ds(r0, 32)
        dd, inv, w6 = faces(
            s[0, q, here, :], s[1, q, here, :], s[1, q + 1, here, :], s[2, q, here, :], s[2, q, up, :],
            s[3, q, here, :], 2, 0.25,
        )
        for a, f in enumerate(w6):
            w1[a, q, out, :] = f
        inv1[q, out, :] = inv
        d1[q, out, :] = dd


def sides(par, k):
    lower, upper = 1 - k, 4 + k
    return jnp.where(par == 0, lower, upper), jnp.where(par == 0, upper, lower)


def level2_load(s, plane):
    def load(i, k, row):
        return s[i, 2 * plane + C0 + k, pl.ds(PAD + row, R2, 2), :]

    return load


def near_coefficients_kernel(own, other, one, beside, s, w1, inv1, d1):
    par = parity()
    for i in range(4):
        s[i, :, PAD + R1 :, :] = jnp.zeros((N1, PAD, PZ), F32)
        rows = pl.ds(R1 * i, R1)
        sent = pl.ds(R1 * (1 + i), R1)
        place_coefficients(s, i, 2 + par, own[rows, :])
        place_coefficients(s, i, 3 - par, other[rows, :])
        place_coefficients(s, i, sides(par, 0)[0], one[sent, :])
        place_coefficients(s, i, sides(par, 1)[0], beside[sent, :])
    for k in range(7):
        middle_faces(s, w1, inv1, d1, 1 + 4 * par + k)


def chip_coefficients_kernel(own, other, xs, out, s, u):
    par = parity()
    for i in range(4):
        rows = pl.ds(R1 * i, R1)
        for p, ref in ((par, own), (1 - par, other)):
            v0, v1 = unpack2(ref[rows, :])
            s[i, 2 * p] = v0
            s[i, 2 * p + 1] = v1
    s[1, 4] = unpack2(xs[pl.ds(SRAW, R1), :])[0]
    q = 3 * par
    u[:R1] = s[2, q]
    u[R1:] = jnp.zeros((PAD, PZ), F32)
    _, inv, _ = faces(s[0, q], s[1, q], s[1, q + 1], u[:R1], u[pl.ds(1, R1), :], s[3, q], 2, 0.25)
    out[:R1] = inv * (1.0 / THETA)
    out[pl.ds(R1, R1), :] = s[1, q]
    for c in range(2):

        def load(i, k, row):
            return s[i, 2 * c + k, pl.ds(row, R2, 2), :]

        out[pl.ds(2 * R1 + R2 * c, R2), :] = pack4(coarser(load, R2, 2))


def extend_kernel(lo, rhs, hi, xedge, raw, chip, send, send1, send2):
    par = parity()
    for out in (send, send1):
        out[:G1] = lo[...]
        out[pl.ds(G1, H1), :] = rhs[...]
        out[pl.ds(G1 + H1, G1), :] = hi[...]
        out[pl.ds(R1, 4 * R1), :] = raw[...]
    send[pl.ds(5 * R1, EY), :] = xedge[...]
    v = send[:R1]
    odd = jnp.broadcast_to(par, v.shape)
    v0, v1 = unpack2(v)
    send2[:R1] = pack2(chip[:R1] * jnp.where(odd == 0, v0, v1), chip[pl.ds(R1, R1), :])
    send2[R1:] = chip[pl.ds(2 * R1, R1), :]


def join_kernel(own, edge, one, beside, two, out):
    out[:R1] = own[:R1]
    out[pl.ds(O_EDGE, EY), :] = edge[...]
    out[pl.ds(O_ONE, R1), :] = one[:R1]
    out[pl.ds(O_BESIDE, R1), :] = beside[:R1]
    out[pl.ds(O_TWO, 2 * R1), :] = two[...]
    out[pl.ds(O_RAW, 4 * R1), :] = one[pl.ds(R1, 4 * R1), :]
    out[pl.ds(O_RAW + 4 * R1, 4 * R1), :] = beside[pl.ds(R1, 4 * R1), :]


def tick_kernel(_, out):
    out[...] = jnp.zeros(out.shape, F32)


def first_to_arrive(v):
    return call(tick_kernel, "tick", shape(PAD, PZ), VMEM, [ANY], [], LARGE)(v)


def both_sides(par, mine, its):
    upper = jnp.broadcast_to(par, mine.shape) == 1
    return jnp.where(upper, its, mine), jnp.where(upper, mine, its)


def middle_kernel(own, one, beside, two, its, s_in, w_in, inv_in, d_in, edge, cc, pre, rhs, s, w, inv, d,
                  x, y, z, t, u):
    par = parity()
    clear_pads(x, R1)
    clear_pads(y, R1)
    body = pl.ds(PAD, R1)
    lower, upper = both_sides(par, two[:R1], its[pl.ds(O_TWO, R1), :])
    x[0, body, :] = unpack2(lower)[0]
    x1, bx = unpack2(upper)
    x[N1 - 1, body, :] = x1
    s[1, N1 - 1, body, :] = bx
    for k in range(2):
        e = sides(par, k)[1]
        for i in range(4):
            place_coefficients(s, i, e, its[pl.ds(O_RAW + (4 * k + i) * R1, R1), :])
    for k in range(5):
        middle_faces(s, w, inv, d, jnp.where(par == 0, 8 + k, 1 + k if k < 4 else 12))

    def place(e, v):
        for k, b in enumerate(unpack2(v)):
            q = 1 + 2 * e + k
            c0 = inv[q] * b
            cc[q] = c0
            x[q, body, :] = c0 * (1.0 / THETA)

    place(2 + par, own[:R1])
    place(3 - par, its[:R1])
    for k, ref, row in ((0, one, O_ONE), (1, beside, O_BESIDE)):
        e, f = sides(par, k)
        place(e, ref[:R1])
        place(f, its[pl.ds(row, R1), :])

    rows = (0, R1)
    sweep(x, None, cc, w, 1, 13, rows, 2, 1, into(y), 32, unroll=12)
    sweep(y, x, cc, w, 2, 12, rows, 2, 2, into(z), 32, unroll=10)

    for c in range(4):
        for r0 in range(0, R1, 32):
            v = 0.0
            for k in range(2):
                q = C0 - 2 + 2 * c + k
                _, zz = defect(z, cc, w, q, r0, 32, 2, q, 0, q, 0)
                v = v + d[q, pl.ds(r0, 32), :] * zz
            t[c, pl.ds(r0, 32), :] = v
        rhs[c] = pair_lanes(t[c, pl.ds(0, R2, 2), :] + t[c, pl.ds(1, R2, 2), :], 2) * 0.125

    def first(k, plane):
        al, bx, by, bz = coarser(level2_load(s, plane), R2, 2)
        after = level2_load(s, plane + 1)
        bx1 = pair_lanes(after(1, 0, 0) + after(1, 0, 1), 2) * 0.25
        u[k, pl.ds(0, R2), :] = by
        u[k, pl.ds(R2, PAD), :] = jnp.zeros((PAD, PZ), F32)
        _, inv2, _ = faces(al, bx, bx1, by, u[k, pl.ds(1, R2), :], bz, 4, 0.0625)
        return inv2 * rhs[plane + 1] * (1.0 / THETA), bx

    below, above = first(0, -1), first(1, 2)
    up = pack4([rhs[3], rhs[2], rhs[1], below[0]])
    down = pack4([rhs[0], rhs[1], rhs[2], above[0]])
    wide = jnp.broadcast_to(lax.axis_index("wide"), up.shape)
    ends = (lanes(R2) & 3) == 0
    down = jnp.where(wide == 0, jnp.where(ends, rhs[1], 0.0), down)
    up = jnp.where(wide == lax.axis_size("wide") - 1, jnp.where(ends, rhs[2], 0.0), up)
    edge[:R2] = jnp.where(jnp.broadcast_to(par, up.shape) == 0, down, up)
    edge[R2:] = above[1]
    for p in range(10):
        pre[p] = z[C0 - 3 + p, body, :]


def coarse_coefficients_kernel(s, two, its, w2, inv2, last, s2):
    par = parity()
    for c in range(2, 8):
        for i, v in enumerate(coarser(level2_load(s, c - 4), R2, 2)):
            s2[i, c, pl.ds(0, R2), :] = v
    for k in range(2):
        rows = pl.ds(R1 + R2 * k, R2)
        lower, upper = both_sides(par, two[rows, :], its[pl.ds(O_TWO + R1 + R2 * k, R2), :])
        for i in range(4):
            s2[i, k, pl.ds(0, R2), :] = unpack4(lower, i)
            s2[i, 8 + k, pl.ds(0, R2), :] = unpack4(upper, i)
    s2[2, :, R2:, :] = jnp.zeros((10, PAD, PZ), F32)
    body = pl.ds(0, R2)
    for c in range(9):
        _, inv, w6 = faces(
            s2[0, c, body, :], s2[1, c, body, :], s2[1, c + 1, body, :], s2[2, c, body, :], s2[2, c, pl.ds(1, R2), :],
            s2[3, c, body, :], 4, 0.0625,
        )
        for a, f in enumerate(w6):
            w2[a, c + 1] = f
        inv2[c + 1] = inv
    for i in range(4):
        last[i] = s2[i, 9]


def last_kernel(two2, its2, rhs, w2, inv2, last, pre1, w1, c1, pre0, sw, xs, w0, c0, out,
                wx, c2, x2, y2, z2, x1, y1, z1, x0, y0):
    par = parity()
    body = pl.ds(PAD, R2)
    lo, hi = both_sides(par, two2[:R2], its2[:R2])
    _, beyond = both_sides(par, two2[R2:], its2[R2:])
    clear_pads(x2, R2)
    clear_pads(y2, R2)
    clear_pads(z2, R2)
    _, inv, w6 = faces(
        last[0, :R2], last[1, :R2], beyond, last[2, :R2], last[2, pl.ds(1, R2), :], last[3, :R2], 4, 0.0625
    )
    for a, f in enumerate(w6):
        wx[a, 0] = f

    def start(j, b, dinv):
        v = dinv * b
        c2[j] = v
        x2[j, body, :] = v * (1.0 / THETA)

    for k in range(3):
        start(3 - k, unpack4(lo, k), inv2[3 - k])
        start(8 + k, unpack4(hi, k), inv2[8 + k] if k < 2 else inv)
    for c in range(4):
        start(c + 4, rhs[c], inv2[c + 4])
    x2[0, body, :] = unpack4(lo, 3)
    x2[11, body, :] = unpack4(hi, 3)
    rows = (0, R2)
    sweep(x2, None, c2, w2, 1, 10, rows, 4, 1, into(y2), R2, unroll=9)
    sweep(x2, None, c2, wx, 10, 11, rows, 4, 1, into(y2), R2, woff=-10)
    sweep(y2, x2, c2, w2, 2, 10, rows, 4, 2, into(z2), R2, unroll=8)
    sweep(z2, y2, c2, w2, 3, 9, rows, 4, 3, into(x2), R2, unroll=6)

    clear_pads(x1, R1)
    clear_pads(y1, R1)
    for q in range(10):
        v = x2[(q - 3) // 2 + M0, body, :]
        z1[q, pl.ds(PAD, R2, 2), :] = v
        z1[q, pl.ds(PAD + 1, R2, 2), :] = v
        x1[q, pl.ds(PAD, R1), :] = pre1[q] + z1[q, pl.ds(PAD, R1), :]
    rows = (0, R1)
    off = C0 - 3
    sweep(x1, None, c1, w1, 1, 9, rows, 2, 0, into(y1), 32, woff=off, coff=off)
    sweep(y1, x1, c1, w1, 2, 8, rows, 2, 1, into(z1), 32, woff=off, coff=off, unroll=6)

    clear_pads(x0, EY)
    clear_pads(y0, EY)
    near, far = 7 - 7 * par, 7 * par
    body = pl.ds(PAD, EY)
    for q in range(8):
        v = z1[(q - 2) // 2 + 3 + 2 * par, pl.ds(PAD + 12, EY // 2), :]
        x0[q, pl.ds(PAD, EY // 2, 2), :] = v
        x0[q, pl.ds(PAD + 1, EY // 2, 2), :] = v
        if 0 < q < 7:
            x0[q, body, :] += pre0[q - 1]
    x0[near, body, :] += sw[pl.ds(O_EDGE, EY), :]
    x0[far, body, :] += xs[pl.ds(5 * R1, EY), :]
    off = Q0 - 2
    sweep(x0, None, c0, w0, 1, 7, (0, EY), 1, 0, into(y0), 40, woff=off, coff=off, unroll=6)

    def finish(q, r0, n, v):
        out[q - 2, pl.ds(r0 - 8, n), :] = v

    sweep(y0, x0, c0, w0, 2, 6, (8, 8 + PY), 1, 1, finish, 32, woff=off, coff=off, unroll=4)


def swap(v):
    return lax.ppermute(v, "wide", [(i, i ^ 1) for i in range(lax.axis_size("wide"))])


def across(v, chips, ends=()):
    count = lax.axis_size("wide")
    step = 2 * chips - 1
    pairs = [(i, i + step) for i in range(1, count, 2) if i + step < count]
    pairs += [(i, i - step) for i in range(0, count, 2) if i - step >= 0]
    return lax.ppermute(v, "wide", pairs + list(ends))


def from_beside(v):
    count = lax.axis_size("wide")
    pairs = [(i, i + 2) for i in range(0, count - 2, 2)] + [(i, i - 2) for i in range(3, count, 2)]
    return lax.ppermute(v, "wide", pairs)


def shifted(v, axis, step):
    count = lax.axis_size(axis)
    return lax.ppermute(v, axis, [(i, i + step) for i in range(count) if 0 <= i + step < count])


def shards(right_side, alpha_coef, beta_x, beta_y, beta_z):
    a, ylo, yhi, raw = call(
        pack_kernel, "pack",
        (shape(5, PX, PY, PZ), shape(SIDE + 4 * G1, PZ), shape(SIDE + 4 * G1, PZ), shape(4, H1, PZ)),
        (VMEM,) * 4, [ANY] * 5, [pltpu.SemaphoreType.DMA((5,))], SMALL,
    )(*[pltpu.with_memory_space_constraint(v, pltpu.HBM) for v in (right_side, alpha_coef, beta_x, beta_y, beta_z)])
    lo = shifted(yhi, "narrow", 1)
    hi = shifted(ylo, "narrow", -1)
    own, sw, xs = call(
        corner_kernel, "corners", (shape(RAW + 4 * R1, PZ), shape(SRAW + 4 * R1, PZ), shape(SRAW + R1, PZ)),
        (VMEM,) * 3, [VMEM] * 4, [scratch(3, EY + 2 * PAD, PZ), scratch(2, 3 * EY, PZ)], SMALL,
    )(a, raw, lo, hi)
    xs = across(xs, 1)
    sw = swap(sw)

    rhs, rhs_lo, rhs_hi, edge0, xedge0, pre0, w0, c0 = call(
        fine_kernel, "level0_pre",
        (shape(H1, PZ), shape(G1, PZ), shape(G1, PZ), shape(EY, PZ), shape(EY, PZ), shape(6, EY, PZ),
         shape(6, 10, EY, PZ), shape(10, EY, PZ)),
        (VMEM,) * 8, [VMEM] * 3 + [ANY],
        [scratch(10, EY, PZ), scratch(10, EY, PZ)] + [scratch(10, EY + 2 * PAD, PZ)] * 3 + [scratch(2, EY, PZ)],
        LARGE,
    )(own, sw, xs, first_to_arrive(xs))
    rhs_below = shifted(rhs_hi, "narrow", 1)
    rhs_above = shifted(rhs_lo, "narrow", -1)
    chip = call(
        chip_coefficients_kernel, "chip_coefficients", shape(3 * R1, PZ), VMEM, [VMEM] * 3,
        [scratch(4, 5, R1, PZ), scratch(R1 + PAD, PZ)], LARGE,
    )(own[RAW:], sw[SRAW:], xs)
    send, send1, send2 = call(
        extend_kernel, "extend", (shape(5 * R1 + EY, PZ), shape(5 * R1, PZ), shape(2 * R1, PZ)), (VMEM,) * 3,
        [VMEM] * 6, [], SMALL,
    )(rhs_below, rhs, rhs_above, xedge0, own[RAW:], chip)

    one = across(send, 1)
    beside = from_beside(send1)
    two = across(send2, 2)
    mine = call(join_kernel, "join", shape(O_END, PZ), VMEM, [VMEM] * 5, [], SMALL)(send, edge0, one, beside, two)
    its = swap(mine)
    w1_shapes = (shape(*S_SHAPE), shape(6, N1, R1, PZ), shape(N1, R1, PZ), shape(N1, R1, PZ))
    s1, w1, inv1, d1 = call(
        near_coefficients_kernel, "near_coefficients", w1_shapes, (VMEM,) * 4, [VMEM] * 4, [], LARGE,
    )(own[RAW:], sw[SRAW:], one, beside)

    edge, c1, pre1, rhs2, s1, w1, _, _ = call(
        middle_kernel, "level1_pre",
        (shape(2 * R2, PZ), shape(N1, R1, PZ), shape(10, R1, PZ), shape(4, R2, PZ)) + w1_shapes,
        (VMEM,) * 8, [VMEM] * 9,
        [scratch(N1, R1 + 2 * PAD, PZ)] * 3 + [scratch(4, R1, PZ), scratch(2, R2 + PAD, PZ)],
        LARGE, aliases={5: 4, 6: 5, 7: 6, 8: 7},
    )(send, one, beside, two, its, s1, w1, inv1, d1)

    w2, inv2, last2 = call(
        coarse_coefficients_kernel, "level2_coefficients",
        (shape(6, 12, R2, PZ), shape(12, R2, PZ), shape(4, R2 + PAD, PZ)),
        (VMEM,) * 3, [VMEM] * 3, [scratch(4, 10, R2 + PAD, PZ)], LARGE,
    )(s1, two, its)
    count = lax.axis_size("wide")
    two2 = across(edge, 2, ((0, 2), (count - 1, count - 3)))
    its2 = swap(two2)
    return call(
        last_kernel, "coarse_and_post", shape(PX, PY, PZ), VMEM, [VMEM] * 14,
        [scratch(6, 1, R2, PZ), scratch(12, R2, PZ)] + [scratch(12, R2 + 2 * PAD, PZ)] * 3
        + [scratch(10, R1 + 2 * PAD, PZ)] * 3 + [scratch(8, EY + 2 * PAD, PZ)] * 2,
        LARGE,
    )(two2, its2, rhs2, w2, inv2, last2, pre1, w1, c1, pre0, its, one, w0, c0)


def solution(mesh):
    spec = P("wide", "narrow", None)
    return jax.shard_map(shards, mesh=mesh, in_specs=(spec,) * 5, out_specs=spec, check_vma=False)
```

```python
import jax
import jax.numpy as jnp
from jax import lax
from jax.experimental import pallas as pl
from jax.experimental.pallas import tpu as pltpu
from jax.sharding import PartitionSpec as P

F32 = jnp.float32
THETA = (2.0 + 0.25) / 2.0
DELTA = (2.0 - 0.25) / 2.0
SIGMA = THETA / DELTA
RHO = [1.0 / SIGMA]
for _step in range(3):
    RHO.append(1.0 / (2.0 * SIGMA - RHO[-1]))
MOMENTUM = [0.0] + [RHO[k] * RHO[k - 1] for k in range(1, 4)]
GAIN = [1.0 / THETA] + [2.0 * RHO[k] / DELTA for k in range(1, 4)]

PX, PY, PZ = 4, 64, 128
HY = 32
EY = PY + 2 * HY
MID = PY + 16
MID0 = HY - 8
R1 = EY // 2
R2 = R1 // 2
RAW = 5 * PX * EY
SRAW = 8 * EY
PAD = 8
SMALL, LARGE = 1000, 2 * 10**10
B, ALPHA, BX, BY, BZ = range(5)
ANY = pl.BlockSpec(memory_space=pl.ANY)
VMEM = pl.BlockSpec(memory_space=pltpu.VMEM)
HBM = pl.BlockSpec(memory_space=pltpu.HBM)


def shape(*dims):
    return jax.ShapeDtypeStruct(dims, F32)


def scratch(*dims):
    return pltpu.VMEM(dims, F32)


def call(kernel, name, out_shape, out_specs, in_specs, scratch_shapes, flops, mib=24, aliases=None):
    return pl.pallas_call(
        kernel,
        out_shape=out_shape,
        in_specs=in_specs,
        out_specs=out_specs,
        scratch_shapes=scratch_shapes,
        compiler_params=pltpu.CompilerParams(vmem_limit_bytes=mib * 1024 * 1024),
        cost_estimate=pl.CostEstimate(flops=flops, bytes_accessed=0, transcendentals=0),
        input_output_aliases=aliases or {},
        name=name,
    )


def parity():
    return lax.rem(lax.axis_index("wide"), 2)


def lanes(rows):
    return lax.broadcasted_iota(jnp.int32, (rows, PZ), 1)


def moved(v, shift):
    return pltpu.roll(v, shift % PZ, 1)


def planes(lo, hi, each, unroll):
    if not unroll:
        each(lo)
        return
    steps = (hi - lo) // unroll

    def body(i, carry):
        for k in range(unroll):
            each(lo + i * unroll + k)
        return carry

    if steps > 1:
        lax.fori_loop(0, steps, body, 0)
    else:
        steps = 0
    for q in range(lo + steps * unroll, hi):
        each(q)


def defect(x_ref, c_ref, w_ref, q, r0, n, reach, cq, cr, wq, wr):
    rows = pl.ds(PAD + r0, n)
    here = pl.ds(wr + r0, n)
    x = x_ref[q, rows, :]
    total = c_ref[cq, pl.ds(cr + r0, n), :] - x
    total += w_ref[0, wq, here, :] * x_ref[q - 1, rows, :]
    total += w_ref[1, wq, here, :] * x_ref[q + 1, rows, :]
    total += w_ref[2, wq, here, :] * x_ref[q, pl.ds(PAD + r0 - 1, n), :]
    total += w_ref[3, wq, here, :] * x_ref[q, pl.ds(PAD + r0 + 1, n), :]
    total += w_ref[4, wq, here, :] * moved(x, reach)
    total += w_ref[5, wq, here, :] * moved(x, -reach)
    return x, total


def sweep(x_ref, prev_ref, c_ref, w_ref, lo, hi, rows, reach, k, store, chunk, woff=0, coff=0, wr=0, cr=0, unroll=8):
    def each(q):
        for r0 in range(rows[0], rows[1], chunk):
            n = min(chunk, rows[1] - r0)
            x, z = defect(x_ref, c_ref, w_ref, q, r0, n, reach, q + coff, cr, q + woff, wr)
            new = x + GAIN[k] * z
            if k > 0:
                gap = x if prev_ref is None else x - prev_ref[q, pl.ds(PAD + r0, n), :]
                new += MOMENTUM[k] * gap
            store(q, r0, n, new)

    planes(lo, hi, each, unroll)


def into(ref):
    def store(q, r0, n, v):
        ref[q, pl.ds(PAD + r0, n), :] = v

    return store


def inverse(d):
    inside = d > 0.0
    return jnp.where(inside, 1.0 / jnp.where(inside, d, 1.0), 0.0)


def faces(alpha, x0, x1, y0, y1, z0, reach, scale):
    z1 = moved(z0, -reach)
    d = alpha + scale * (x0 + x1 + y0 + y1 + z0 + z1)
    inv = inverse(d)
    si = scale * inv
    return d, inv, [si * f for f in (x0, x1, y0, y1, z0, z1)]


def next_rows(load, r0, n, rows):
    if r0 + n < rows:
        return load(r0 + 1, n)
    return pltpu.roll(load(r0, n), n - 1, 0)


def clear_pads(ref, rows):
    ref[:, :PAD, :] = jnp.zeros((ref.shape[0], PAD, PZ), F32)
    ref[:, PAD + rows :, :] = jnp.zeros((ref.shape[0], PAD, PZ), F32)


def pair_lanes(v, reach):
    low = (lanes(v.shape[0]) & reach) == 0
    return v + jnp.where(low, moved(v, -reach), moved(v, reach))


def low_lanes(v, reach):
    low = (lanes(v.shape[0]) & reach) == 0
    return jnp.where(low, v, moved(v, reach))


def pack2(v0, v1):
    return jnp.where((lanes(v0.shape[0]) & 1) == 0, v0, v1)


def unpack2(v):
    even = (lanes(v.shape[0]) & 1) == 0
    return jnp.where(even, v, moved(v, 1)), jnp.where(even, moved(v, -1), v)


def pack4(items):
    place = lanes(items[0].shape[0]) & 3
    out = items[0]
    for i, item in enumerate(items[1:], 1):
        out = jnp.where(place == i, item, out)
    return out


def unpack4(v, i):
    place = lanes(v.shape[0]) & 3
    out = v
    for m in range(4):
        if m != i:
            out = jnp.where(place == m, moved(v, m - i), out)
    return out


def coarser(load, rows, reach):
    def cell(i):
        return load(i, 0, 0) + load(i, 0, 1) + load(i, 1, 0) + load(i, 1, 1)

    al = pair_lanes(cell(0), reach) * 0.125
    bx = pair_lanes(load(1, 0, 0) + load(1, 0, 1), reach) * 0.25
    by = pair_lanes(load(2, 0, 0) + load(2, 1, 0), reach) * 0.25
    bz = low_lanes(cell(3), reach) * 0.25
    return al, bx, by, bz


def pack_kernel(b, al, bx, by, bz, a, lo_out, hi_out, sems):
    wide, narrow = lax.axis_index("wide"), lax.axis_index("narrow")
    copies = [pltpu.make_async_copy(ref, a.at[i], sems.at[i]) for i, ref in enumerate((b, al, bx, by, bz))]
    for c in copies:
        c.start()
    for c in copies:
        c.wait()
    row = lax.broadcasted_iota(jnp.int32, (PAD, PZ), 0)
    first_row = jnp.logical_and(row == 0, jnp.broadcast_to(narrow, (PAD, PZ)) == 0)
    a[BX, 0] = jnp.where(jnp.broadcast_to(wide, (PY, PZ)) == 0, 0.0, a[BX, 0])
    first_z = lanes(PY) == 0
    for p in range(PX):
        a[BY, p, :PAD] = jnp.where(first_row, 0.0, a[BY, p, :PAD])
        a[BZ, p] = jnp.where(first_z, 0.0, a[BZ, p])
    for i in range(5):
        for p in range(PX):
            here = pl.ds((PX * i + p) * HY, HY)
            lo_out[here, :] = a[i, p, :HY]
            hi_out[here, :] = a[i, p, PY - HY :]


def plane(ref, k, r0=0, n=EY):
    start = k * EY + r0
    return ref[pl.ds(pl.multiple_of(start, 8) if r0 % 8 == 0 else start, n), :]


def corner_kernel(a, lo, hi, own, sw, xs, x, v):
    par = parity()
    for i in range(5):
        for p in range(PX):
            k = PX * i + p
            own[pl.ds(k * EY, HY), :] = lo[pl.ds(k * HY, HY), :]
            own[pl.ds(k * EY + HY, PY), :] = a[i, p]
            own[pl.ds(k * EY + HY + PY, HY), :] = hi[pl.ds(k * HY, HY), :]
    got = []
    for c in range(2):

        def load(i, k, row):
            return own[pl.ds((PX * (i + 1) + 2 * c + k) * EY + row, R1, 2), :]

        got.append(coarser(load, R1, 1))
    for i in range(4):
        t = pack2(got[0][i], got[1][i])
        own[pl.ds(RAW + R1 * i, R1), :] = t
        sw[pl.ds(SRAW + R1 * i, R1), :] = t
    xs[pl.ds(SRAW, R1), :] = own[pl.ds(RAW + R1, R1), :]
    for i in range(5):
        here = pl.ds(i * EY, EY)
        xs[here, :] = plane(own, PX * i + 3 * par)
        sw[here, :] = plane(own, PX * i + 3 - 3 * par)
    clear_pads(x, EY)
    body = pl.ds(PAD, EY)
    kept = []
    for p in range(3):
        by = plane(own, PX * BY + p)
        _, inv, w = faces(
            plane(own, PX * ALPHA + p), plane(own, PX * BX + p), plane(own, PX * BX + p + 1), by,
            pltpu.roll(by, EY - 1, 0), plane(own, PX * BZ + p), 1, 1.0,
        )
        c0 = inv * plane(own, PX * B + p)
        x[p, body, :] = c0 * (1.0 / THETA)
        kept.append((w, c0))
    for up in range(2):
        second = 1 + up
        w, c0 = kept[second]
        here = x[second, body, :]
        z = c0 - here + w[0] * x[second - 1, body, :]
        if not up:
            z += w[1] * x[2, body, :]
        z += w[2] * x[second, pl.ds(PAD - 1, EY), :] + w[3] * x[second, pl.ds(PAD + 1, EY), :]
        z += w[4] * moved(here, 1) + w[5] * moved(here, -1)
        v[up, pl.ds(0, EY), :] = here
        v[up, pl.ds(EY, EY), :] = here + GAIN[1] * z + MOMENTUM[1] * here
        v[up, pl.ds(2 * EY, EY), :] = w[1] if up else plane(own, PX * BX + second)
    xs[pl.ds(5 * EY, 3 * EY), :] = v[par]
    sw[pl.ds(5 * EY, 3 * EY), :] = v[1 - par]


Q0 = 3


def fine_kernel(own, sw, xs, _, send, send1, send2, edge, pre, w, cc, sx, d, x, y, z, t, s, u):
    par = parity()
    sides2 = ((xs, par), (sw, 1 - par))
    for i in range(4):
        for p, ref, base in ((par, own, RAW), (1 - par, sw, SRAW)):
            v0, v1 = unpack2(ref[pl.ds(base + R1 * i, R1), :])
            s[i, 2 * p] = v0
            s[i, 2 * p + 1] = v1
    s[1, 4] = unpack2(xs[pl.ds(SRAW, R1), :])[0]
    for p in range(PX):
        sx[Q0 + p] = plane(own, PX * BX + p)
    for ref, above in sides2:
        sx[2 + 5 * above] = plane(ref, BX)
        sx[9 - above] = plane(ref, 7)
    clear_pads(x, EY)
    clear_pads(y, EY)
    chunk = 32

    def prepare(q, get):
        for r0 in range(0, EY, chunk):
            here = pl.ds(r0, chunk)

            def load(i):
                return lambda r, n: get(i, r, n)

            dd, inv, w6 = faces(
                load(ALPHA)(r0, chunk), sx[q, here, :], sx[q + 1, here, :], load(BY)(r0, chunk),
                next_rows(load(BY), r0, chunk, EY), load(BZ)(r0, chunk), 1, 1.0,
            )
            for a, f in enumerate(w6):
                w[a, q, here, :] = f
            c0 = inv * load(B)(r0, chunk)
            cc[q, here, :] = c0
            x[q, pl.ds(PAD + r0, chunk), :] = c0 * (1.0 / THETA)
            d[q, here, :] = dd

    for p in range(PX):
        prepare(Q0 + p, lambda i, r, n: plane(own, PX * i + p, r, n))
    body = pl.ds(PAD, EY)
    for ref, above in sides2:
        q = 2 + 5 * above
        prepare(q, lambda i, r, n: plane(ref, i, r, n))
        x[1 + 7 * above, body, :] = plane(ref, 5)
        missing = GAIN[1] * plane(ref, 7) * x[q, body, :]
        below = jnp.broadcast_to(above, missing.shape) == 0
        y[1 + 7 * above, body, :] = plane(ref, 6) + jnp.where(below, missing, 0.0)

    rows = (0, EY)
    sweep(x, None, cc, w, 2, 8, rows, 1, 1, into(y), chunk)
    sweep(y, x, cc, w, 2, 8, rows, 1, 2, into(z), chunk)
    got = []
    for c in range(2):
        for r0 in range(0, EY, chunk):
            v = 0.0
            for q in (Q0 + 2 * c, Q0 + 2 * c + 1):
                _, zz = defect(z, cc, w, q, r0, chunk, 1, q, 0, q, 0)
                v = v + d[q, pl.ds(r0, chunk), :] * zz
            t[c, pl.ds(r0, chunk), :] = v
        got.append(pair_lanes(t[c, pl.ds(0, R1, 2), :] + t[c, pl.ds(1, R1, 2), :], 1) * 0.125)
    mid = pl.ds(PAD + MID0, MID)
    rhs = pack2(got[0], got[1])
    for out in (send, send1):
        out[:R1] = rhs
        out[pl.ds(R1, 4 * R1), :] = own[pl.ds(RAW, 4 * R1), :]
    edge[...] = z[Q0 + 2 - par, mid, :]
    send[pl.ds(5 * R1, MID), :] = z[Q0 + 1 + par, mid, :]
    q = 3 * par
    u[:R1] = s[2, q]
    u[R1:] = jnp.zeros((PAD, PZ), F32)
    _, inv, _ = faces(s[0, q], s[1, q], s[1, q + 1], u[:R1], u[pl.ds(1, R1), :], s[3, q], 2, 0.25)
    x1 = inv * jnp.where(jnp.broadcast_to(par, rhs.shape) == 0, *unpack2(rhs)) * (1.0 / THETA)
    send2[:R1] = pack2(x1, s[1, q])
    for c in range(2):

        def load(i, k, row):
            return s[i, 2 * c + k, pl.ds(row, R2, 2), :]

        send2[pl.ds(R1 + R2 * c, R2), :] = pack4(coarser(load, R2, 2))
    for p in range(6):
        pre[p] = z[Q0 - 1 + p, mid, :]


C0 = 5
N1 = 14
M0 = 5
S_SHAPE = (4, N1, R1 + 2 * PAD, PZ)
O_EDGE = R1
O_ONE = O_EDGE + MID
O_BESIDE = O_ONE + R1
O_TWO = O_BESIDE + R1
O_RAW = O_TWO + 2 * R1
O_END = O_RAW + 8 * R1


def place_coefficients(s, i, e, v):
    v0, v1 = unpack2(v)
    s[i, 1 + 2 * e, pl.ds(PAD, R1), :] = v0
    s[i, 2 + 2 * e, pl.ds(PAD, R1), :] = v1


def middle_faces(s, w1, inv1, d1, q):
    for r0 in range(0, R1, 32):
        here, up, out = pl.ds(PAD + r0, 32), pl.ds(PAD + r0 + 1, 32), pl.ds(r0, 32)
        dd, inv, w6 = faces(
            s[0, q, here, :], s[1, q, here, :], s[1, q + 1, here, :], s[2, q, here, :], s[2, q, up, :],
            s[3, q, here, :], 2, 0.25,
        )
        for a, f in enumerate(w6):
            w1[a, q, out, :] = f
        inv1[q, out, :] = inv
        d1[q, out, :] = dd


def sides(par, k):
    lower, upper = 1 - k, 4 + k
    return jnp.where(par == 0, lower, upper), jnp.where(par == 0, upper, lower)


def level2_load(s, plane):
    def load(i, k, row):
        return s[i, 2 * plane + C0 + k, pl.ds(PAD + row, R2, 2), :]

    return load


def near_coefficients_kernel(own, other, one, beside, s, w1, inv1, d1):
    par = parity()
    for i in range(4):
        s[i, :, PAD + R1 :, :] = jnp.zeros((N1, PAD, PZ), F32)
        rows = pl.ds(R1 * i, R1)
        sent = pl.ds(R1 * (1 + i), R1)
        place_coefficients(s, i, 2 + par, own[rows, :])
        place_coefficients(s, i, 3 - par, other[rows, :])
        place_coefficients(s, i, sides(par, 0)[0], one[sent, :])
        place_coefficients(s, i, sides(par, 1)[0], beside[sent, :])
    for k in range(7):
        middle_faces(s, w1, inv1, d1, 1 + 4 * par + k)


def join_kernel(own, edge, one, beside, two, out):
    out[:R1] = own[:R1]
    out[pl.ds(O_EDGE, MID), :] = edge[...]
    out[pl.ds(O_ONE, R1), :] = one[:R1]
    out[pl.ds(O_BESIDE, R1), :] = beside[:R1]
    out[pl.ds(O_TWO, 2 * R1), :] = two[...]
    out[pl.ds(O_RAW, 4 * R1), :] = one[pl.ds(R1, 4 * R1), :]
    out[pl.ds(O_RAW + 4 * R1, 4 * R1), :] = beside[pl.ds(R1, 4 * R1), :]


def tick_kernel(_, out):
    out[...] = jnp.zeros(out.shape, F32)


def first_to_arrive(v):
    return call(tick_kernel, "tick", shape(PAD, PZ), VMEM, [ANY], [], LARGE)(v)


def both_sides(par, mine, its):
    upper = jnp.broadcast_to(par, mine.shape) == 1
    return jnp.where(upper, its, mine), jnp.where(upper, mine, its)


def middle_kernel(own, one, beside, two, its, s_in, w_in, inv_in, d_in, edge, cc, pre, rhs, s, w, inv, d,
                  x, y, z, t, u):
    par = parity()
    clear_pads(x, R1)
    clear_pads(y, R1)
    body = pl.ds(PAD, R1)
    lower, upper = both_sides(par, two[:R1], its[pl.ds(O_TWO, R1), :])
    x[0, body, :] = unpack2(lower)[0]
    x1, bx = unpack2(upper)
    x[N1 - 1, body, :] = x1
    s[1, N1 - 1, body, :] = bx
    for k in range(2):
        e = sides(par, k)[1]
        for i in range(4):
            place_coefficients(s, i, e, its[pl.ds(O_RAW + (4 * k + i) * R1, R1), :])
    for k in range(5):
        middle_faces(s, w, inv, d, jnp.where(par == 0, 8 + k, 1 + k if k < 4 else 12))

    def place(e, v):
        for k, b in enumerate(unpack2(v)):
            q = 1 + 2 * e + k
            c0 = inv[q] * b
            cc[q] = c0
            x[q, body, :] = c0 * (1.0 / THETA)

    place(2 + par, own[:R1])
    place(3 - par, its[:R1])
    for k, ref, row in ((0, one, O_ONE), (1, beside, O_BESIDE)):
        e, f = sides(par, k)
        place(e, ref[:R1])
        place(f, its[pl.ds(row, R1), :])

    rows = (0, R1)
    sweep(x, None, cc, w, 1, 13, rows, 2, 1, into(y), 32, unroll=12)
    sweep(y, x, cc, w, 2, 12, rows, 2, 2, into(z), 32, unroll=10)

    for c in range(4):
        for r0 in range(0, R1, 32):
            v = 0.0
            for k in range(2):
                q = C0 - 2 + 2 * c + k
                _, zz = defect(z, cc, w, q, r0, 32, 2, q, 0, q, 0)
                v = v + d[q, pl.ds(r0, 32), :] * zz
            t[c, pl.ds(r0, 32), :] = v
        rhs[c] = pair_lanes(t[c, pl.ds(0, R2, 2), :] + t[c, pl.ds(1, R2, 2), :], 2) * 0.125

    def first(k, plane):
        al, bx, by, bz = coarser(level2_load(s, plane), R2, 2)
        after = level2_load(s, plane + 1)
        bx1 = pair_lanes(after(1, 0, 0) + after(1, 0, 1), 2) * 0.25
        u[k, pl.ds(0, R2), :] = by
        u[k, pl.ds(R2, PAD), :] = jnp.zeros((PAD, PZ), F32)
        _, inv2, _ = faces(al, bx, bx1, by, u[k, pl.ds(1, R2), :], bz, 4, 0.0625)
        return inv2 * rhs[plane + 1] * (1.0 / THETA), bx

    below, above = first(0, -1), first(1, 2)
    up = pack4([rhs[3], rhs[2], rhs[1], below[0]])
    down = pack4([rhs[0], rhs[1], rhs[2], above[0]])
    wide = jnp.broadcast_to(lax.axis_index("wide"), up.shape)
    ends = (lanes(R2) & 3) == 0
    down = jnp.where(wide == 0, jnp.where(ends, rhs[1], 0.0), down)
    up = jnp.where(wide == lax.axis_size("wide") - 1, jnp.where(ends, rhs[2], 0.0), up)
    edge[:R2] = jnp.where(jnp.broadcast_to(par, up.shape) == 0, down, up)
    edge[R2:] = above[1]
    for p in range(10):
        pre[p] = z[C0 - 3 + p, body, :]


def coarse_coefficients_kernel(s, two, its, w2, inv2, last, s2):
    par = parity()
    for c in range(2, 8):
        for i, v in enumerate(coarser(level2_load(s, c - 4), R2, 2)):
            s2[i, c, pl.ds(0, R2), :] = v
    for k in range(2):
        rows = pl.ds(R1 + R2 * k, R2)
        lower, upper = both_sides(par, two[rows, :], its[pl.ds(O_TWO + R1 + R2 * k, R2), :])
        for i in range(4):
            s2[i, k, pl.ds(0, R2), :] = unpack4(lower, i)
            s2[i, 8 + k, pl.ds(0, R2), :] = unpack4(upper, i)
    s2[2, :, R2:, :] = jnp.zeros((10, PAD, PZ), F32)
    body = pl.ds(0, R2)
    for c in range(9):
        _, inv, w6 = faces(
            s2[0, c, body, :], s2[1, c, body, :], s2[1, c + 1, body, :], s2[2, c, body, :], s2[2, c, pl.ds(1, R2), :],
            s2[3, c, body, :], 4, 0.0625,
        )
        for a, f in enumerate(w6):
            w2[a, c + 1] = f
        inv2[c + 1] = inv
    for i in range(4):
        last[i] = s2[i, 9]


def last_kernel(two2, its2, rhs, w2, inv2, last, pre1, w1, c1, pre0, sw, xs, w0, c0, out,
                wx, c2, x2, y2, z2, x1, y1, z1, x0, y0):
    par = parity()
    body = pl.ds(PAD, R2)
    lo, hi = both_sides(par, two2[:R2], its2[:R2])
    _, beyond = both_sides(par, two2[R2:], its2[R2:])
    clear_pads(x2, R2)
    clear_pads(y2, R2)
    clear_pads(z2, R2)
    _, inv, w6 = faces(
        last[0, :R2], last[1, :R2], beyond, last[2, :R2], last[2, pl.ds(1, R2), :], last[3, :R2], 4, 0.0625
    )
    for a, f in enumerate(w6):
        wx[a, 0] = f

    def start(j, b, dinv):
        v = dinv * b
        c2[j] = v
        x2[j, body, :] = v * (1.0 / THETA)

    for k in range(3):
        start(3 - k, unpack4(lo, k), inv2[3 - k])
        start(8 + k, unpack4(hi, k), inv2[8 + k] if k < 2 else inv)
    for c in range(4):
        start(c + 4, rhs[c], inv2[c + 4])
    x2[0, body, :] = unpack4(lo, 3)
    x2[11, body, :] = unpack4(hi, 3)
    rows = (0, R2)
    sweep(x2, None, c2, w2, 1, 10, rows, 4, 1, into(y2), R2, unroll=9)
    sweep(x2, None, c2, wx, 10, 11, rows, 4, 1, into(y2), R2, woff=-10)
    sweep(y2, x2, c2, w2, 2, 10, rows, 4, 2, into(z2), R2, unroll=8)
    sweep(z2, y2, c2, w2, 3, 9, rows, 4, 3, into(x2), R2, unroll=6)

    clear_pads(x1, R1)
    clear_pads(y1, R1)
    for q in range(10):
        v = x2[(q - 3) // 2 + M0, body, :]
        z1[q, pl.ds(PAD, R2, 2), :] = v
        z1[q, pl.ds(PAD + 1, R2, 2), :] = v
        x1[q, pl.ds(PAD, R1), :] = pre1[q] + z1[q, pl.ds(PAD, R1), :]
    rows = (0, R1)
    off = C0 - 3
    sweep(x1, None, c1, w1, 1, 9, rows, 2, 0, into(y1), 32, woff=off, coff=off)
    sweep(y1, x1, c1, w1, 2, 8, rows, 2, 1, into(z1), 32, woff=off, coff=off, unroll=6)

    clear_pads(x0, MID)
    clear_pads(y0, MID)
    near, far = 7 - 7 * par, 7 * par
    body = pl.ds(PAD, MID)
    for q in range(8):
        v = z1[(q - 2) // 2 + 3 + 2 * par, pl.ds(PAD + 12, MID // 2), :]
        x0[q, pl.ds(PAD, MID // 2, 2), :] = v
        x0[q, pl.ds(PAD + 1, MID // 2, 2), :] = v
        if 0 < q < 7:
            x0[q, body, :] += pre0[q - 1]
    x0[near, body, :] += sw[pl.ds(O_EDGE, MID), :]
    x0[far, body, :] += xs[pl.ds(5 * R1, MID), :]
    off = Q0 - 2
    sweep(x0, None, c0, w0, 1, 7, (0, MID), 1, 0, into(y0), 40, woff=off, coff=off, wr=MID0, cr=MID0, unroll=6)

    def finish(q, r0, n, v):
        out[q - 2, pl.ds(r0 - 8, n), :] = v

    sweep(y0, x0, c0, w0, 2, 6, (8, 8 + PY), 1, 1, finish, 32, woff=off, coff=off, wr=MID0, cr=MID0, unroll=4)


def swap(v):
    return lax.ppermute(v, "wide", [(i, i ^ 1) for i in range(lax.axis_size("wide"))])


def across(v, chips, ends=()):
    count = lax.axis_size("wide")
    step = 2 * chips - 1
    pairs = [(i, i + step) for i in range(1, count, 2) if i + step < count]
    pairs += [(i, i - step) for i in range(0, count, 2) if i - step >= 0]
    return lax.ppermute(v, "wide", pairs + list(ends))


def from_beside(v):
    count = lax.axis_size("wide")
    pairs = [(i, i + 2) for i in range(0, count - 2, 2)] + [(i, i - 2) for i in range(3, count, 2)]
    return lax.ppermute(v, "wide", pairs)


def shifted(v, axis, step):
    count = lax.axis_size(axis)
    return lax.ppermute(v, axis, [(i, i + step) for i in range(count) if 0 <= i + step < count])


def shards(right_side, alpha_coef, beta_x, beta_y, beta_z):
    a, ylo, yhi = call(
        pack_kernel, "pack", (shape(5, PX, PY, PZ), shape(5 * PX * HY, PZ), shape(5 * PX * HY, PZ)),
        (VMEM,) * 3, [ANY] * 5, [pltpu.SemaphoreType.DMA((5,))], SMALL,
    )(*[pltpu.with_memory_space_constraint(v, pltpu.HBM) for v in (right_side, alpha_coef, beta_x, beta_y, beta_z)])
    lo = shifted(yhi, "narrow", 1)
    hi = shifted(ylo, "narrow", -1)
    own, sw, xs = call(
        corner_kernel, "corners", (shape(RAW + 4 * R1, PZ), shape(SRAW + 4 * R1, PZ), shape(SRAW + R1, PZ)),
        (VMEM,) * 3, [VMEM] * 3, [scratch(3, EY + 2 * PAD, PZ), scratch(2, 3 * EY, PZ)], SMALL,
    )(a, lo, hi)
    xs = across(xs, 1)
    sw = swap(sw)

    send, send1, send2, edge0, pre0, w0, c0 = call(
        fine_kernel, "level0_pre",
        (shape(5 * R1 + MID, PZ), shape(5 * R1, PZ), shape(2 * R1, PZ), shape(MID, PZ), shape(6, MID, PZ),
         shape(6, 10, EY, PZ), shape(10, EY, PZ)),
        (VMEM,) * 7, [VMEM] * 3 + [ANY],
        [scratch(10, EY, PZ), scratch(10, EY, PZ)] + [scratch(10, EY + 2 * PAD, PZ)] * 3
        + [scratch(2, EY, PZ), scratch(4, 5, R1, PZ), scratch(R1 + PAD, PZ)],
        LARGE,
    )(own, sw, xs, first_to_arrive(xs))

    one = across(send, 1)
    beside = from_beside(send1)
    two = across(send2, 2)
    mine = call(join_kernel, "join", shape(O_END, PZ), VMEM, [VMEM] * 5, [], SMALL)(send, edge0, one, beside, two)
    its = swap(mine)
    w1_shapes = (shape(*S_SHAPE), shape(6, N1, R1, PZ), shape(N1, R1, PZ), shape(N1, R1, PZ))
    s1, w1, inv1, d1 = call(
        near_coefficients_kernel, "near_coefficients", w1_shapes, (VMEM,) * 4, [VMEM] * 4, [], LARGE,
    )(own[RAW:], sw[SRAW:], one, beside)

    edge, c1, pre1, rhs2, s1, w1, _, _ = call(
        middle_kernel, "level1_pre",
        (shape(2 * R2, PZ), shape(N1, R1, PZ), shape(10, R1, PZ), shape(4, R2, PZ)) + w1_shapes,
        (VMEM,) * 8, [VMEM] * 9,
        [scratch(N1, R1 + 2 * PAD, PZ)] * 3 + [scratch(4, R1, PZ), scratch(2, R2 + PAD, PZ)],
        LARGE, aliases={5: 4, 6: 5, 7: 6, 8: 7},
    )(send, one, beside, two, its, s1, w1, inv1, d1)

    w2, inv2, last2 = call(
        coarse_coefficients_kernel, "level2_coefficients",
        (shape(6, 12, R2, PZ), shape(12, R2, PZ), shape(4, R2 + PAD, PZ)),
        (VMEM,) * 3, [VMEM] * 3, [scratch(4, 10, R2 + PAD, PZ)], LARGE,
    )(s1, two, its)
    count = lax.axis_size("wide")
    two2 = across(edge, 2, ((0, 2), (count - 1, count - 3)))
    its2 = swap(two2)
    return call(
        last_kernel, "coarse_and_post", shape(PX, PY, PZ), VMEM, [VMEM] * 14,
        [scratch(6, 1, R2, PZ), scratch(12, R2, PZ)] + [scratch(12, R2 + 2 * PAD, PZ)] * 3
        + [scratch(10, R1 + 2 * PAD, PZ)] * 3 + [scratch(8, MID + 2 * PAD, PZ)] * 2,
        LARGE,
    )(two2, its2, rhs2, w2, inv2, last2, pre1, w1, c1, pre0, its, one, w0, c0)


def solution(mesh):
    spec = P("wide", "narrow", None)
    return jax.shard_map(shards, mesh=mesh, in_specs=(spec,) * 5, out_specs=spec, check_vma=False)
```

```python
import jax
import jax.numpy as jnp
from jax import lax
from jax.experimental import pallas as pl
from jax.experimental.pallas import tpu as pltpu
from jax.sharding import PartitionSpec as P

F32 = jnp.float32
THETA = (2.0 + 0.25) / 2.0
DELTA = (2.0 - 0.25) / 2.0
SIGMA = THETA / DELTA
RHO = [1.0 / SIGMA]
for _step in range(3):
    RHO.append(1.0 / (2.0 * SIGMA - RHO[-1]))
MOMENTUM = [0.0] + [RHO[k] * RHO[k - 1] for k in range(1, 4)]
GAIN = [1.0 / THETA] + [2.0 * RHO[k] / DELTA for k in range(1, 4)]

PX, PY, PZ = 4, 64, 128
HY = 32
EY = PY + 2 * HY
MID = PY + 16
MID0 = HY - 8
R1 = EY // 2
R2 = R1 // 2
RAW = 5 * PX * EY
SRAW = 8 * EY
XP = 5 * 2 * HY
XB = XP + 3 * EY
PAD = 8
SMALL, LARGE = 1000, 2 * 10**10
B, ALPHA, BX, BY, BZ = range(5)
ANY = pl.BlockSpec(memory_space=pl.ANY)
VMEM = pl.BlockSpec(memory_space=pltpu.VMEM)
HBM = pl.BlockSpec(memory_space=pltpu.HBM)


def shape(*dims):
    return jax.ShapeDtypeStruct(dims, F32)


def scratch(*dims):
    return pltpu.VMEM(dims, F32)


def call(kernel, name, out_shape, out_specs, in_specs, scratch_shapes, flops, mib=24, aliases=None):
    return pl.pallas_call(
        kernel,
        out_shape=out_shape,
        in_specs=in_specs,
        out_specs=out_specs,
        scratch_shapes=scratch_shapes,
        compiler_params=pltpu.CompilerParams(vmem_limit_bytes=mib * 1024 * 1024),
        cost_estimate=pl.CostEstimate(flops=flops, bytes_accessed=0, transcendentals=0),
        input_output_aliases=aliases or {},
        name=name,
    )


def parity():
    return lax.rem(lax.axis_index("wide"), 2)


def lanes(rows):
    return lax.broadcasted_iota(jnp.int32, (rows, PZ), 1)


def moved(v, shift):
    return pltpu.roll(v, shift % PZ, 1)


def planes(lo, hi, each, unroll):
    if not unroll:
        each(lo)
        return
    steps = (hi - lo) // unroll

    def body(i, carry):
        for k in range(unroll):
            each(lo + i * unroll + k)
        return carry

    if steps > 1:
        lax.fori_loop(0, steps, body, 0)
    else:
        steps = 0
    for q in range(lo + steps * unroll, hi):
        each(q)


def defect(x_ref, c_ref, w_ref, q, r0, n, reach, cq, cr, wq, wr):
    rows = pl.ds(PAD + r0, n)
    here = pl.ds(wr + r0, n)
    x = x_ref[q, rows, :]
    total = c_ref[cq, pl.ds(cr + r0, n), :] - x
    total += w_ref[0, wq, here, :] * x_ref[q - 1, rows, :]
    total += w_ref[1, wq, here, :] * x_ref[q + 1, rows, :]
    total += w_ref[2, wq, here, :] * x_ref[q, pl.ds(PAD + r0 - 1, n), :]
    total += w_ref[3, wq, here, :] * x_ref[q, pl.ds(PAD + r0 + 1, n), :]
    total += w_ref[4, wq, here, :] * moved(x, reach)
    total += w_ref[5, wq, here, :] * moved(x, -reach)
    return x, total


def sweep(x_ref, prev_ref, c_ref, w_ref, lo, hi, rows, reach, k, store, chunk, woff=0, coff=0, wr=0, cr=0, unroll=8):
    def each(q):
        for r0 in range(rows[0], rows[1], chunk):
            n = min(chunk, rows[1] - r0)
            x, z = defect(x_ref, c_ref, w_ref, q, r0, n, reach, q + coff, cr, q + woff, wr)
            new = x + GAIN[k] * z
            if k > 0:
                gap = x if prev_ref is None else x - prev_ref[q, pl.ds(PAD + r0, n), :]
                new += MOMENTUM[k] * gap
            store(q, r0, n, new)

    planes(lo, hi, each, unroll)


def into(ref):
    def store(q, r0, n, v):
        ref[q, pl.ds(PAD + r0, n), :] = v

    return store


def inverse(d):
    inside = d > 0.0
    return jnp.where(inside, 1.0 / jnp.where(inside, d, 1.0), 0.0)


def faces(alpha, x0, x1, y0, y1, z0, reach, scale):
    z1 = moved(z0, -reach)
    d = alpha + scale * (x0 + x1 + y0 + y1 + z0 + z1)
    inv = inverse(d)
    si = scale * inv
    return d, inv, [si * f for f in (x0, x1, y0, y1, z0, z1)]


def next_rows(load, r0, n, rows):
    if r0 + n < rows:
        return load(r0 + 1, n)
    return pltpu.roll(load(r0, n), n - 1, 0)


def clear_pads(ref, rows):
    ref[:, :PAD, :] = jnp.zeros((ref.shape[0], PAD, PZ), F32)
    ref[:, PAD + rows :, :] = jnp.zeros((ref.shape[0], PAD, PZ), F32)


def pair_lanes(v, reach):
    low = (lanes(v.shape[0]) & reach) == 0
    return v + jnp.where(low, moved(v, -reach), moved(v, reach))


def low_lanes(v, reach):
    low = (lanes(v.shape[0]) & reach) == 0
    return jnp.where(low, v, moved(v, reach))


def pack2(v0, v1):
    return jnp.where((lanes(v0.shape[0]) & 1) == 0, v0, v1)


def unpack2(v):
    even = (lanes(v.shape[0]) & 1) == 0
    return jnp.where(even, v, moved(v, 1)), jnp.where(even, moved(v, -1), v)


def pack4(items):
    place = lanes(items[0].shape[0]) & 3
    out = items[0]
    for i, item in enumerate(items[1:], 1):
        out = jnp.where(place == i, item, out)
    return out


def unpack4(v, i):
    place = lanes(v.shape[0]) & 3
    out = v
    for m in range(4):
        if m != i:
            out = jnp.where(place == m, moved(v, m - i), out)
    return out


def coarser(load, rows, reach):
    def cell(i):
        return load(i, 0, 0) + load(i, 0, 1) + load(i, 1, 0) + load(i, 1, 1)

    al = pair_lanes(cell(0), reach) * 0.125
    bx = pair_lanes(load(1, 0, 0) + load(1, 0, 1), reach) * 0.25
    by = pair_lanes(load(2, 0, 0) + load(2, 1, 0), reach) * 0.25
    bz = low_lanes(cell(3), reach) * 0.25
    return al, bx, by, bz


def pack_kernel(b, al, bx, by, bz, a, lo_out, hi_out, xs_out, sems):
    wide, narrow = lax.axis_index("wide"), lax.axis_index("narrow")
    par = lax.rem(wide, 2)
    copies = [pltpu.make_async_copy(ref, a.at[i], sems.at[i]) for i, ref in enumerate((b, al, bx, by, bz))]
    for c in copies:
        c.start()
    for c in copies:
        c.wait()
    row = lax.broadcasted_iota(jnp.int32, (PAD, PZ), 0)
    first_row = jnp.logical_and(row == 0, jnp.broadcast_to(narrow, (PAD, PZ)) == 0)
    a[BX, 0] = jnp.where(jnp.broadcast_to(wide, (PY, PZ)) == 0, 0.0, a[BX, 0])
    first_z = lanes(PY) == 0
    for p in range(PX):
        a[BY, p, :PAD] = jnp.where(first_row, 0.0, a[BY, p, :PAD])
        a[BZ, p] = jnp.where(first_z, 0.0, a[BZ, p])
    for i in range(5):
        for p in range(PX):
            here = pl.ds((PX * i + p) * HY, HY)
            lo_out[here, :] = a[i, p, :HY]
            hi_out[here, :] = a[i, p, PY - HY :]
        xs_out[pl.ds(i * PY, PY), :] = a[i, 3 * par]


def plane(ref, k, r0=0, n=EY):
    start = k * EY + r0
    return ref[pl.ds(pl.multiple_of(start, 8) if r0 % 8 == 0 else start, n), :]


def corner_kernel(a, lo, hi, _, __, own, sw, xs, x, v):
    par = parity()
    for i in range(5):
        for p in range(PX):
            k = PX * i + p
            own[pl.ds(k * EY, HY), :] = lo[pl.ds(k * HY, HY), :]
            own[pl.ds(k * EY + HY, PY), :] = a[i, p]
            own[pl.ds(k * EY + HY + PY, HY), :] = hi[pl.ds(k * HY, HY), :]
    got = []
    for c in range(2):

        def load(i, k, row):
            return own[pl.ds((PX * (i + 1) + 2 * c + k) * EY + row, R1, 2), :]

        got.append(coarser(load, R1, 1))
    for i in range(4):
        t = pack2(got[0][i], got[1][i])
        own[pl.ds(RAW + R1 * i, R1), :] = t
        sw[pl.ds(SRAW + R1 * i, R1), :] = t
    xs[pl.ds(XB, R1), :] = own[pl.ds(RAW + R1, R1), :]
    for i in range(5):
        xs[pl.ds(2 * HY * i, HY), :] = plane(own, PX * i + 3 * par, 0, HY)
        xs[pl.ds(2 * HY * i + HY, HY), :] = plane(own, PX * i + 3 * par, HY + PY, HY)
        sw[pl.ds(i * EY, EY), :] = plane(own, PX * i + 3 - 3 * par)
    clear_pads(x, EY)
    body = pl.ds(PAD, EY)
    kept = []
    for p in range(3):
        by = plane(own, PX * BY + p)
        _, inv, w = faces(
            plane(own, PX * ALPHA + p), plane(own, PX * BX + p), plane(own, PX * BX + p + 1), by,
            pltpu.roll(by, EY - 1, 0), plane(own, PX * BZ + p), 1, 1.0,
        )
        c0 = inv * plane(own, PX * B + p)
        x[p, body, :] = c0 * (1.0 / THETA)
        kept.append((w, c0))
    for up in range(2):
        second = 1 + up
        w, c0 = kept[second]
        here = x[second, body, :]
        z = c0 - here + w[0] * x[second - 1, body, :]
        if not up:
            z += w[1] * x[2, body, :]
        z += w[2] * x[second, pl.ds(PAD - 1, EY), :] + w[3] * x[second, pl.ds(PAD + 1, EY), :]
        z += w[4] * moved(here, 1) + w[5] * moved(here, -1)
        v[up, pl.ds(0, EY), :] = here
        v[up, pl.ds(EY, EY), :] = here + GAIN[1] * z + MOMENTUM[1] * here
        v[up, pl.ds(2 * EY, EY), :] = w[1] if up else plane(own, PX * BX + second)
    xs[pl.ds(XP, 3 * EY), :] = v[par]
    sw[pl.ds(5 * EY, 3 * EY), :] = v[1 - par]


Q0 = 3


def fine_kernel(own, sw, xs, ex, _, send, send1, send2, edge, pre, w, cc, sx, d, x, y, z, t, s, u, sf):
    par = parity()
    for i in range(5):
        sf[i, :HY] = xs[pl.ds(2 * HY * i, HY), :]
        sf[i, HY : HY + PY] = ex[pl.ds(PY * i, PY), :]
        sf[i, HY + PY :] = xs[pl.ds(2 * HY * i + HY, HY), :]

    def far(i, r, n):
        return sf[i, pl.ds(r, n), :] if i < 5 else xs[pl.ds(XP + (i - 5) * EY + r, n), :]

    def near(i, r, n):
        return plane(sw, i, r, n)

    sides2 = ((far, par), (near, 1 - par))
    for i in range(4):
        for p, ref, base in ((par, own, RAW), (1 - par, sw, SRAW)):
            v0, v1 = unpack2(ref[pl.ds(base + R1 * i, R1), :])
            s[i, 2 * p] = v0
            s[i, 2 * p + 1] = v1
    s[1, 4] = unpack2(xs[pl.ds(XB, R1), :])[0]
    for p in range(PX):
        sx[Q0 + p] = plane(own, PX * BX + p)
    for get, above in sides2:
        sx[2 + 5 * above] = get(BX, 0, EY)
        sx[9 - above] = get(7, 0, EY)
    clear_pads(x, EY)
    clear_pads(y, EY)
    chunk = 32

    def prepare(q, get):
        for r0 in range(0, EY, chunk):
            here = pl.ds(r0, chunk)

            def load(i):
                return lambda r, n: get(i, r, n)

            dd, inv, w6 = faces(
                load(ALPHA)(r0, chunk), sx[q, here, :], sx[q + 1, here, :], load(BY)(r0, chunk),
                next_rows(load(BY), r0, chunk, EY), load(BZ)(r0, chunk), 1, 1.0,
            )
            for a, f in enumerate(w6):
                w[a, q, here, :] = f
            c0 = inv * load(B)(r0, chunk)
            cc[q, here, :] = c0
            x[q, pl.ds(PAD + r0, chunk), :] = c0 * (1.0 / THETA)
            d[q, here, :] = dd

    for p in range(PX):
        prepare(Q0 + p, lambda i, r, n: plane(own, PX * i + p, r, n))
    body = pl.ds(PAD, EY)
    for get, above in sides2:
        q = 2 + 5 * above
        prepare(q, get)
        x[1 + 7 * above, body, :] = get(5, 0, EY)
        missing = GAIN[1] * get(7, 0, EY) * x[q, body, :]
        below = jnp.broadcast_to(above, missing.shape) == 0
        y[1 + 7 * above, body, :] = get(6, 0, EY) + jnp.where(below, missing, 0.0)

    rows = (0, EY)
    sweep(x, None, cc, w, 2, 8, rows, 1, 1, into(y), chunk)
    sweep(y, x, cc, w, 2, 8, rows, 1, 2, into(z), chunk)
    got = []
    for c in range(2):
        for r0 in range(0, EY, chunk):
            v = 0.0
            for q in (Q0 + 2 * c, Q0 + 2 * c + 1):
                _, zz = defect(z, cc, w, q, r0, chunk, 1, q, 0, q, 0)
                v = v + d[q, pl.ds(r0, chunk), :] * zz
            t[c, pl.ds(r0, chunk), :] = v
        got.append(pair_lanes(t[c, pl.ds(0, R1, 2), :] + t[c, pl.ds(1, R1, 2), :], 1) * 0.125)
    mid = pl.ds(PAD + MID0, MID)
    rhs = pack2(got[0], got[1])
    for out in (send, send1):
        out[:R1] = rhs
        out[pl.ds(R1, 4 * R1), :] = own[pl.ds(RAW, 4 * R1), :]
    edge[...] = z[Q0 + 2 - par, mid, :]
    send[pl.ds(5 * R1, MID), :] = z[Q0 + 1 + par, mid, :]
    q = 3 * par
    u[:R1] = s[2, q]
    u[R1:] = jnp.zeros((PAD, PZ), F32)
    _, inv, _ = faces(s[0, q], s[1, q], s[1, q + 1], u[:R1], u[pl.ds(1, R1), :], s[3, q], 2, 0.25)
    x1 = inv * jnp.where(jnp.broadcast_to(par, rhs.shape) == 0, *unpack2(rhs)) * (1.0 / THETA)
    send2[:R1] = pack2(x1, s[1, q])
    for c in range(2):

        def load(i, k, row):
            return s[i, 2 * c + k, pl.ds(row, R2, 2), :]

        send2[pl.ds(R1 + R2 * c, R2), :] = pack4(coarser(load, R2, 2))
    for p in range(6):
        pre[p] = z[Q0 - 1 + p, mid, :]


C0 = 5
N1 = 14
M0 = 5
S_SHAPE = (4, N1, R1 + 2 * PAD, PZ)
O_EDGE = R1
O_ONE = O_EDGE + MID
O_BESIDE = O_ONE + R1
O_TWO = O_BESIDE + R1
O_RAW = O_TWO + 2 * R1
O_END = O_RAW + 8 * R1


def place_coefficients(s, i, e, v):
    v0, v1 = unpack2(v)
    s[i, 1 + 2 * e, pl.ds(PAD, R1), :] = v0
    s[i, 2 + 2 * e, pl.ds(PAD, R1), :] = v1


def middle_faces(s, w1, inv1, d1, q):
    for r0 in range(0, R1, 32):
        here, up, out = pl.ds(PAD + r0, 32), pl.ds(PAD + r0 + 1, 32), pl.ds(r0, 32)
        dd, inv, w6 = faces(
            s[0, q, here, :], s[1, q, here, :], s[1, q + 1, here, :], s[2, q, here, :], s[2, q, up, :],
            s[3, q, here, :], 2, 0.25,
        )
        for a, f in enumerate(w6):
            w1[a, q, out, :] = f
        inv1[q, out, :] = inv
        d1[q, out, :] = dd


def sides(par, k):
    lower, upper = 1 - k, 4 + k
    return jnp.where(par == 0, lower, upper), jnp.where(par == 0, upper, lower)


def level2_load(s, plane):
    def load(i, k, row):
        return s[i, 2 * plane + C0 + k, pl.ds(PAD + row, R2, 2), :]

    return load


def near_coefficients_kernel(own, other, one, beside, s, w1, inv1, d1):
    par = parity()
    for i in range(4):
        s[i, :, PAD + R1 :, :] = jnp.zeros((N1, PAD, PZ), F32)
        rows = pl.ds(R1 * i, R1)
        sent = pl.ds(R1 * (1 + i), R1)
        place_coefficients(s, i, 2 + par, own[rows, :])
        place_coefficients(s, i, 3 - par, other[rows, :])
        place_coefficients(s, i, sides(par, 0)[0], one[sent, :])
        place_coefficients(s, i, sides(par, 1)[0], beside[sent, :])
    for k in range(7):
        middle_faces(s, w1, inv1, d1, 1 + 4 * par + k)


def join_kernel(own, edge, one, beside, two, out):
    out[:R1] = own[:R1]
    out[pl.ds(O_EDGE, MID), :] = edge[...]
    out[pl.ds(O_ONE, R1), :] = one[:R1]
    out[pl.ds(O_BESIDE, R1), :] = beside[:R1]
    out[pl.ds(O_TWO, 2 * R1), :] = two[...]
    out[pl.ds(O_RAW, 4 * R1), :] = one[pl.ds(R1, 4 * R1), :]
    out[pl.ds(O_RAW + 4 * R1, 4 * R1), :] = beside[pl.ds(R1, 4 * R1), :]


def tick_kernel(*refs):
    refs[-1][...] = jnp.zeros(refs[-1].shape, F32)


def first_to_arrive(*values):
    return call(tick_kernel, "tick", shape(PAD, PZ), VMEM, [ANY] * len(values), [], LARGE)(*values)


def both_sides(par, mine, its):
    upper = jnp.broadcast_to(par, mine.shape) == 1
    return jnp.where(upper, its, mine), jnp.where(upper, mine, its)


def middle_kernel(own, one, beside, two, its, s_in, w_in, inv_in, d_in, edge, cc, pre, rhs, s, w, inv, d,
                  x, y, z, t, u):
    par = parity()
    clear_pads(x, R1)
    clear_pads(y, R1)
    body = pl.ds(PAD, R1)
    lower, upper = both_sides(par, two[:R1], its[pl.ds(O_TWO, R1), :])
    x[0, body, :] = unpack2(lower)[0]
    x1, bx = unpack2(upper)
    x[N1 - 1, body, :] = x1
    s[1, N1 - 1, body, :] = bx
    for k in range(2):
        e = sides(par, k)[1]
        for i in range(4):
            place_coefficients(s, i, e, its[pl.ds(O_RAW + (4 * k + i) * R1, R1), :])
    for k in range(5):
        middle_faces(s, w, inv, d, jnp.where(par == 0, 8 + k, 1 + k if k < 4 else 12))

    def place(e, v):
        for k, b in enumerate(unpack2(v)):
            q = 1 + 2 * e + k
            c0 = inv[q] * b
            cc[q] = c0
            x[q, body, :] = c0 * (1.0 / THETA)

    place(2 + par, own[:R1])
    place(3 - par, its[:R1])
    for k, ref, row in ((0, one, O_ONE), (1, beside, O_BESIDE)):
        e, f = sides(par, k)
        place(e, ref[:R1])
        place(f, its[pl.ds(row, R1), :])

    rows = (0, R1)
    sweep(x, None, cc, w, 1, 13, rows, 2, 1, into(y), 32, unroll=12)
    sweep(y, x, cc, w, 2, 12, rows, 2, 2, into(z), 32, unroll=10)

    for c in range(4):
        for r0 in range(0, R1, 32):
            v = 0.0
            for k in range(2):
                q = C0 - 2 + 2 * c + k
                _, zz = defect(z, cc, w, q, r0, 32, 2, q, 0, q, 0)
                v = v + d[q, pl.ds(r0, 32), :] * zz
            t[c, pl.ds(r0, 32), :] = v
        rhs[c] = pair_lanes(t[c, pl.ds(0, R2, 2), :] + t[c, pl.ds(1, R2, 2), :], 2) * 0.125

    def first(k, plane):
        al, bx, by, bz = coarser(level2_load(s, plane), R2, 2)
        after = level2_load(s, plane + 1)
        bx1 = pair_lanes(after(1, 0, 0) + after(1, 0, 1), 2) * 0.25
        u[k, pl.ds(0, R2), :] = by
        u[k, pl.ds(R2, PAD), :] = jnp.zeros((PAD, PZ), F32)
        _, inv2, _ = faces(al, bx, bx1, by, u[k, pl.ds(1, R2), :], bz, 4, 0.0625)
        return inv2 * rhs[plane + 1] * (1.0 / THETA), bx

    below, above = first(0, -1), first(1, 2)
    up = pack4([rhs[3], rhs[2], rhs[1], below[0]])
    down = pack4([rhs[0], rhs[1], rhs[2], above[0]])
    wide = jnp.broadcast_to(lax.axis_index("wide"), up.shape)
    ends = (lanes(R2) & 3) == 0
    down = jnp.where(wide == 0, jnp.where(ends, rhs[1], 0.0), down)
    up = jnp.where(wide == lax.axis_size("wide") - 1, jnp.where(ends, rhs[2], 0.0), up)
    edge[:R2] = jnp.where(jnp.broadcast_to(par, up.shape) == 0, down, up)
    edge[R2:] = above[1]
    for p in range(10):
        pre[p] = z[C0 - 3 + p, body, :]


def coarse_coefficients_kernel(s, two, its, w2, inv2, last, s2):
    par = parity()
    for c in range(2, 8):
        for i, v in enumerate(coarser(level2_load(s, c - 4), R2, 2)):
            s2[i, c, pl.ds(0, R2), :] = v
    for k in range(2):
        rows = pl.ds(R1 + R2 * k, R2)
        lower, upper = both_sides(par, two[rows, :], its[pl.ds(O_TWO + R1 + R2 * k, R2), :])
        for i in range(4):
            s2[i, k, pl.ds(0, R2), :] = unpack4(lower, i)
            s2[i, 8 + k, pl.ds(0, R2), :] = unpack4(upper, i)
    s2[2, :, R2:, :] = jnp.zeros((10, PAD, PZ), F32)
    body = pl.ds(0, R2)
    for c in range(9):
        _, inv, w6 = faces(
            s2[0, c, body, :], s2[1, c, body, :], s2[1, c + 1, body, :], s2[2, c, body, :], s2[2, c, pl.ds(1, R2), :],
            s2[3, c, body, :], 4, 0.0625,
        )
        for a, f in enumerate(w6):
            w2[a, c + 1] = f
        inv2[c + 1] = inv
    for i in range(4):
        last[i] = s2[i, 9]


def last_kernel(two2, its2, rhs, w2, inv2, last, pre1, w1, c1, pre0, sw, xs, w0, c0, out,
                wx, c2, x2, y2, z2, x1, y1, z1, x0, y0):
    par = parity()
    body = pl.ds(PAD, R2)
    lo, hi = both_sides(par, two2[:R2], its2[:R2])
    _, beyond = both_sides(par, two2[R2:], its2[R2:])
    clear_pads(x2, R2)
    clear_pads(y2, R2)
    clear_pads(z2, R2)
    _, inv, w6 = faces(
        last[0, :R2], last[1, :R2], beyond, last[2, :R2], last[2, pl.ds(1, R2), :], last[3, :R2], 4, 0.0625
    )
    for a, f in enumerate(w6):
        wx[a, 0] = f

    def start(j, b, dinv):
        v = dinv * b
        c2[j] = v
        x2[j, body, :] = v * (1.0 / THETA)

    for k in range(3):
        start(3 - k, unpack4(lo, k), inv2[3 - k])
        start(8 + k, unpack4(hi, k), inv2[8 + k] if k < 2 else inv)
    for c in range(4):
        start(c + 4, rhs[c], inv2[c + 4])
    x2[0, body, :] = unpack4(lo, 3)
    x2[11, body, :] = unpack4(hi, 3)
    rows = (0, R2)
    sweep(x2, None, c2, w2, 1, 10, rows, 4, 1, into(y2), R2, unroll=9)
    sweep(x2, None, c2, wx, 10, 11, rows, 4, 1, into(y2), R2, woff=-10)
    sweep(y2, x2, c2, w2, 2, 10, rows, 4, 2, into(z2), R2, unroll=8)
    sweep(z2, y2, c2, w2, 3, 9, rows, 4, 3, into(x2), R2, unroll=6)

    for q in range(8):
        v = x2[(q - 3) // 2 + M0 + par, body, :]
        z1[q, pl.ds(PAD, R2, 2), :] = v
        z1[q, pl.ds(PAD + 1, R2, 2), :] = v
        x1[q, pl.ds(PAD, R1), :] = pre1[q + 2 * par] + z1[q, pl.ds(PAD, R1), :]
    rows = (8, R1 - 8)
    off = C0 - 3 + 2 * par
    sweep(x1, None, c1, w1, 1, 7, rows, 2, 0, into(y1), 24, woff=off, coff=off, unroll=6)
    sweep(y1, x1, c1, w1, 2, 6, rows, 2, 1, into(z1), 24, woff=off, coff=off, unroll=4)

    clear_pads(x0, MID)
    clear_pads(y0, MID)
    near, far = 7 - 7 * par, 7 * par
    body = pl.ds(PAD, MID)
    for q in range(8):
        v = z1[(q - 2) // 2 + 3, pl.ds(PAD + 12, MID // 2), :]
        x0[q, pl.ds(PAD, MID // 2, 2), :] = v
        x0[q, pl.ds(PAD + 1, MID // 2, 2), :] = v
        if 0 < q < 7:
            x0[q, body, :] += pre0[q - 1]
    x0[near, body, :] += sw[pl.ds(O_EDGE, MID), :]
    x0[far, body, :] += xs[pl.ds(5 * R1, MID), :]
    off = Q0 - 2
    sweep(x0, None, c0, w0, 1, 7, (0, MID), 1, 0, into(y0), 40, woff=off, coff=off, wr=MID0, cr=MID0, unroll=6)

    def finish(q, r0, n, v):
        out[q - 2, pl.ds(r0 - 8, n), :] = v

    sweep(y0, x0, c0, w0, 2, 6, (8, 8 + PY), 1, 1, finish, 32, woff=off, coff=off, wr=MID0, cr=MID0, unroll=4)


def swap(v):
    return lax.ppermute(v, "wide", [(i, i ^ 1) for i in range(lax.axis_size("wide"))])


def across(v, chips, ends=()):
    count = lax.axis_size("wide")
    step = 2 * chips - 1
    pairs = [(i, i + step) for i in range(1, count, 2) if i + step < count]
    pairs += [(i, i - step) for i in range(0, count, 2) if i - step >= 0]
    return lax.ppermute(v, "wide", pairs + list(ends))


def from_beside(v):
    count = lax.axis_size("wide")
    pairs = [(i, i + 2) for i in range(0, count - 2, 2)] + [(i, i - 2) for i in range(3, count, 2)]
    return lax.ppermute(v, "wide", pairs)


def shifted(v, axis, step):
    count = lax.axis_size(axis)
    return lax.ppermute(v, axis, [(i, i + step) for i in range(count) if 0 <= i + step < count])


def shards(right_side, alpha_coef, beta_x, beta_y, beta_z):
    a, ylo, yhi, ex = call(
        pack_kernel, "pack", (shape(5, PX, PY, PZ), shape(5 * PX * HY, PZ), shape(5 * PX * HY, PZ), shape(5 * PY, PZ)),
        (VMEM,) * 4, [ANY] * 5, [pltpu.SemaphoreType.DMA((5,))], SMALL,
    )(*[pltpu.with_memory_space_constraint(v, pltpu.HBM) for v in (right_side, alpha_coef, beta_x, beta_y, beta_z)])
    lo = shifted(yhi, "narrow", 1)
    hi = shifted(ylo, "narrow", -1)
    ex = across(ex, 1)
    own, sw, xs = call(
        corner_kernel, "corners", (shape(RAW + 4 * R1, PZ), shape(SRAW + 4 * R1, PZ), shape(XB + R1, PZ)),
        (VMEM,) * 3, [VMEM] * 3 + [ANY] * 2, [scratch(3, EY + 2 * PAD, PZ), scratch(2, 3 * EY, PZ)], SMALL,
    )(a, lo, hi, ex, first_to_arrive(lo, hi))
    xs = across(xs, 1)
    sw = swap(sw)

    send, send1, send2, edge0, pre0, w0, c0 = call(
        fine_kernel, "level0_pre",
        (shape(5 * R1 + MID, PZ), shape(5 * R1, PZ), shape(2 * R1, PZ), shape(MID, PZ), shape(6, MID, PZ),
         shape(6, 10, EY, PZ), shape(10, EY, PZ)),
        (VMEM,) * 7, [VMEM] * 4 + [ANY],
        [scratch(10, EY, PZ), scratch(10, EY, PZ)] + [scratch(10, EY + 2 * PAD, PZ)] * 3
        + [scratch(2, EY, PZ), scratch(4, 5, R1, PZ), scratch(R1 + PAD, PZ), scratch(5, EY, PZ)],
        LARGE,
    )(own, sw, xs, ex, first_to_arrive(xs))

    one = across(send, 1)
    beside = from_beside(send1)
    two = across(send2, 2)
    mine = call(join_kernel, "join", shape(O_END, PZ), VMEM, [VMEM] * 5, [], SMALL)(send, edge0, one, beside, two)
    its = swap(mine)
    w1_shapes = (shape(*S_SHAPE), shape(6, N1, R1, PZ), shape(N1, R1, PZ), shape(N1, R1, PZ))
    s1, w1, inv1, d1 = call(
        near_coefficients_kernel, "near_coefficients", w1_shapes, (VMEM,) * 4, [VMEM] * 4, [], LARGE,
    )(own[RAW:], sw[SRAW:], one, beside)

    edge, c1, pre1, rhs2, s1, w1, _, _ = call(
        middle_kernel, "level1_pre",
        (shape(2 * R2, PZ), shape(N1, R1, PZ), shape(10, R1, PZ), shape(4, R2, PZ)) + w1_shapes,
        (VMEM,) * 8, [VMEM] * 9,
        [scratch(N1, R1 + 2 * PAD, PZ)] * 3 + [scratch(4, R1, PZ), scratch(2, R2 + PAD, PZ)],
        LARGE, aliases={5: 4, 6: 5, 7: 6, 8: 7},
    )(send, one, beside, two, its, s1, w1, inv1, d1)

    w2, inv2, last2 = call(
        coarse_coefficients_kernel, "level2_coefficients",
        (shape(6, 12, R2, PZ), shape(12, R2, PZ), shape(4, R2 + PAD, PZ)),
        (VMEM,) * 3, [VMEM] * 3, [scratch(4, 10, R2 + PAD, PZ)], LARGE,
    )(s1, two, its)
    count = lax.axis_size("wide")
    two2 = across(edge, 2, ((0, 2), (count - 1, count - 3)))
    its2 = swap(two2)
    return call(
        last_kernel, "coarse_and_post", shape(PX, PY, PZ), VMEM, [VMEM] * 14,
        [scratch(6, 1, R2, PZ), scratch(12, R2, PZ)] + [scratch(12, R2 + 2 * PAD, PZ)] * 3
        + [scratch(8, R1 + 2 * PAD, PZ)] * 3 + [scratch(8, MID + 2 * PAD, PZ)] * 2,
        LARGE,
    )(two2, its2, rhs2, w2, inv2, last2, pre1, w1, c1, pre0, its, one, w0, c0)


def solution(mesh):
    spec = P("wide", "narrow", None)
    return jax.shard_map(shards, mesh=mesh, in_specs=(spec,) * 5, out_specs=spec, check_vma=False)
```

```python
import jax
import jax.numpy as jnp
from jax import lax
from jax.experimental import pallas as pl
from jax.experimental.pallas import tpu as pltpu
from jax.sharding import PartitionSpec as P

F32 = jnp.float32
THETA = (2.0 + 0.25) / 2.0
DELTA = (2.0 - 0.25) / 2.0
SIGMA = THETA / DELTA
RHO = [1.0 / SIGMA]
for _step in range(3):
    RHO.append(1.0 / (2.0 * SIGMA - RHO[-1]))
MOMENTUM = [0.0] + [RHO[k] * RHO[k - 1] for k in range(1, 4)]
GAIN = [1.0 / THETA] + [2.0 * RHO[k] / DELTA for k in range(1, 4)]

PX, PY, PZ = 4, 64, 128
HY = 32
EY = PY + 2 * HY
MID = PY + 16
MID0 = HY - 8
R1 = EY // 2
R2 = R1 // 2
RAW = 5 * PX * EY
SRAW = 8 * EY
XP = 5 * 2 * HY
XB = XP + 3 * EY
PAD = 8
SMALL, LARGE = 1000, 2 * 10**10
B, ALPHA, BX, BY, BZ = range(5)
ANY = pl.BlockSpec(memory_space=pl.ANY)
VMEM = pl.BlockSpec(memory_space=pltpu.VMEM)
HBM = pl.BlockSpec(memory_space=pltpu.HBM)


def shape(*dims):
    return jax.ShapeDtypeStruct(dims, F32)


def scratch(*dims):
    return pltpu.VMEM(dims, F32)


def call(kernel, name, out_shape, out_specs, in_specs, scratch_shapes, flops, mib=24, aliases=None):
    return pl.pallas_call(
        kernel,
        out_shape=out_shape,
        in_specs=in_specs,
        out_specs=out_specs,
        scratch_shapes=scratch_shapes,
        compiler_params=pltpu.CompilerParams(vmem_limit_bytes=mib * 1024 * 1024),
        cost_estimate=pl.CostEstimate(flops=flops, bytes_accessed=0, transcendentals=0),
        input_output_aliases=aliases or {},
        name=name,
    )


def parity():
    return lax.rem(lax.axis_index("wide"), 2)


def lanes(rows):
    return lax.broadcasted_iota(jnp.int32, (rows, PZ), 1)


def moved(v, shift):
    return pltpu.roll(v, shift % PZ, 1)


def planes(lo, hi, each, unroll):
    if not unroll:
        each(lo)
        return
    steps = (hi - lo) // unroll

    def body(i, carry):
        for k in range(unroll):
            each(lo + i * unroll + k)
        return carry

    if steps > 1:
        lax.fori_loop(0, steps, body, 0)
    else:
        steps = 0
    for q in range(lo + steps * unroll, hi):
        each(q)


def defect(x_ref, c_ref, w_ref, q, r0, n, reach, cq, cr, wq, wr):
    rows = pl.ds(PAD + r0, n)
    here = pl.ds(wr + r0, n)
    x = x_ref[q, rows, :]
    total = c_ref[cq, pl.ds(cr + r0, n), :] - x
    total += w_ref[0, wq, here, :] * x_ref[q - 1, rows, :]
    total += w_ref[1, wq, here, :] * x_ref[q + 1, rows, :]
    total += w_ref[2, wq, here, :] * x_ref[q, pl.ds(PAD + r0 - 1, n), :]
    total += w_ref[3, wq, here, :] * x_ref[q, pl.ds(PAD + r0 + 1, n), :]
    total += w_ref[4, wq, here, :] * moved(x, reach)
    total += w_ref[5, wq, here, :] * moved(x, -reach)
    return x, total


def sweep(x_ref, prev_ref, c_ref, w_ref, lo, hi, rows, reach, k, store, chunk, woff=0, coff=0, wr=0, cr=0, unroll=8):
    def each(q):
        for r0 in range(rows[0], rows[1], chunk):
            n = min(chunk, rows[1] - r0)
            x, z = defect(x_ref, c_ref, w_ref, q, r0, n, reach, q + coff, cr, q + woff, wr)
            new = x + GAIN[k] * z
            if k > 0:
                gap = x if prev_ref is None else x - prev_ref[q, pl.ds(PAD + r0, n), :]
                new += MOMENTUM[k] * gap
            store(q, r0, n, new)

    planes(lo, hi, each, unroll)


def into(ref):
    def store(q, r0, n, v):
        ref[q, pl.ds(PAD + r0, n), :] = v

    return store


def inverse(d):
    inside = d > 0.0
    return jnp.where(inside, 1.0 / jnp.where(inside, d, 1.0), 0.0)


def faces(alpha, x0, x1, y0, y1, z0, reach, scale):
    z1 = moved(z0, -reach)
    d = alpha + scale * (x0 + x1 + y0 + y1 + z0 + z1)
    inv = inverse(d)
    si = scale * inv
    return d, inv, [si * f for f in (x0, x1, y0, y1, z0, z1)]


def next_rows(load, r0, n, rows):
    if r0 + n < rows:
        return load(r0 + 1, n)
    return pltpu.roll(load(r0, n), n - 1, 0)


def clear_pads(ref, rows):
    ref[:, :PAD, :] = jnp.zeros((ref.shape[0], PAD, PZ), F32)
    ref[:, PAD + rows :, :] = jnp.zeros((ref.shape[0], PAD, PZ), F32)


def pair_lanes(v, reach):
    low = (lanes(v.shape[0]) & reach) == 0
    return v + jnp.where(low, moved(v, -reach), moved(v, reach))


def low_lanes(v, reach):
    low = (lanes(v.shape[0]) & reach) == 0
    return jnp.where(low, v, moved(v, reach))


def pack2(v0, v1):
    return jnp.where((lanes(v0.shape[0]) & 1) == 0, v0, v1)


def unpack2(v):
    even = (lanes(v.shape[0]) & 1) == 0
    return jnp.where(even, v, moved(v, 1)), jnp.where(even, moved(v, -1), v)


def pack4(items):
    place = lanes(items[0].shape[0]) & 3
    out = items[0]
    for i, item in enumerate(items[1:], 1):
        out = jnp.where(place == i, item, out)
    return out


def unpack4(v, i):
    place = lanes(v.shape[0]) & 3
    out = v
    for m in range(4):
        if m != i:
            out = jnp.where(place == m, moved(v, m - i), out)
    return out


def coarser(load, rows, reach):
    def cell(i):
        return load(i, 0, 0) + load(i, 0, 1) + load(i, 1, 0) + load(i, 1, 1)

    al = pair_lanes(cell(0), reach) * 0.125
    bx = pair_lanes(load(1, 0, 0) + load(1, 0, 1), reach) * 0.25
    by = pair_lanes(load(2, 0, 0) + load(2, 1, 0), reach) * 0.25
    bz = low_lanes(cell(3), reach) * 0.25
    return al, bx, by, bz


def pack_kernel(b, al, bx, by, bz, a, one_out, two_out, xs_out, sems):
    wide, narrow = lax.axis_index("wide"), lax.axis_index("narrow")
    par = lax.rem(wide, 2)
    copies = [pltpu.make_async_copy(ref, a.at[i], sems.at[i]) for i, ref in enumerate((b, al, bx, by, bz))]
    for c in copies:
        c.start()
    for c in copies:
        c.wait()
    row = lax.broadcasted_iota(jnp.int32, (PAD, PZ), 0)
    first_row = jnp.logical_and(row == 0, jnp.broadcast_to(narrow, (PAD, PZ)) == 0)
    a[BX, 0] = jnp.where(jnp.broadcast_to(wide, (PY, PZ)) == 0, 0.0, a[BX, 0])
    first_z = lanes(PY) == 0
    for p in range(PX):
        a[BY, p, :PAD] = jnp.where(first_row, 0.0, a[BY, p, :PAD])
        a[BZ, p] = jnp.where(first_z, 0.0, a[BZ, p])
    for i in range(5):
        for p in range(PX):
            here = pl.ds((PX * i + p) * HY, HY)
            one_out[here, :] = a[i, p, pl.ds(pl.multiple_of((1 - par) * (PY - HY), 8), HY), :]
            two_out[here, :] = a[i, p, pl.ds(pl.multiple_of(par * (PY - HY), 8), HY), :]
        xs_out[pl.ds(i * PY, PY), :] = a[i, 3 * par]


def plane(ref, k, r0=0, n=EY):
    start = k * EY + r0
    return ref[pl.ds(pl.multiple_of(start, 8) if r0 % 8 == 0 else start, n), :]


def corner_kernel(a, one, two, _, __, own, sw, xs, x, v):
    par = parity()
    for i in range(5):
        for p in range(PX):
            k = PX * i + p
            here = pl.ds(k * HY, HY)
            own[pl.ds(pl.multiple_of(k * EY + par * (HY + PY), 8), HY), :] = one[here, :]
            own[pl.ds(k * EY + HY, PY), :] = a[i, p]
            own[pl.ds(pl.multiple_of(k * EY + (1 - par) * (HY + PY), 8), HY), :] = two[here, :]
    got = []
    for c in range(2):

        def load(i, k, row):
            return own[pl.ds((PX * (i + 1) + 2 * c + k) * EY + row, R1, 2), :]

        got.append(coarser(load, R1, 1))
    for i in range(4):
        t = pack2(got[0][i], got[1][i])
        own[pl.ds(RAW + R1 * i, R1), :] = t
        sw[pl.ds(SRAW + R1 * i, R1), :] = t
    xs[pl.ds(XB, R1), :] = own[pl.ds(RAW + R1, R1), :]
    for i in range(5):
        xs[pl.ds(2 * HY * i, HY), :] = plane(own, PX * i + 3 * par, 0, HY)
        xs[pl.ds(2 * HY * i + HY, HY), :] = plane(own, PX * i + 3 * par, HY + PY, HY)
        sw[pl.ds(i * EY, EY), :] = plane(own, PX * i + 3 - 3 * par)
    clear_pads(x, EY)
    body = pl.ds(PAD, EY)
    kept = []
    for p in range(3):
        by = plane(own, PX * BY + p)
        _, inv, w = faces(
            plane(own, PX * ALPHA + p), plane(own, PX * BX + p), plane(own, PX * BX + p + 1), by,
            pltpu.roll(by, EY - 1, 0), plane(own, PX * BZ + p), 1, 1.0,
        )
        c0 = inv * plane(own, PX * B + p)
        x[p, body, :] = c0 * (1.0 / THETA)
        kept.append((w, c0))
    for up in range(2):
        second = 1 + up
        w, c0 = kept[second]
        here = x[second, body, :]
        z = c0 - here + w[0] * x[second - 1, body, :]
        if not up:
            z += w[1] * x[2, body, :]
        z += w[2] * x[second, pl.ds(PAD - 1, EY), :] + w[3] * x[second, pl.ds(PAD + 1, EY), :]
        z += w[4] * moved(here, 1) + w[5] * moved(here, -1)
        v[up, pl.ds(0, EY), :] = here
        v[up, pl.ds(EY, EY), :] = here + GAIN[1] * z + MOMENTUM[1] * here
        v[up, pl.ds(2 * EY, EY), :] = w[1] if up else plane(own, PX * BX + second)
    xs[pl.ds(XP, 3 * EY), :] = v[par]
    sw[pl.ds(5 * EY, 3 * EY), :] = v[1 - par]


Q0 = 3


def fine_kernel(own, sw, xs, ex, _, send, send1, send2, edge, pre, w, cc, sx, d, x, y, z, t, s, u, sf):
    par = parity()
    for i in range(5):
        sf[i, :HY] = xs[pl.ds(2 * HY * i, HY), :]
        sf[i, HY : HY + PY] = ex[pl.ds(PY * i, PY), :]
        sf[i, HY + PY :] = xs[pl.ds(2 * HY * i + HY, HY), :]

    def far(i, r, n):
        return sf[i, pl.ds(r, n), :] if i < 5 else xs[pl.ds(XP + (i - 5) * EY + r, n), :]

    def near(i, r, n):
        return plane(sw, i, r, n)

    sides2 = ((far, par), (near, 1 - par))
    for i in range(4):
        for p, ref, base in ((par, own, RAW), (1 - par, sw, SRAW)):
            v0, v1 = unpack2(ref[pl.ds(base + R1 * i, R1), :])
            s[i, 2 * p] = v0
            s[i, 2 * p + 1] = v1
    s[1, 4] = unpack2(xs[pl.ds(XB, R1), :])[0]
    for p in range(PX):
        sx[Q0 + p] = plane(own, PX * BX + p)
    for get, above in sides2:
        sx[2 + 5 * above] = get(BX, 0, EY)
        sx[9 - above] = get(7, 0, EY)
    clear_pads(x, EY)
    clear_pads(y, EY)
    chunk = 32

    def prepare(q, get):
        for r0 in range(0, EY, chunk):
            here = pl.ds(r0, chunk)

            def load(i):
                return lambda r, n: get(i, r, n)

            dd, inv, w6 = faces(
                load(ALPHA)(r0, chunk), sx[q, here, :], sx[q + 1, here, :], load(BY)(r0, chunk),
                next_rows(load(BY), r0, chunk, EY), load(BZ)(r0, chunk), 1, 1.0,
            )
            for a, f in enumerate(w6):
                w[a, q, here, :] = f
            c0 = inv * load(B)(r0, chunk)
            cc[q, here, :] = c0
            x[q, pl.ds(PAD + r0, chunk), :] = c0 * (1.0 / THETA)
            d[q, here, :] = dd

    for p in range(PX):
        prepare(Q0 + p, lambda i, r, n: plane(own, PX * i + p, r, n))
    body = pl.ds(PAD, EY)
    for get, above in sides2:
        q = 2 + 5 * above
        prepare(q, get)
        x[1 + 7 * above, body, :] = get(5, 0, EY)
        missing = GAIN[1] * get(7, 0, EY) * x[q, body, :]
        below = jnp.broadcast_to(above, missing.shape) == 0
        y[1 + 7 * above, body, :] = get(6, 0, EY) + jnp.where(below, missing, 0.0)

    rows = (0, EY)
    sweep(x, None, cc, w, 2, 8, rows, 1, 1, into(y), chunk)
    sweep(y, x, cc, w, 2, 8, rows, 1, 2, into(z), chunk)
    got = []
    for c in range(2):
        for r0 in range(0, EY, chunk):
            v = 0.0
            for q in (Q0 + 2 * c, Q0 + 2 * c + 1):
                _, zz = defect(z, cc, w, q, r0, chunk, 1, q, 0, q, 0)
                v = v + d[q, pl.ds(r0, chunk), :] * zz
            t[c, pl.ds(r0, chunk), :] = v
        got.append(pair_lanes(t[c, pl.ds(0, R1, 2), :] + t[c, pl.ds(1, R1, 2), :], 1) * 0.125)
    mid = pl.ds(PAD + MID0, MID)
    rhs = pack2(got[0], got[1])
    for out in (send, send1):
        out[:R1] = rhs
        out[pl.ds(R1, 4 * R1), :] = own[pl.ds(RAW, 4 * R1), :]
    edge[...] = z[Q0 + 2 - par, mid, :]
    send[pl.ds(5 * R1, MID), :] = z[Q0 + 1 + par, mid, :]
    q = 3 * par
    u[:R1] = s[2, q]
    u[R1:] = jnp.zeros((PAD, PZ), F32)
    _, inv, _ = faces(s[0, q], s[1, q], s[1, q + 1], u[:R1], u[pl.ds(1, R1), :], s[3, q], 2, 0.25)
    x1 = inv * jnp.where(jnp.broadcast_to(par, rhs.shape) == 0, *unpack2(rhs)) * (1.0 / THETA)
    send2[:R1] = pack2(x1, s[1, q])
    for c in range(2):

        def load(i, k, row):
            return s[i, 2 * c + k, pl.ds(row, R2, 2), :]

        send2[pl.ds(R1 + R2 * c, R2), :] = pack4(coarser(load, R2, 2))
    for p in range(6):
        pre[p] = z[Q0 - 1 + p, mid, :]


C0 = 5
N1 = 14
M0 = 5
S_SHAPE = (4, N1, R1 + 2 * PAD, PZ)
O_EDGE = R1
O_ONE = O_EDGE + MID
O_BESIDE = O_ONE + R1
O_TWO = O_BESIDE + R1
O_RAW = O_TWO + 2 * R1
O_END = O_RAW + 8 * R1


def place_coefficients(s, i, e, v):
    v0, v1 = unpack2(v)
    s[i, 1 + 2 * e, pl.ds(PAD, R1), :] = v0
    s[i, 2 + 2 * e, pl.ds(PAD, R1), :] = v1


def middle_faces(s, w1, inv1, d1, q):
    for r0 in range(0, R1, 32):
        here, up, out = pl.ds(PAD + r0, 32), pl.ds(PAD + r0 + 1, 32), pl.ds(r0, 32)
        dd, inv, w6 = faces(
            s[0, q, here, :], s[1, q, here, :], s[1, q + 1, here, :], s[2, q, here, :], s[2, q, up, :],
            s[3, q, here, :], 2, 0.25,
        )
        for a, f in enumerate(w6):
            w1[a, q, out, :] = f
        inv1[q, out, :] = inv
        d1[q, out, :] = dd


def sides(par, k):
    lower, upper = 1 - k, 4 + k
    return jnp.where(par == 0, lower, upper), jnp.where(par == 0, upper, lower)


def level2_load(s, plane):
    def load(i, k, row):
        return s[i, 2 * plane + C0 + k, pl.ds(PAD + row, R2, 2), :]

    return load


def near_coefficients_kernel(own, other, one, beside, s, w1, inv1, d1):
    par = parity()
    for i in range(4):
        s[i, :, PAD + R1 :, :] = jnp.zeros((N1, PAD, PZ), F32)
        rows = pl.ds(R1 * i, R1)
        sent = pl.ds(R1 * (1 + i), R1)
        place_coefficients(s, i, 2 + par, own[rows, :])
        place_coefficients(s, i, 3 - par, other[rows, :])
        place_coefficients(s, i, sides(par, 0)[0], one[sent, :])
        place_coefficients(s, i, sides(par, 1)[0], beside[sent, :])
    for k in range(7):
        middle_faces(s, w1, inv1, d1, 1 + 4 * par + k)


def join_kernel(own, edge, one, beside, two, out):
    out[:R1] = own[:R1]
    out[pl.ds(O_EDGE, MID), :] = edge[...]
    out[pl.ds(O_ONE, R1), :] = one[:R1]
    out[pl.ds(O_BESIDE, R1), :] = beside[:R1]
    out[pl.ds(O_TWO, 2 * R1), :] = two[...]
    out[pl.ds(O_RAW, 4 * R1), :] = one[pl.ds(R1, 4 * R1), :]
    out[pl.ds(O_RAW + 4 * R1, 4 * R1), :] = beside[pl.ds(R1, 4 * R1), :]


def tick_kernel(*refs):
    refs[-1][...] = jnp.zeros(refs[-1].shape, F32)


def first_to_arrive(*values):
    return call(tick_kernel, "tick", shape(PAD, PZ), VMEM, [ANY] * len(values), [], LARGE)(*values)


def both_sides(par, mine, its):
    upper = jnp.broadcast_to(par, mine.shape) == 1
    return jnp.where(upper, its, mine), jnp.where(upper, mine, its)


def middle_kernel(own, one, beside, two, its, s_in, w_in, inv_in, d_in, edge, cc, pre, rhs, s, w, inv, d,
                  x, y, z, t, u):
    par = parity()
    clear_pads(x, R1)
    clear_pads(y, R1)
    body = pl.ds(PAD, R1)
    lower, upper = both_sides(par, two[:R1], its[pl.ds(O_TWO, R1), :])
    x[0, body, :] = unpack2(lower)[0]
    x1, bx = unpack2(upper)
    x[N1 - 1, body, :] = x1
    s[1, N1 - 1, body, :] = bx
    for k in range(2):
        e = sides(par, k)[1]
        for i in range(4):
            place_coefficients(s, i, e, its[pl.ds(O_RAW + (4 * k + i) * R1, R1), :])
    for k in range(5):
        middle_faces(s, w, inv, d, jnp.where(par == 0, 8 + k, 1 + k if k < 4 else 12))

    def place(e, v):
        for k, b in enumerate(unpack2(v)):
            q = 1 + 2 * e + k
            c0 = inv[q] * b
            cc[q] = c0
            x[q, body, :] = c0 * (1.0 / THETA)

    place(2 + par, own[:R1])
    place(3 - par, its[:R1])
    for k, ref, row in ((0, one, O_ONE), (1, beside, O_BESIDE)):
        e, f = sides(par, k)
        place(e, ref[:R1])
        place(f, its[pl.ds(row, R1), :])

    rows = (0, R1)
    sweep(x, None, cc, w, 1, 13, rows, 2, 1, into(y), 32, unroll=12)
    sweep(y, x, cc, w, 2, 12, rows, 2, 2, into(z), 32, unroll=10)

    for c in range(4):
        for r0 in range(0, R1, 32):
            v = 0.0
            for k in range(2):
                q = C0 - 2 + 2 * c + k
                _, zz = defect(z, cc, w, q, r0, 32, 2, q, 0, q, 0)
                v = v + d[q, pl.ds(r0, 32), :] * zz
            t[c, pl.ds(r0, 32), :] = v
        rhs[c] = pair_lanes(t[c, pl.ds(0, R2, 2), :] + t[c, pl.ds(1, R2, 2), :], 2) * 0.125

    def first(k, plane):
        al, bx, by, bz = coarser(level2_load(s, plane), R2, 2)
        after = level2_load(s, plane + 1)
        bx1 = pair_lanes(after(1, 0, 0) + after(1, 0, 1), 2) * 0.25
        u[k, pl.ds(0, R2), :] = by
        u[k, pl.ds(R2, PAD), :] = jnp.zeros((PAD, PZ), F32)
        _, inv2, _ = faces(al, bx, bx1, by, u[k, pl.ds(1, R2), :], bz, 4, 0.0625)
        return inv2 * rhs[plane + 1] * (1.0 / THETA), bx

    below, above = first(0, -1), first(1, 2)
    up = pack4([rhs[3], rhs[2], rhs[1], below[0]])
    down = pack4([rhs[0], rhs[1], rhs[2], above[0]])
    wide = jnp.broadcast_to(lax.axis_index("wide"), up.shape)
    ends = (lanes(R2) & 3) == 0
    down = jnp.where(wide == 0, jnp.where(ends, rhs[1], 0.0), down)
    up = jnp.where(wide == lax.axis_size("wide") - 1, jnp.where(ends, rhs[2], 0.0), up)
    edge[:R2] = jnp.where(jnp.broadcast_to(par, up.shape) == 0, down, up)
    edge[R2:] = above[1]
    for p in range(10):
        pre[p] = z[C0 - 3 + p, body, :]


def coarse_coefficients_kernel(s, two, its, w2, inv2, last, s2):
    par = parity()
    for c in range(2, 8):
        for i, v in enumerate(coarser(level2_load(s, c - 4), R2, 2)):
            s2[i, c, pl.ds(0, R2), :] = v
    for k in range(2):
        rows = pl.ds(R1 + R2 * k, R2)
        lower, upper = both_sides(par, two[rows, :], its[pl.ds(O_TWO + R1 + R2 * k, R2), :])
        for i in range(4):
            s2[i, k, pl.ds(0, R2), :] = unpack4(lower, i)
            s2[i, 8 + k, pl.ds(0, R2), :] = unpack4(upper, i)
    s2[2, :, R2:, :] = jnp.zeros((10, PAD, PZ), F32)
    body = pl.ds(0, R2)
    for c in range(9):
        _, inv, w6 = faces(
            s2[0, c, body, :], s2[1, c, body, :], s2[1, c + 1, body, :], s2[2, c, body, :], s2[2, c, pl.ds(1, R2), :],
            s2[3, c, body, :], 4, 0.0625,
        )
        for a, f in enumerate(w6):
            w2[a, c + 1] = f
        inv2[c + 1] = inv
    for i in range(4):
        last[i] = s2[i, 9]


def last_kernel(two2, its2, rhs, w2, inv2, last, pre1, w1, c1, pre0, sw, xs, w0, c0, out,
                wx, c2, x2, y2, z2, x1, y1, z1, x0, y0):
    par = parity()
    body = pl.ds(PAD, R2)
    lo, hi = both_sides(par, two2[:R2], its2[:R2])
    _, beyond = both_sides(par, two2[R2:], its2[R2:])
    clear_pads(x2, R2)
    clear_pads(y2, R2)
    clear_pads(z2, R2)
    _, inv, w6 = faces(
        last[0, :R2], last[1, :R2], beyond, last[2, :R2], last[2, pl.ds(1, R2), :], last[3, :R2], 4, 0.0625
    )
    for a, f in enumerate(w6):
        wx[a, 0] = f

    def start(j, b, dinv):
        v = dinv * b
        c2[j] = v
        x2[j, body, :] = v * (1.0 / THETA)

    for k in range(3):
        start(3 - k, unpack4(lo, k), inv2[3 - k])
        start(8 + k, unpack4(hi, k), inv2[8 + k] if k < 2 else inv)
    for c in range(4):
        start(c + 4, rhs[c], inv2[c + 4])
    x2[0, body, :] = unpack4(lo, 3)
    x2[11, body, :] = unpack4(hi, 3)
    rows = (0, R2)
    sweep(x2, None, c2, w2, 1, 10, rows, 4, 1, into(y2), R2, unroll=9)
    sweep(x2, None, c2, wx, 10, 11, rows, 4, 1, into(y2), R2, woff=-10)
    sweep(y2, x2, c2, w2, 2, 10, rows, 4, 2, into(z2), R2, unroll=8)
    sweep(z2, y2, c2, w2, 3, 9, rows, 4, 3, into(x2), R2, unroll=6)

    for q in range(8):
        v = x2[(q - 3) // 2 + M0 + par, body, :]
        z1[q, pl.ds(PAD, R2, 2), :] = v
        z1[q, pl.ds(PAD + 1, R2, 2), :] = v
        x1[q, pl.ds(PAD, R1), :] = pre1[q + 2 * par] + z1[q, pl.ds(PAD, R1), :]
    rows = (8, R1 - 8)
    off = C0 - 3 + 2 * par
    sweep(x1, None, c1, w1, 1, 7, rows, 2, 0, into(y1), 24, woff=off, coff=off, unroll=6)
    sweep(y1, x1, c1, w1, 2, 6, rows, 2, 1, into(z1), 24, woff=off, coff=off, unroll=4)

    clear_pads(x0, MID)
    clear_pads(y0, MID)
    near, far = 7 - 7 * par, 7 * par
    body = pl.ds(PAD, MID)
    for q in range(8):
        v = z1[(q - 2) // 2 + 3, pl.ds(PAD + 12, MID // 2), :]
        x0[q, pl.ds(PAD, MID // 2, 2), :] = v
        x0[q, pl.ds(PAD + 1, MID // 2, 2), :] = v
        if 0 < q < 7:
            x0[q, body, :] += pre0[q - 1]
    x0[near, body, :] += sw[pl.ds(O_EDGE, MID), :]
    x0[far, body, :] += xs[pl.ds(5 * R1, MID), :]
    off = Q0 - 2
    sweep(x0, None, c0, w0, 1, 7, (0, MID), 1, 0, into(y0), 40, woff=off, coff=off, wr=MID0, cr=MID0, unroll=6)

    def finish(q, r0, n, v):
        out[q - 2, pl.ds(r0 - 8, n), :] = v

    sweep(y0, x0, c0, w0, 2, 6, (8, 8 + PY), 1, 1, finish, 32, woff=off, coff=off, wr=MID0, cr=MID0, unroll=4)


def swap(v):
    return lax.ppermute(v, "wide", [(i, i ^ 1) for i in range(lax.axis_size("wide"))])


def across(v, chips, ends=()):
    count = lax.axis_size("wide")
    step = 2 * chips - 1
    pairs = [(i, i + step) for i in range(1, count, 2) if i + step < count]
    pairs += [(i, i - step) for i in range(0, count, 2) if i - step >= 0]
    return lax.ppermute(v, "wide", pairs + list(ends))


def from_beside(v):
    count = lax.axis_size("wide")
    pairs = [(i, i + 2) for i in range(0, count - 2, 2)] + [(i, i - 2) for i in range(3, count, 2)]
    return lax.ppermute(v, "wide", pairs)


def along_narrow(v, step):
    wide, narrow = lax.axis_size("wide"), lax.axis_size("narrow")
    pairs = []
    for i in range(wide):
        to = step if i % 2 == 0 else -step
        pairs += [(i * narrow + j, i * narrow + j + to) for j in range(narrow) if 0 <= j + to < narrow]
    return lax.ppermute(v, ("wide", "narrow"), pairs)


def shards(right_side, alpha_coef, beta_x, beta_y, beta_z):
    a, y1, y2, ex = call(
        pack_kernel, "pack", (shape(5, PX, PY, PZ), shape(5 * PX * HY, PZ), shape(5 * PX * HY, PZ), shape(5 * PY, PZ)),
        (VMEM,) * 4, [ANY] * 5, [pltpu.SemaphoreType.DMA((5,))], SMALL,
    )(*[pltpu.with_memory_space_constraint(v, pltpu.HBM) for v in (right_side, alpha_coef, beta_x, beta_y, beta_z)])
    y1, y2 = along_narrow(y1, 1), along_narrow(y2, -1)
    ex = across(ex, 1)
    own, sw, xs = call(
        corner_kernel, "corners", (shape(RAW + 4 * R1, PZ), shape(SRAW + 4 * R1, PZ), shape(XB + R1, PZ)),
        (VMEM,) * 3, [VMEM] * 3 + [ANY] * 2, [scratch(3, EY + 2 * PAD, PZ), scratch(2, 3 * EY, PZ)], SMALL,
    )(a, y1, y2, ex, first_to_arrive(y1, y2))
    xs = across(xs, 1)
    sw = swap(sw)

    send, send1, send2, edge0, pre0, w0, c0 = call(
        fine_kernel, "level0_pre",
        (shape(5 * R1 + MID, PZ), shape(5 * R1, PZ), shape(2 * R1, PZ), shape(MID, PZ), shape(6, MID, PZ),
         shape(6, 10, EY, PZ), shape(10, EY, PZ)),
        (VMEM,) * 7, [VMEM] * 4 + [ANY],
        [scratch(10, EY, PZ), scratch(10, EY, PZ)] + [scratch(10, EY + 2 * PAD, PZ)] * 3
        + [scratch(2, EY, PZ), scratch(4, 5, R1, PZ), scratch(R1 + PAD, PZ), scratch(5, EY, PZ)],
        LARGE,
    )(own, sw, xs, ex, first_to_arrive(xs))

    one = across(send, 1)
    beside = from_beside(send1)
    two = across(send2, 2)
    mine = call(join_kernel, "join", shape(O_END, PZ), VMEM, [VMEM] * 5, [], SMALL)(send, edge0, one, beside, two)
    its = swap(mine)
    w1_shapes = (shape(*S_SHAPE), shape(6, N1, R1, PZ), shape(N1, R1, PZ), shape(N1, R1, PZ))
    s1, w1, inv1, d1 = call(
        near_coefficients_kernel, "near_coefficients", w1_shapes, (VMEM,) * 4, [VMEM] * 4, [], LARGE,
    )(own[RAW:], sw[SRAW:], one, beside)

    edge, c1, pre1, rhs2, s1, w1, _, _ = call(
        middle_kernel, "level1_pre",
        (shape(2 * R2, PZ), shape(N1, R1, PZ), shape(10, R1, PZ), shape(4, R2, PZ)) + w1_shapes,
        (VMEM,) * 8, [VMEM] * 9,
        [scratch(N1, R1 + 2 * PAD, PZ)] * 3 + [scratch(4, R1, PZ), scratch(2, R2 + PAD, PZ)],
        LARGE, aliases={5: 4, 6: 5, 7: 6, 8: 7},
    )(send, one, beside, two, its, s1, w1, inv1, d1)

    w2, inv2, last2 = call(
        coarse_coefficients_kernel, "level2_coefficients",
        (shape(6, 12, R2, PZ), shape(12, R2, PZ), shape(4, R2 + PAD, PZ)),
        (VMEM,) * 3, [VMEM] * 3, [scratch(4, 10, R2 + PAD, PZ)], LARGE,
    )(s1, two, its)
    count = lax.axis_size("wide")
    two2 = across(edge, 2, ((0, 2), (count - 1, count - 3)))
    its2 = swap(two2)
    return call(
        last_kernel, "coarse_and_post", shape(PX, PY, PZ), VMEM, [VMEM] * 14,
        [scratch(6, 1, R2, PZ), scratch(12, R2, PZ)] + [scratch(12, R2 + 2 * PAD, PZ)] * 3
        + [scratch(8, R1 + 2 * PAD, PZ)] * 3 + [scratch(8, MID + 2 * PAD, PZ)] * 2,
        LARGE,
    )(two2, its2, rhs2, w2, inv2, last2, pre1, w1, c1, pre0, its, one, w0, c0)


def solution(mesh):
    spec = P("wide", "narrow", None)
    return jax.shard_map(shards, mesh=mesh, in_specs=(spec,) * 5, out_specs=spec, check_vma=False)
```

```python
import jax
import jax.numpy as jnp
from jax import lax
from jax.experimental import pallas as pl
from jax.experimental.pallas import tpu as pltpu
from jax.sharding import PartitionSpec as P

F32 = jnp.float32
THETA = (2.0 + 0.25) / 2.0
DELTA = (2.0 - 0.25) / 2.0
SIGMA = THETA / DELTA
RHO = [1.0 / SIGMA]
for _step in range(3):
    RHO.append(1.0 / (2.0 * SIGMA - RHO[-1]))
MOMENTUM = [0.0] + [RHO[k] * RHO[k - 1] for k in range(1, 4)]
GAIN = [1.0 / THETA] + [2.0 * RHO[k] / DELTA for k in range(1, 4)]

PX, PY, PZ = 4, 64, 128
HY = 32
EY = PY + 2 * HY
MID = PY + 16
MID0 = HY - 8
R1 = EY // 2
R2 = R1 // 2
RAW = 5 * PX * EY
SRAW = 8 * EY
XP = 5 * 2 * HY
INNER, EDGE = PY - 16, HY + 8
XB = XP + 3 * 2 * EDGE
EX_IN = 5 * PY
PAD = 8
SMALL, LARGE = 1000, 2 * 10**10
B, ALPHA, BX, BY, BZ = range(5)
ANY = pl.BlockSpec(memory_space=pl.ANY)
VMEM = pl.BlockSpec(memory_space=pltpu.VMEM)
HBM = pl.BlockSpec(memory_space=pltpu.HBM)


def shape(*dims):
    return jax.ShapeDtypeStruct(dims, F32)


def scratch(*dims):
    return pltpu.VMEM(dims, F32)


def call(kernel, name, out_shape, out_specs, in_specs, scratch_shapes, flops, mib=24, aliases=None):
    return pl.pallas_call(
        kernel,
        out_shape=out_shape,
        in_specs=in_specs,
        out_specs=out_specs,
        scratch_shapes=scratch_shapes,
        compiler_params=pltpu.CompilerParams(vmem_limit_bytes=mib * 1024 * 1024),
        cost_estimate=pl.CostEstimate(flops=flops, bytes_accessed=0, transcendentals=0),
        input_output_aliases=aliases or {},
        name=name,
    )


def parity():
    return lax.rem(lax.axis_index("wide"), 2)


def lanes(rows):
    return lax.broadcasted_iota(jnp.int32, (rows, PZ), 1)


def moved(v, shift):
    return pltpu.roll(v, shift % PZ, 1)


def planes(lo, hi, each, unroll):
    if not unroll:
        each(lo)
        return
    steps = (hi - lo) // unroll

    def body(i, carry):
        for k in range(unroll):
            each(lo + i * unroll + k)
        return carry

    if steps > 1:
        lax.fori_loop(0, steps, body, 0)
    else:
        steps = 0
    for q in range(lo + steps * unroll, hi):
        each(q)


def defect(x_ref, c_ref, w_ref, q, r0, n, reach, cq, cr, wq, wr):
    rows = pl.ds(PAD + r0, n)
    here = pl.ds(wr + r0, n)
    x = x_ref[q, rows, :]
    total = c_ref[cq, pl.ds(cr + r0, n), :] - x
    total += w_ref[0, wq, here, :] * x_ref[q - 1, rows, :]
    total += w_ref[1, wq, here, :] * x_ref[q + 1, rows, :]
    total += w_ref[2, wq, here, :] * x_ref[q, pl.ds(PAD + r0 - 1, n), :]
    total += w_ref[3, wq, here, :] * x_ref[q, pl.ds(PAD + r0 + 1, n), :]
    total += w_ref[4, wq, here, :] * moved(x, reach)
    total += w_ref[5, wq, here, :] * moved(x, -reach)
    return x, total


def sweep(x_ref, prev_ref, c_ref, w_ref, lo, hi, rows, reach, k, store, chunk, woff=0, coff=0, wr=0, cr=0, unroll=8):
    def each(q):
        for r0 in range(rows[0], rows[1], chunk):
            n = min(chunk, rows[1] - r0)
            x, z = defect(x_ref, c_ref, w_ref, q, r0, n, reach, q + coff, cr, q + woff, wr)
            new = x + GAIN[k] * z
            if k > 0:
                gap = x if prev_ref is None else x - prev_ref[q, pl.ds(PAD + r0, n), :]
                new += MOMENTUM[k] * gap
            store(q, r0, n, new)

    planes(lo, hi, each, unroll)


def into(ref):
    def store(q, r0, n, v):
        ref[q, pl.ds(PAD + r0, n), :] = v

    return store


def inverse(d):
    inside = d > 0.0
    return jnp.where(inside, 1.0 / jnp.where(inside, d, 1.0), 0.0)


def faces(alpha, x0, x1, y0, y1, z0, reach, scale):
    z1 = moved(z0, -reach)
    d = alpha + scale * (x0 + x1 + y0 + y1 + z0 + z1)
    inv = inverse(d)
    si = scale * inv
    return d, inv, [si * f for f in (x0, x1, y0, y1, z0, z1)]


def next_rows(load, r0, n, rows):
    if r0 + n < rows:
        return load(r0 + 1, n)
    return pltpu.roll(load(r0, n), n - 1, 0)


def clear_pads(ref, rows):
    ref[:, :PAD, :] = jnp.zeros((ref.shape[0], PAD, PZ), F32)
    ref[:, PAD + rows :, :] = jnp.zeros((ref.shape[0], PAD, PZ), F32)


def pair_lanes(v, reach):
    low = (lanes(v.shape[0]) & reach) == 0
    return v + jnp.where(low, moved(v, -reach), moved(v, reach))


def low_lanes(v, reach):
    low = (lanes(v.shape[0]) & reach) == 0
    return jnp.where(low, v, moved(v, reach))


def pack2(v0, v1):
    return jnp.where((lanes(v0.shape[0]) & 1) == 0, v0, v1)


def unpack2(v):
    even = (lanes(v.shape[0]) & 1) == 0
    return jnp.where(even, v, moved(v, 1)), jnp.where(even, moved(v, -1), v)


def pack4(items):
    place = lanes(items[0].shape[0]) & 3
    out = items[0]
    for i, item in enumerate(items[1:], 1):
        out = jnp.where(place == i, item, out)
    return out


def unpack4(v, i):
    place = lanes(v.shape[0]) & 3
    out = v
    for m in range(4):
        if m != i:
            out = jnp.where(place == m, moved(v, m - i), out)
    return out


def coarser(load, rows, reach):
    def cell(i):
        return load(i, 0, 0) + load(i, 0, 1) + load(i, 1, 0) + load(i, 1, 1)

    al = pair_lanes(cell(0), reach) * 0.125
    bx = pair_lanes(load(1, 0, 0) + load(1, 0, 1), reach) * 0.25
    by = pair_lanes(load(2, 0, 0) + load(2, 1, 0), reach) * 0.25
    bz = low_lanes(cell(3), reach) * 0.25
    return al, bx, by, bz


def pack_kernel(b, al, bx, by, bz, a, one_out, two_out, sems):
    wide, narrow = lax.axis_index("wide"), lax.axis_index("narrow")
    par = lax.rem(wide, 2)
    copies = [pltpu.make_async_copy(ref, a.at[i], sems.at[i]) for i, ref in enumerate((b, al, bx, by, bz))]
    for c in copies:
        c.start()
    for c in copies:
        c.wait()
    row = lax.broadcasted_iota(jnp.int32, (PAD, PZ), 0)
    first_row = jnp.logical_and(row == 0, jnp.broadcast_to(narrow, (PAD, PZ)) == 0)
    a[BX, 0] = jnp.where(jnp.broadcast_to(wide, (PY, PZ)) == 0, 0.0, a[BX, 0])
    first_z = lanes(PY) == 0
    for p in range(PX):
        a[BY, p, :PAD] = jnp.where(first_row, 0.0, a[BY, p, :PAD])
        a[BZ, p] = jnp.where(first_z, 0.0, a[BZ, p])
    for i in range(5):
        for p in range(PX):
            here = pl.ds((PX * i + p) * HY, HY)
            one_out[here, :] = a[i, p, pl.ds(pl.multiple_of((1 - par) * (PY - HY), 8), HY), :]
            two_out[here, :] = a[i, p, pl.ds(pl.multiple_of(par * (PY - HY), 8), HY), :]


def plane(ref, k, r0=0, n=EY):
    start = k * EY + r0
    return ref[pl.ds(pl.multiple_of(start, 8) if r0 % 8 == 0 else start, n), :]


def second_planes(get, rows, x, keep):
    clear_pads(x, rows)
    body = pl.ds(PAD, rows)
    kept = []
    for p in range(3):
        by = get(BY, p)
        _, inv, w = faces(
            get(ALPHA, p), get(BX, p), get(BX, p + 1), by, pltpu.roll(by, rows - 1, 0), get(BZ, p), 1, 1.0
        )
        c0 = inv * get(B, p)
        x[p, body, :] = c0 * (1.0 / THETA)
        kept.append((w, c0))
    for up in range(2):
        second = 1 + up
        w, c0 = kept[second]
        here = x[second, body, :]
        z = c0 - here + w[0] * x[second - 1, body, :]
        if not up:
            z += w[1] * x[2, body, :]
        z += w[2] * x[second, pl.ds(PAD - 1, rows), :] + w[3] * x[second, pl.ds(PAD + 1, rows), :]
        z += w[4] * moved(here, 1) + w[5] * moved(here, -1)
        keep(up, 0, here)
        keep(up, 1, here + GAIN[1] * z + MOMENTUM[1] * here)
        keep(up, 2, w[1] if up else get(BX, second))


def inner_kernel(a, ex, v, x):
    par = parity()

    def keep(up, k, value):
        v[up, pl.ds(INNER * k, INNER), :] = value[8 : 8 + INNER]

    second_planes(lambda i, p: a[i, p], PY, x, keep)
    for i in range(5):
        ex[pl.ds(i * PY, PY), :] = a[i, 3 * par]
    ex[pl.ds(EX_IN, 3 * INNER), :] = v[par]


def corner_kernel(a, one, two, inner, _, own, sw, xs, x, v):
    par = parity()
    for i in range(5):
        for p in range(PX):
            k = PX * i + p
            here = pl.ds(k * HY, HY)
            own[pl.ds(pl.multiple_of(k * EY + par * (HY + PY), 8), HY), :] = one[here, :]
            own[pl.ds(k * EY + HY, PY), :] = a[i, p]
            own[pl.ds(pl.multiple_of(k * EY + (1 - par) * (HY + PY), 8), HY), :] = two[here, :]
    got = []
    for c in range(2):

        def load(i, k, row):
            return own[pl.ds((PX * (i + 1) + 2 * c + k) * EY + row, R1, 2), :]

        got.append(coarser(load, R1, 1))
    for i in range(4):
        t = pack2(got[0][i], got[1][i])
        own[pl.ds(RAW + R1 * i, R1), :] = t
        sw[pl.ds(SRAW + R1 * i, R1), :] = t
    xs[pl.ds(XB, R1), :] = own[pl.ds(RAW + R1, R1), :]
    for i in range(5):
        xs[pl.ds(2 * HY * i, HY), :] = plane(own, PX * i + 3 * par, 0, HY)
        xs[pl.ds(2 * HY * i + HY, HY), :] = plane(own, PX * i + 3 * par, HY + PY, HY)
        sw[pl.ds(i * EY, EY), :] = plane(own, PX * i + 3 - 3 * par)
    span = EDGE + 8
    for side, r0 in ((0, 0), (1, EY - span)):

        def keep(up, k, value):
            v[up, pl.ds((2 * k + side) * EDGE, EDGE), :] = value[8 * side : 8 * side + EDGE]

        second_planes(lambda i, p: plane(own, PX * i + p, r0, span), span, x.at[side], keep)
    xs[pl.ds(XP, 6 * EDGE), :] = v[par]
    for k in range(3):
        base = (5 + k) * EY
        sw[pl.ds(base, EDGE), :] = v[1 - par, pl.ds(2 * k * EDGE, EDGE), :]
        sw[pl.ds(base + EDGE, INNER), :] = inner[1 - par, pl.ds(k * INNER, INNER), :]
        sw[pl.ds(base + EDGE + INNER, EDGE), :] = v[1 - par, pl.ds((2 * k + 1) * EDGE, EDGE), :]


Q0 = 3


def fine_kernel(own, sw, xs, ex, _, send, send1, send2, edge, pre, w, cc, sx, d, x, y, z, t, s, u, sf):
    par = parity()
    for i in range(5):
        sf[i, :HY] = xs[pl.ds(2 * HY * i, HY), :]
        sf[i, HY : HY + PY] = ex[pl.ds(PY * i, PY), :]
        sf[i, HY + PY :] = xs[pl.ds(2 * HY * i + HY, HY), :]

    for k in range(3):
        sf[5 + k, :EDGE] = xs[pl.ds(XP + 2 * k * EDGE, EDGE), :]
        sf[5 + k, EDGE : EDGE + INNER] = ex[pl.ds(EX_IN + k * INNER, INNER), :]
        sf[5 + k, EDGE + INNER :] = xs[pl.ds(XP + (2 * k + 1) * EDGE, EDGE), :]

    def far(i, r, n):
        return sf[i, pl.ds(r, n), :]

    def near(i, r, n):
        return plane(sw, i, r, n)

    sides2 = ((far, par), (near, 1 - par))
    for i in range(4):
        for p, ref, base in ((par, own, RAW), (1 - par, sw, SRAW)):
            v0, v1 = unpack2(ref[pl.ds(base + R1 * i, R1), :])
            s[i, 2 * p] = v0
            s[i, 2 * p + 1] = v1
    s[1, 4] = unpack2(xs[pl.ds(XB, R1), :])[0]
    for p in range(PX):
        sx[Q0 + p] = plane(own, PX * BX + p)
    for get, above in sides2:
        sx[2 + 5 * above] = get(BX, 0, EY)
        sx[9 - above] = get(7, 0, EY)
    clear_pads(x, EY)
    clear_pads(y, EY)
    chunk = 32

    def prepare(q, get):
        for r0 in range(0, EY, chunk):
            here = pl.ds(r0, chunk)

            def load(i):
                return lambda r, n: get(i, r, n)

            dd, inv, w6 = faces(
                load(ALPHA)(r0, chunk), sx[q, here, :], sx[q + 1, here, :], load(BY)(r0, chunk),
                next_rows(load(BY), r0, chunk, EY), load(BZ)(r0, chunk), 1, 1.0,
            )
            for a, f in enumerate(w6):
                w[a, q, here, :] = f
            c0 = inv * load(B)(r0, chunk)
            cc[q, here, :] = c0
            x[q, pl.ds(PAD + r0, chunk), :] = c0 * (1.0 / THETA)
            d[q, here, :] = dd

    for p in range(PX):
        prepare(Q0 + p, lambda i, r, n: plane(own, PX * i + p, r, n))
    body = pl.ds(PAD, EY)
    for get, above in sides2:
        q = 2 + 5 * above
        prepare(q, get)
        x[1 + 7 * above, body, :] = get(5, 0, EY)
        missing = GAIN[1] * get(7, 0, EY) * x[q, body, :]
        below = jnp.broadcast_to(above, missing.shape) == 0
        y[1 + 7 * above, body, :] = get(6, 0, EY) + jnp.where(below, missing, 0.0)

    rows = (0, EY)
    sweep(x, None, cc, w, 2, 8, rows, 1, 1, into(y), chunk)
    sweep(y, x, cc, w, 2, 8, rows, 1, 2, into(z), chunk)
    got = []
    for c in range(2):
        for r0 in range(0, EY, chunk):
            v = 0.0
            for q in (Q0 + 2 * c, Q0 + 2 * c + 1):
                _, zz = defect(z, cc, w, q, r0, chunk, 1, q, 0, q, 0)
                v = v + d[q, pl.ds(r0, chunk), :] * zz
            t[c, pl.ds(r0, chunk), :] = v
        got.append(pair_lanes(t[c, pl.ds(0, R1, 2), :] + t[c, pl.ds(1, R1, 2), :], 1) * 0.125)
    mid = pl.ds(PAD + MID0, MID)
    rhs = pack2(got[0], got[1])
    for out in (send, send1):
        out[:R1] = rhs
        out[pl.ds(R1, 4 * R1), :] = own[pl.ds(RAW, 4 * R1), :]
    edge[...] = z[Q0 + 2 - par, mid, :]
    send[pl.ds(5 * R1, MID), :] = z[Q0 + 1 + par, mid, :]
    q = 3 * par
    u[:R1] = s[2, q]
    u[R1:] = jnp.zeros((PAD, PZ), F32)
    _, inv, _ = faces(s[0, q], s[1, q], s[1, q + 1], u[:R1], u[pl.ds(1, R1), :], s[3, q], 2, 0.25)
    x1 = inv * jnp.where(jnp.broadcast_to(par, rhs.shape) == 0, *unpack2(rhs)) * (1.0 / THETA)
    send2[:R1] = pack2(x1, s[1, q])
    for c in range(2):

        def load(i, k, row):
            return s[i, 2 * c + k, pl.ds(row, R2, 2), :]

        send2[pl.ds(R1 + R2 * c, R2), :] = pack4(coarser(load, R2, 2))
    for p in range(6):
        pre[p] = z[Q0 - 1 + p, mid, :]


C0 = 5
N1 = 14
M0 = 5
S_SHAPE = (4, N1, R1 + 2 * PAD, PZ)
O_EDGE = R1
O_ONE = O_EDGE + MID
O_BESIDE = O_ONE + R1
O_TWO = O_BESIDE + R1
O_RAW = O_TWO + 2 * R1
O_END = O_RAW + 8 * R1


def place_coefficients(s, i, e, v):
    v0, v1 = unpack2(v)
    s[i, 1 + 2 * e, pl.ds(PAD, R1), :] = v0
    s[i, 2 + 2 * e, pl.ds(PAD, R1), :] = v1


def middle_faces(s, w1, inv1, d1, q):
    for r0 in range(0, R1, 32):
        here, up, out = pl.ds(PAD + r0, 32), pl.ds(PAD + r0 + 1, 32), pl.ds(r0, 32)
        dd, inv, w6 = faces(
            s[0, q, here, :], s[1, q, here, :], s[1, q + 1, here, :], s[2, q, here, :], s[2, q, up, :],
            s[3, q, here, :], 2, 0.25,
        )
        for a, f in enumerate(w6):
            w1[a, q, out, :] = f
        inv1[q, out, :] = inv
        d1[q, out, :] = dd


def sides(par, k):
    lower, upper = 1 - k, 4 + k
    return jnp.where(par == 0, lower, upper), jnp.where(par == 0, upper, lower)


def level2_load(s, plane):
    def load(i, k, row):
        return s[i, 2 * plane + C0 + k, pl.ds(PAD + row, R2, 2), :]

    return load


def near_coefficients_kernel(own, other, one, beside, s, w1, inv1, d1):
    par = parity()
    for i in range(4):
        s[i, :, PAD + R1 :, :] = jnp.zeros((N1, PAD, PZ), F32)
        rows = pl.ds(R1 * i, R1)
        sent = pl.ds(R1 * (1 + i), R1)
        place_coefficients(s, i, 2 + par, own[rows, :])
        place_coefficients(s, i, 3 - par, other[rows, :])
        place_coefficients(s, i, sides(par, 0)[0], one[sent, :])
        place_coefficients(s, i, sides(par, 1)[0], beside[sent, :])
    for k in range(7):
        middle_faces(s, w1, inv1, d1, 1 + 4 * par + k)


def join_kernel(own, edge, one, beside, two, out):
    out[:R1] = own[:R1]
    out[pl.ds(O_EDGE, MID), :] = edge[...]
    out[pl.ds(O_ONE, R1), :] = one[:R1]
    out[pl.ds(O_BESIDE, R1), :] = beside[:R1]
    out[pl.ds(O_TWO, 2 * R1), :] = two[...]
    out[pl.ds(O_RAW, 4 * R1), :] = one[pl.ds(R1, 4 * R1), :]
    out[pl.ds(O_RAW + 4 * R1, 4 * R1), :] = beside[pl.ds(R1, 4 * R1), :]


def tick_kernel(*refs):
    refs[-1][...] = jnp.zeros(refs[-1].shape, F32)


def first_to_arrive(*values):
    return call(tick_kernel, "tick", shape(PAD, PZ), VMEM, [ANY] * len(values), [], LARGE)(*values)


def both_sides(par, mine, its):
    upper = jnp.broadcast_to(par, mine.shape) == 1
    return jnp.where(upper, its, mine), jnp.where(upper, mine, its)


def middle_kernel(own, one, beside, two, its, s_in, w_in, inv_in, d_in, edge, cc, pre, rhs, s, w, inv, d,
                  x, y, z, t, u):
    par = parity()
    clear_pads(x, R1)
    clear_pads(y, R1)
    body = pl.ds(PAD, R1)
    lower, upper = both_sides(par, two[:R1], its[pl.ds(O_TWO, R1), :])
    x[0, body, :] = unpack2(lower)[0]
    x1, bx = unpack2(upper)
    x[N1 - 1, body, :] = x1
    s[1, N1 - 1, body, :] = bx
    for k in range(2):
        e = sides(par, k)[1]
        for i in range(4):
            place_coefficients(s, i, e, its[pl.ds(O_RAW + (4 * k + i) * R1, R1), :])
    for k in range(5):
        middle_faces(s, w, inv, d, jnp.where(par == 0, 8 + k, 1 + k if k < 4 else 12))

    def place(e, v):
        for k, b in enumerate(unpack2(v)):
            q = 1 + 2 * e + k
            c0 = inv[q] * b
            cc[q] = c0
            x[q, body, :] = c0 * (1.0 / THETA)

    place(2 + par, own[:R1])
    place(3 - par, its[:R1])
    for k, ref, row in ((0, one, O_ONE), (1, beside, O_BESIDE)):
        e, f = sides(par, k)
        place(e, ref[:R1])
        place(f, its[pl.ds(row, R1), :])

    rows = (0, R1)
    sweep(x, None, cc, w, 1, 13, rows, 2, 1, into(y), 32, unroll=12)
    sweep(y, x, cc, w, 2, 12, rows, 2, 2, into(z), 32, unroll=10)

    for c in range(4):
        for r0 in range(0, R1, 32):
            v = 0.0
            for k in range(2):
                q = C0 - 2 + 2 * c + k
                _, zz = defect(z, cc, w, q, r0, 32, 2, q, 0, q, 0)
                v = v + d[q, pl.ds(r0, 32), :] * zz
            t[c, pl.ds(r0, 32), :] = v
        rhs[c] = pair_lanes(t[c, pl.ds(0, R2, 2), :] + t[c, pl.ds(1, R2, 2), :], 2) * 0.125

    def first(k, plane):
        al, bx, by, bz = coarser(level2_load(s, plane), R2, 2)
        after = level2_load(s, plane + 1)
        bx1 = pair_lanes(after(1, 0, 0) + after(1, 0, 1), 2) * 0.25
        u[k, pl.ds(0, R2), :] = by
        u[k, pl.ds(R2, PAD), :] = jnp.zeros((PAD, PZ), F32)
        _, inv2, _ = faces(al, bx, bx1, by, u[k, pl.ds(1, R2), :], bz, 4, 0.0625)
        return inv2 * rhs[plane + 1] * (1.0 / THETA), bx

    below, above = first(0, -1), first(1, 2)
    up = pack4([rhs[3], rhs[2], rhs[1], below[0]])
    down = pack4([rhs[0], rhs[1], rhs[2], above[0]])
    wide = jnp.broadcast_to(lax.axis_index("wide"), up.shape)
    ends = (lanes(R2) & 3) == 0
    down = jnp.where(wide == 0, jnp.where(ends, rhs[1], 0.0), down)
    up = jnp.where(wide == lax.axis_size("wide") - 1, jnp.where(ends, rhs[2], 0.0), up)
    edge[:R2] = jnp.where(jnp.broadcast_to(par, up.shape) == 0, down, up)
    edge[R2:] = above[1]
    for p in range(10):
        pre[p] = z[C0 - 3 + p, body, :]


def coarse_coefficients_kernel(s, two, its, w2, inv2, last, s2):
    par = parity()
    for c in range(2, 8):
        for i, v in enumerate(coarser(level2_load(s, c - 4), R2, 2)):
            s2[i, c, pl.ds(0, R2), :] = v
    for k in range(2):
        rows = pl.ds(R1 + R2 * k, R2)
        lower, upper = both_sides(par, two[rows, :], its[pl.ds(O_TWO + R1 + R2 * k, R2), :])
        for i in range(4):
            s2[i, k, pl.ds(0, R2), :] = unpack4(lower, i)
            s2[i, 8 + k, pl.ds(0, R2), :] = unpack4(upper, i)
    s2[2, :, R2:, :] = jnp.zeros((10, PAD, PZ), F32)
    body = pl.ds(0, R2)
    for c in range(9):
        _, inv, w6 = faces(
            s2[0, c, body, :], s2[1, c, body, :], s2[1, c + 1, body, :], s2[2, c, body, :], s2[2, c, pl.ds(1, R2), :],
            s2[3, c, body, :], 4, 0.0625,
        )
        for a, f in enumerate(w6):
            w2[a, c + 1] = f
        inv2[c + 1] = inv
    for i in range(4):
        last[i] = s2[i, 9]


def last_kernel(two2, its2, rhs, w2, inv2, last, pre1, w1, c1, pre0, sw, xs, w0, c0, out,
                wx, c2, x2, y2, z2, x1, y1, z1, x0, y0):
    par = parity()
    body = pl.ds(PAD, R2)
    lo, hi = both_sides(par, two2[:R2], its2[:R2])
    _, beyond = both_sides(par, two2[R2:], its2[R2:])
    clear_pads(x2, R2)
    clear_pads(y2, R2)
    clear_pads(z2, R2)
    _, inv, w6 = faces(
        last[0, :R2], last[1, :R2], beyond, last[2, :R2], last[2, pl.ds(1, R2), :], last[3, :R2], 4, 0.0625
    )
    for a, f in enumerate(w6):
        wx[a, 0] = f

    def start(j, b, dinv):
        v = dinv * b
        c2[j] = v
        x2[j, body, :] = v * (1.0 / THETA)

    for k in range(3):
        start(3 - k, unpack4(lo, k), inv2[3 - k])
        start(8 + k, unpack4(hi, k), inv2[8 + k] if k < 2 else inv)
    for c in range(4):
        start(c + 4, rhs[c], inv2[c + 4])
    x2[0, body, :] = unpack4(lo, 3)
    x2[11, body, :] = unpack4(hi, 3)
    rows = (0, R2)
    sweep(x2, None, c2, w2, 1, 10, rows, 4, 1, into(y2), R2, unroll=9)
    sweep(x2, None, c2, wx, 10, 11, rows, 4, 1, into(y2), R2, woff=-10)
    sweep(y2, x2, c2, w2, 2, 10, rows, 4, 2, into(z2), R2, unroll=8)
    sweep(z2, y2, c2, w2, 3, 9, rows, 4, 3, into(x2), R2, unroll=6)

    for q in range(8):
        v = x2[(q - 3) // 2 + M0 + par, body, :]
        z1[q, pl.ds(PAD, R2, 2), :] = v
        z1[q, pl.ds(PAD + 1, R2, 2), :] = v
        x1[q, pl.ds(PAD, R1), :] = pre1[q + 2 * par] + z1[q, pl.ds(PAD, R1), :]
    rows = (8, R1 - 8)
    off = C0 - 3 + 2 * par
    sweep(x1, None, c1, w1, 1, 7, rows, 2, 0, into(y1), 24, woff=off, coff=off, unroll=6)
    sweep(y1, x1, c1, w1, 2, 6, rows, 2, 1, into(z1), 24, woff=off, coff=off, unroll=4)

    clear_pads(x0, MID)
    clear_pads(y0, MID)
    near, far = 7 - 7 * par, 7 * par
    body = pl.ds(PAD, MID)
    for q in range(8):
        v = z1[(q - 2) // 2 + 3, pl.ds(PAD + 12, MID // 2), :]
        x0[q, pl.ds(PAD, MID // 2, 2), :] = v
        x0[q, pl.ds(PAD + 1, MID // 2, 2), :] = v
        if 0 < q < 7:
            x0[q, body, :] += pre0[q - 1]
    x0[near, body, :] += sw[pl.ds(O_EDGE, MID), :]
    x0[far, body, :] += xs[pl.ds(5 * R1, MID), :]
    off = Q0 - 2
    sweep(x0, None, c0, w0, 1, 7, (0, MID), 1, 0, into(y0), 40, woff=off, coff=off, wr=MID0, cr=MID0, unroll=6)

    def finish(q, r0, n, v):
        out[q - 2, pl.ds(r0 - 8, n), :] = v

    sweep(y0, x0, c0, w0, 2, 6, (8, 8 + PY), 1, 1, finish, 32, woff=off, coff=off, wr=MID0, cr=MID0, unroll=4)


def swap(v):
    return lax.ppermute(v, "wide", [(i, i ^ 1) for i in range(lax.axis_size("wide"))])


def across(v, chips, ends=()):
    count = lax.axis_size("wide")
    step = 2 * chips - 1
    pairs = [(i, i + step) for i in range(1, count, 2) if i + step < count]
    pairs += [(i, i - step) for i in range(0, count, 2) if i - step >= 0]
    return lax.ppermute(v, "wide", pairs + list(ends))


def from_beside(v):
    count = lax.axis_size("wide")
    pairs = [(i, i + 2) for i in range(0, count - 2, 2)] + [(i, i - 2) for i in range(3, count, 2)]
    return lax.ppermute(v, "wide", pairs)


def along_narrow(v, step):
    wide, narrow = lax.axis_size("wide"), lax.axis_size("narrow")
    pairs = []
    for i in range(wide):
        to = step if i % 2 == 0 else -step
        pairs += [(i * narrow + j, i * narrow + j + to) for j in range(narrow) if 0 <= j + to < narrow]
    return lax.ppermute(v, ("wide", "narrow"), pairs)


def shards(right_side, alpha_coef, beta_x, beta_y, beta_z):
    a, y1, y2 = call(
        pack_kernel, "pack", (shape(5, PX, PY, PZ), shape(5 * PX * HY, PZ), shape(5 * PX * HY, PZ)),
        (VMEM,) * 3, [ANY] * 5, [pltpu.SemaphoreType.DMA((5,))], SMALL,
    )(*[pltpu.with_memory_space_constraint(v, pltpu.HBM) for v in (right_side, alpha_coef, beta_x, beta_y, beta_z)])
    y1, y2 = along_narrow(y1, 1), along_narrow(y2, -1)
    ex, inner = call(
        inner_kernel, "inner_rows", (shape(EX_IN + 3 * INNER, PZ), shape(2, 3 * INNER, PZ)), (VMEM,) * 2, [VMEM],
        [scratch(3, PY + 2 * PAD, PZ)], LARGE,
    )(a)
    ex = across(ex, 1)
    own, sw, xs = call(
        corner_kernel, "corners", (shape(RAW + 4 * R1, PZ), shape(SRAW + 4 * R1, PZ), shape(XB + R1, PZ)),
        (VMEM,) * 3, [VMEM] * 4 + [ANY], [scratch(2, 3, EDGE + 8 + 2 * PAD, PZ), scratch(2, 6 * EDGE, PZ)], SMALL,
    )(a, y1, y2, inner, first_to_arrive(y1, y2))
    xs = across(xs, 1)
    sw = swap(sw)

    send, send1, send2, edge0, pre0, w0, c0 = call(
        fine_kernel, "level0_pre",
        (shape(5 * R1 + MID, PZ), shape(5 * R1, PZ), shape(2 * R1, PZ), shape(MID, PZ), shape(6, MID, PZ),
         shape(6, 10, EY, PZ), shape(10, EY, PZ)),
        (VMEM,) * 7, [VMEM] * 4 + [ANY],
        [scratch(10, EY, PZ), scratch(10, EY, PZ)] + [scratch(10, EY + 2 * PAD, PZ)] * 3
        + [scratch(2, EY, PZ), scratch(4, 5, R1, PZ), scratch(R1 + PAD, PZ), scratch(8, EY, PZ)],
        LARGE,
    )(own, sw, xs, ex, first_to_arrive(xs, first_to_arrive(ex)))

    one = across(send, 1)
    beside = from_beside(send1)
    two = across(send2, 2)
    mine = call(join_kernel, "join", shape(O_END, PZ), VMEM, [VMEM] * 5, [], SMALL)(send, edge0, one, beside, two)
    its = swap(mine)
    w1_shapes = (shape(*S_SHAPE), shape(6, N1, R1, PZ), shape(N1, R1, PZ), shape(N1, R1, PZ))
    s1, w1, inv1, d1 = call(
        near_coefficients_kernel, "near_coefficients", w1_shapes, (VMEM,) * 4, [VMEM] * 4, [], LARGE,
    )(own[RAW:], sw[SRAW:], one, beside)

    edge, c1, pre1, rhs2, s1, w1, _, _ = call(
        middle_kernel, "level1_pre",
        (shape(2 * R2, PZ), shape(N1, R1, PZ), shape(10, R1, PZ), shape(4, R2, PZ)) + w1_shapes,
        (VMEM,) * 8, [VMEM] * 9,
        [scratch(N1, R1 + 2 * PAD, PZ)] * 3 + [scratch(4, R1, PZ), scratch(2, R2 + PAD, PZ)],
        LARGE, aliases={5: 4, 6: 5, 7: 6, 8: 7},
    )(send, one, beside, two, its, s1, w1, inv1, d1)

    w2, inv2, last2 = call(
        coarse_coefficients_kernel, "level2_coefficients",
        (shape(6, 12, R2, PZ), shape(12, R2, PZ), shape(4, R2 + PAD, PZ)),
        (VMEM,) * 3, [VMEM] * 3, [scratch(4, 10, R2 + PAD, PZ)], LARGE,
    )(s1, two, its)
    count = lax.axis_size("wide")
    two2 = across(edge, 2, ((0, 2), (count - 1, count - 3)))
    its2 = swap(two2)
    return call(
        last_kernel, "coarse_and_post", shape(PX, PY, PZ), VMEM, [VMEM] * 14,
        [scratch(6, 1, R2, PZ), scratch(12, R2, PZ)] + [scratch(12, R2 + 2 * PAD, PZ)] * 3
        + [scratch(8, R1 + 2 * PAD, PZ)] * 3 + [scratch(8, MID + 2 * PAD, PZ)] * 2,
        LARGE,
    )(two2, its2, rhs2, w2, inv2, last2, pre1, w1, c1, pre0, its, one, w0, c0)


def solution(mesh):
    spec = P("wide", "narrow", None)
    return jax.shard_map(shards, mesh=mesh, in_specs=(spec,) * 5, out_specs=spec, check_vma=False)
```

```python
import jax
import jax.numpy as jnp
from jax import lax
from jax.experimental import pallas as pl
from jax.experimental.pallas import tpu as pltpu
from jax.sharding import PartitionSpec as P

F32 = jnp.float32
THETA = (2.0 + 0.25) / 2.0
DELTA = (2.0 - 0.25) / 2.0
SIGMA = THETA / DELTA
RHO = [1.0 / SIGMA]
for _step in range(3):
    RHO.append(1.0 / (2.0 * SIGMA - RHO[-1]))
MOMENTUM = [0.0] + [RHO[k] * RHO[k - 1] for k in range(1, 4)]
GAIN = [1.0 / THETA] + [2.0 * RHO[k] / DELTA for k in range(1, 4)]

PX, PY, PZ = 4, 64, 128
HY = 32
EY = PY + 2 * HY
MID = PY + 16
MID0 = HY - 8
R1 = EY // 2
R2 = R1 // 2
RAW = 5 * PX * EY
SRAW = 8 * EY
XP = 5 * 2 * HY
INNER, EDGE = PY - 16, HY + 8
XB = XP + 3 * 2 * EDGE
EX_IN = 5 * PY
H1 = PY // 2
G1 = (R1 - H1) // 2
PAD = 8
SMALL, LARGE = 1000, 2 * 10**10
B, ALPHA, BX, BY, BZ = range(5)
ANY = pl.BlockSpec(memory_space=pl.ANY)
VMEM = pl.BlockSpec(memory_space=pltpu.VMEM)
HBM = pl.BlockSpec(memory_space=pltpu.HBM)


def shape(*dims):
    return jax.ShapeDtypeStruct(dims, F32)


def scratch(*dims):
    return pltpu.VMEM(dims, F32)


def call(kernel, name, out_shape, out_specs, in_specs, scratch_shapes, flops, mib=24, aliases=None):
    return pl.pallas_call(
        kernel,
        out_shape=out_shape,
        in_specs=in_specs,
        out_specs=out_specs,
        scratch_shapes=scratch_shapes,
        compiler_params=pltpu.CompilerParams(vmem_limit_bytes=mib * 1024 * 1024),
        cost_estimate=pl.CostEstimate(flops=flops, bytes_accessed=0, transcendentals=0),
        input_output_aliases=aliases or {},
        name=name,
    )


def parity():
    return lax.rem(lax.axis_index("wide"), 2)


def lanes(rows):
    return lax.broadcasted_iota(jnp.int32, (rows, PZ), 1)


def moved(v, shift):
    return pltpu.roll(v, shift % PZ, 1)


def planes(lo, hi, each, unroll):
    if not unroll:
        each(lo)
        return
    steps = (hi - lo) // unroll

    def body(i, carry):
        for k in range(unroll):
            each(lo + i * unroll + k)
        return carry

    if steps > 1:
        lax.fori_loop(0, steps, body, 0)
    else:
        steps = 0
    for q in range(lo + steps * unroll, hi):
        each(q)


def defect(x_ref, c_ref, w_ref, q, r0, n, reach, cq, cr, wq, wr):
    rows = pl.ds(PAD + r0, n)
    here = pl.ds(wr + r0, n)
    x = x_ref[q, rows, :]
    total = c_ref[cq, pl.ds(cr + r0, n), :] - x
    total += w_ref[0, wq, here, :] * x_ref[q - 1, rows, :]
    total += w_ref[1, wq, here, :] * x_ref[q + 1, rows, :]
    total += w_ref[2, wq, here, :] * x_ref[q, pl.ds(PAD + r0 - 1, n), :]
    total += w_ref[3, wq, here, :] * x_ref[q, pl.ds(PAD + r0 + 1, n), :]
    total += w_ref[4, wq, here, :] * moved(x, reach)
    total += w_ref[5, wq, here, :] * moved(x, -reach)
    return x, total


def sweep(x_ref, prev_ref, c_ref, w_ref, lo, hi, rows, reach, k, store, chunk, woff=0, coff=0, wr=0, cr=0, unroll=8):
    def each(q):
        for r0 in range(rows[0], rows[1], chunk):
            n = min(chunk, rows[1] - r0)
            x, z = defect(x_ref, c_ref, w_ref, q, r0, n, reach, q + coff, cr, q + woff, wr)
            new = x + GAIN[k] * z
            if k > 0:
                gap = x if prev_ref is None else x - prev_ref[q, pl.ds(PAD + r0, n), :]
                new += MOMENTUM[k] * gap
            store(q, r0, n, new)

    planes(lo, hi, each, unroll)


def into(ref):
    def store(q, r0, n, v):
        ref[q, pl.ds(PAD + r0, n), :] = v

    return store


def inverse(d):
    inside = d > 0.0
    return jnp.where(inside, 1.0 / jnp.where(inside, d, 1.0), 0.0)


def faces(alpha, x0, x1, y0, y1, z0, reach, scale):
    z1 = moved(z0, -reach)
    d = alpha + scale * (x0 + x1 + y0 + y1 + z0 + z1)
    inv = inverse(d)
    si = scale * inv
    return d, inv, [si * f for f in (x0, x1, y0, y1, z0, z1)]


def next_rows(load, r0, n, rows):
    if r0 + n < rows:
        return load(r0 + 1, n)
    return pltpu.roll(load(r0, n), n - 1, 0)


def clear_pads(ref, rows):
    ref[:, :PAD, :] = jnp.zeros((ref.shape[0], PAD, PZ), F32)
    ref[:, PAD + rows :, :] = jnp.zeros((ref.shape[0], PAD, PZ), F32)


def pair_lanes(v, reach):
    low = (lanes(v.shape[0]) & reach) == 0
    return v + jnp.where(low, moved(v, -reach), moved(v, reach))


def low_lanes(v, reach):
    low = (lanes(v.shape[0]) & reach) == 0
    return jnp.where(low, v, moved(v, reach))


def pack2(v0, v1):
    return jnp.where((lanes(v0.shape[0]) & 1) == 0, v0, v1)


def unpack2(v):
    even = (lanes(v.shape[0]) & 1) == 0
    return jnp.where(even, v, moved(v, 1)), jnp.where(even, moved(v, -1), v)


def pack4(items):
    place = lanes(items[0].shape[0]) & 3
    out = items[0]
    for i, item in enumerate(items[1:], 1):
        out = jnp.where(place == i, item, out)
    return out


def unpack4(v, i):
    place = lanes(v.shape[0]) & 3
    out = v
    for m in range(4):
        if m != i:
            out = jnp.where(place == m, moved(v, m - i), out)
    return out


def coarser(load, rows, reach):
    def cell(i):
        return load(i, 0, 0) + load(i, 0, 1) + load(i, 1, 0) + load(i, 1, 1)

    al = pair_lanes(cell(0), reach) * 0.125
    bx = pair_lanes(load(1, 0, 0) + load(1, 0, 1), reach) * 0.25
    by = pair_lanes(load(2, 0, 0) + load(2, 1, 0), reach) * 0.25
    bz = low_lanes(cell(3), reach) * 0.25
    return al, bx, by, bz


def pack_kernel(b, al, bx, by, bz, a, one_out, two_out, sems):
    wide, narrow = lax.axis_index("wide"), lax.axis_index("narrow")
    par = lax.rem(wide, 2)
    copies = [pltpu.make_async_copy(ref, a.at[i], sems.at[i]) for i, ref in enumerate((b, al, bx, by, bz))]
    for c in copies:
        c.start()
    for c in copies:
        c.wait()
    row = lax.broadcasted_iota(jnp.int32, (PAD, PZ), 0)
    first_row = jnp.logical_and(row == 0, jnp.broadcast_to(narrow, (PAD, PZ)) == 0)
    a[BX, 0] = jnp.where(jnp.broadcast_to(wide, (PY, PZ)) == 0, 0.0, a[BX, 0])
    first_z = lanes(PY) == 0
    for p in range(PX):
        a[BY, p, :PAD] = jnp.where(first_row, 0.0, a[BY, p, :PAD])
        a[BZ, p] = jnp.where(first_z, 0.0, a[BZ, p])
    for i in range(5):
        for p in range(PX):
            here = pl.ds((PX * i + p) * HY, HY)
            one_out[here, :] = a[i, p, pl.ds(pl.multiple_of((1 - par) * (PY - HY), 8), HY), :]
            two_out[here, :] = a[i, p, pl.ds(pl.multiple_of(par * (PY - HY), 8), HY), :]


def plane(ref, k, r0=0, n=EY):
    start = k * EY + r0
    return ref[pl.ds(pl.multiple_of(start, 8) if r0 % 8 == 0 else start, n), :]


def second_planes(get, rows, x, keep):
    clear_pads(x, rows)
    body = pl.ds(PAD, rows)
    kept = []
    for p in range(3):
        by = get(BY, p)
        _, inv, w = faces(
            get(ALPHA, p), get(BX, p), get(BX, p + 1), by, pltpu.roll(by, rows - 1, 0), get(BZ, p), 1, 1.0
        )
        c0 = inv * get(B, p)
        x[p, body, :] = c0 * (1.0 / THETA)
        kept.append((w, c0))
    for up in range(2):
        second = 1 + up
        w, c0 = kept[second]
        here = x[second, body, :]
        z = c0 - here + w[0] * x[second - 1, body, :]
        if not up:
            z += w[1] * x[2, body, :]
        z += w[2] * x[second, pl.ds(PAD - 1, rows), :] + w[3] * x[second, pl.ds(PAD + 1, rows), :]
        z += w[4] * moved(here, 1) + w[5] * moved(here, -1)
        keep(up, 0, here)
        keep(up, 1, here + GAIN[1] * z + MOMENTUM[1] * here)
        keep(up, 2, w[1] if up else get(BX, second))


def inner_kernel(a, ex, v, own, x):
    par = parity()

    def keep(up, k, value):
        v[up, pl.ds(INNER * k, INNER), :] = value[8 : 8 + INNER]

    second_planes(lambda i, p: a[i, p], PY, x, keep)
    for i in range(5):
        ex[pl.ds(i * PY, PY), :] = a[i, 3 * par]
    ex[pl.ds(EX_IN, 3 * INNER), :] = v[par]
    for i in range(5):
        for p in range(PX):
            own[pl.ds((PX * i + p) * EY + HY, PY), :] = a[i, p]
    got = []
    for c in range(2):

        def load(i, k, row):
            return a[i + 1, 2 * c + k, pl.ds(row, H1, 2), :]

        got.append(coarser(load, H1, 1))
    for i in range(4):
        own[pl.ds(RAW + R1 * i + G1, H1), :] = pack2(got[0][i], got[1][i])


def corner_kernel(own_in, one, two, inner, _, own, sw, xs, x, v):
    par = parity()
    for i in range(5):
        for p in range(PX):
            k = PX * i + p
            here = pl.ds(k * HY, HY)
            own[pl.ds(pl.multiple_of(k * EY + par * (HY + PY), 8), HY), :] = one[here, :]
            own[pl.ds(pl.multiple_of(k * EY + (1 - par) * (HY + PY), 8), HY), :] = two[here, :]
    for r0, r1 in ((0, 0), (HY + PY, G1 + H1)):
        got = []
        for c in range(2):

            def load(i, k, row):
                return own[pl.ds((PX * (i + 1) + 2 * c + k) * EY + r0 + row, G1, 2), :]

            got.append(coarser(load, G1, 1))
        for i in range(4):
            own[pl.ds(RAW + R1 * i + r1, G1), :] = pack2(got[0][i], got[1][i])
    sw[pl.ds(SRAW, 4 * R1), :] = own[pl.ds(RAW, 4 * R1), :]
    xs[pl.ds(XB, R1), :] = own[pl.ds(RAW + R1, R1), :]
    for i in range(5):
        xs[pl.ds(2 * HY * i, HY), :] = plane(own, PX * i + 3 * par, 0, HY)
        xs[pl.ds(2 * HY * i + HY, HY), :] = plane(own, PX * i + 3 * par, HY + PY, HY)
        sw[pl.ds(i * EY, EY), :] = plane(own, PX * i + 3 - 3 * par)
    span = EDGE + 8
    for side, r0 in ((0, 0), (1, EY - span)):

        def keep(up, k, value):
            v[up, pl.ds((2 * k + side) * EDGE, EDGE), :] = value[8 * side : 8 * side + EDGE]

        second_planes(lambda i, p: plane(own, PX * i + p, r0, span), span, x.at[side], keep)
    xs[pl.ds(XP, 6 * EDGE), :] = v[par]
    for k in range(3):
        base = (5 + k) * EY
        sw[pl.ds(base, EDGE), :] = v[1 - par, pl.ds(2 * k * EDGE, EDGE), :]
        sw[pl.ds(base + EDGE, INNER), :] = inner[1 - par, pl.ds(k * INNER, INNER), :]
        sw[pl.ds(base + EDGE + INNER, EDGE), :] = v[1 - par, pl.ds((2 * k + 1) * EDGE, EDGE), :]


Q0 = 3


def fine_kernel(own, sw, xs, ex, _, send, send1, send2, edge, pre, w, cc, sx, d, x, y, z, t, s, u, sf):
    par = parity()
    for i in range(5):
        sf[i, :HY] = xs[pl.ds(2 * HY * i, HY), :]
        sf[i, HY : HY + PY] = ex[pl.ds(PY * i, PY), :]
        sf[i, HY + PY :] = xs[pl.ds(2 * HY * i + HY, HY), :]

    for k in range(3):
        sf[5 + k, :EDGE] = xs[pl.ds(XP + 2 * k * EDGE, EDGE), :]
        sf[5 + k, EDGE : EDGE + INNER] = ex[pl.ds(EX_IN + k * INNER, INNER), :]
        sf[5 + k, EDGE + INNER :] = xs[pl.ds(XP + (2 * k + 1) * EDGE, EDGE), :]

    def far(i, r, n):
        return sf[i, pl.ds(r, n), :]

    def near(i, r, n):
        return plane(sw, i, r, n)

    sides2 = ((far, par), (near, 1 - par))
    for i in range(4):
        for p, ref, base in ((par, own, RAW), (1 - par, sw, SRAW)):
            v0, v1 = unpack2(ref[pl.ds(base + R1 * i, R1), :])
            s[i, 2 * p] = v0
            s[i, 2 * p + 1] = v1
    s[1, 4] = unpack2(xs[pl.ds(XB, R1), :])[0]
    for p in range(PX):
        sx[Q0 + p] = plane(own, PX * BX + p)
    for get, above in sides2:
        sx[2 + 5 * above] = get(BX, 0, EY)
        sx[9 - above] = get(7, 0, EY)
    clear_pads(x, EY)
    clear_pads(y, EY)
    chunk = 32

    def prepare(q, get):
        for r0 in range(0, EY, chunk):
            here = pl.ds(r0, chunk)

            def load(i):
                return lambda r, n: get(i, r, n)

            dd, inv, w6 = faces(
                load(ALPHA)(r0, chunk), sx[q, here, :], sx[q + 1, here, :], load(BY)(r0, chunk),
                next_rows(load(BY), r0, chunk, EY), load(BZ)(r0, chunk), 1, 1.0,
            )
            for a, f in enumerate(w6):
                w[a, q, here, :] = f
            c0 = inv * load(B)(r0, chunk)
            cc[q, here, :] = c0
            x[q, pl.ds(PAD + r0, chunk), :] = c0 * (1.0 / THETA)
            d[q, here, :] = dd

    for p in range(PX):
        prepare(Q0 + p, lambda i, r, n: plane(own, PX * i + p, r, n))
    body = pl.ds(PAD, EY)
    for get, above in sides2:
        q = 2 + 5 * above
        prepare(q, get)
        x[1 + 7 * above, body, :] = get(5, 0, EY)
        missing = GAIN[1] * get(7, 0, EY) * x[q, body, :]
        below = jnp.broadcast_to(above, missing.shape) == 0
        y[1 + 7 * above, body, :] = get(6, 0, EY) + jnp.where(below, missing, 0.0)

    rows = (0, EY)
    sweep(x, None, cc, w, 2, 8, rows, 1, 1, into(y), chunk)
    sweep(y, x, cc, w, 2, 8, rows, 1, 2, into(z), chunk)
    got = []
    for c in range(2):
        for r0 in range(0, EY, chunk):
            v = 0.0
            for q in (Q0 + 2 * c, Q0 + 2 * c + 1):
                _, zz = defect(z, cc, w, q, r0, chunk, 1, q, 0, q, 0)
                v = v + d[q, pl.ds(r0, chunk), :] * zz
            t[c, pl.ds(r0, chunk), :] = v
        got.append(pair_lanes(t[c, pl.ds(0, R1, 2), :] + t[c, pl.ds(1, R1, 2), :], 1) * 0.125)
    mid = pl.ds(PAD + MID0, MID)
    rhs = pack2(got[0], got[1])
    for out in (send, send1):
        out[:R1] = rhs
        out[pl.ds(R1, 4 * R1), :] = own[pl.ds(RAW, 4 * R1), :]
    edge[...] = z[Q0 + 2 - par, mid, :]
    send[pl.ds(5 * R1, MID), :] = z[Q0 + 1 + par, mid, :]
    q = 3 * par
    u[:R1] = s[2, q]
    u[R1:] = jnp.zeros((PAD, PZ), F32)
    _, inv, _ = faces(s[0, q], s[1, q], s[1, q + 1], u[:R1], u[pl.ds(1, R1), :], s[3, q], 2, 0.25)
    x1 = inv * jnp.where(jnp.broadcast_to(par, rhs.shape) == 0, *unpack2(rhs)) * (1.0 / THETA)
    send2[:R1] = pack2(x1, s[1, q])
    for c in range(2):

        def load(i, k, row):
            return s[i, 2 * c + k, pl.ds(row, R2, 2), :]

        send2[pl.ds(R1 + R2 * c, R2), :] = pack4(coarser(load, R2, 2))
    for p in range(6):
        pre[p] = z[Q0 - 1 + p, mid, :]


C0 = 5
N1 = 14
M0 = 5
S_SHAPE = (4, N1, R1 + 2 * PAD, PZ)
O_EDGE = R1
O_ONE = O_EDGE + MID
O_BESIDE = O_ONE + R1
O_TWO = O_BESIDE + R1
O_RAW = O_TWO + 2 * R1
O_END = O_RAW + 8 * R1


def place_coefficients(s, i, e, v):
    v0, v1 = unpack2(v)
    s[i, 1 + 2 * e, pl.ds(PAD, R1), :] = v0
    s[i, 2 + 2 * e, pl.ds(PAD, R1), :] = v1


def middle_faces(s, w1, inv1, d1, q):
    for r0 in range(0, R1, 32):
        here, up, out = pl.ds(PAD + r0, 32), pl.ds(PAD + r0 + 1, 32), pl.ds(r0, 32)
        dd, inv, w6 = faces(
            s[0, q, here, :], s[1, q, here, :], s[1, q + 1, here, :], s[2, q, here, :], s[2, q, up, :],
            s[3, q, here, :], 2, 0.25,
        )
        for a, f in enumerate(w6):
            w1[a, q, out, :] = f
        inv1[q, out, :] = inv
        d1[q, out, :] = dd


def sides(par, k):
    lower, upper = 1 - k, 4 + k
    return jnp.where(par == 0, lower, upper), jnp.where(par == 0, upper, lower)


def level2_load(s, plane):
    def load(i, k, row):
        return s[i, 2 * plane + C0 + k, pl.ds(PAD + row, R2, 2), :]

    return load


def near_coefficients_kernel(own, other, one, beside, s, w1, inv1, d1):
    par = parity()
    for i in range(4):
        s[i, :, PAD + R1 :, :] = jnp.zeros((N1, PAD, PZ), F32)
        rows = pl.ds(R1 * i, R1)
        sent = pl.ds(R1 * (1 + i), R1)
        place_coefficients(s, i, 2 + par, own[rows, :])
        place_coefficients(s, i, 3 - par, other[rows, :])
        place_coefficients(s, i, sides(par, 0)[0], one[sent, :])
        place_coefficients(s, i, sides(par, 1)[0], beside[sent, :])
    for k in range(7):
        middle_faces(s, w1, inv1, d1, 1 + 4 * par + k)


def join_kernel(own, edge, one, beside, two, out):
    out[:R1] = own[:R1]
    out[pl.ds(O_EDGE, MID), :] = edge[...]
    out[pl.ds(O_ONE, R1), :] = one[:R1]
    out[pl.ds(O_BESIDE, R1), :] = beside[:R1]
    out[pl.ds(O_TWO, 2 * R1), :] = two[...]
    out[pl.ds(O_RAW, 4 * R1), :] = one[pl.ds(R1, 4 * R1), :]
    out[pl.ds(O_RAW + 4 * R1, 4 * R1), :] = beside[pl.ds(R1, 4 * R1), :]


def tick_kernel(*refs):
    refs[-1][...] = jnp.zeros(refs[-1].shape, F32)


def first_to_arrive(*values):
    return call(tick_kernel, "tick", shape(PAD, PZ), VMEM, [ANY] * len(values), [], LARGE)(*values)


def both_sides(par, mine, its):
    upper = jnp.broadcast_to(par, mine.shape) == 1
    return jnp.where(upper, its, mine), jnp.where(upper, mine, its)


def middle_kernel(own, one, beside, two, its, s_in, w_in, inv_in, d_in, edge, cc, pre, rhs, s, w, inv, d,
                  x, y, z, t, u):
    par = parity()
    clear_pads(x, R1)
    clear_pads(y, R1)
    body = pl.ds(PAD, R1)
    lower, upper = both_sides(par, two[:R1], its[pl.ds(O_TWO, R1), :])
    x[0, body, :] = unpack2(lower)[0]
    x1, bx = unpack2(upper)
    x[N1 - 1, body, :] = x1
    s[1, N1 - 1, body, :] = bx
    for k in range(2):
        e = sides(par, k)[1]
        for i in range(4):
            place_coefficients(s, i, e, its[pl.ds(O_RAW + (4 * k + i) * R1, R1), :])
    for k in range(5):
        middle_faces(s, w, inv, d, jnp.where(par == 0, 8 + k, 1 + k if k < 4 else 12))

    def place(e, v):
        for k, b in enumerate(unpack2(v)):
            q = 1 + 2 * e + k
            c0 = inv[q] * b
            cc[q] = c0
            x[q, body, :] = c0 * (1.0 / THETA)

    place(2 + par, own[:R1])
    place(3 - par, its[:R1])
    for k, ref, row in ((0, one, O_ONE), (1, beside, O_BESIDE)):
        e, f = sides(par, k)
        place(e, ref[:R1])
        place(f, its[pl.ds(row, R1), :])

    rows = (0, R1)
    sweep(x, None, cc, w, 1, 13, rows, 2, 1, into(y), 32, unroll=12)
    sweep(y, x, cc, w, 2, 12, rows, 2, 2, into(z), 32, unroll=10)

    for c in range(4):
        for r0 in range(0, R1, 32):
            v = 0.0
            for k in range(2):
                q = C0 - 2 + 2 * c + k
                _, zz = defect(z, cc, w, q, r0, 32, 2, q, 0, q, 0)
                v = v + d[q, pl.ds(r0, 32), :] * zz
            t[c, pl.ds(r0, 32), :] = v
        rhs[c] = pair_lanes(t[c, pl.ds(0, R2, 2), :] + t[c, pl.ds(1, R2, 2), :], 2) * 0.125

    def first(k, plane):
        al, bx, by, bz = coarser(level2_load(s, plane), R2, 2)
        after = level2_load(s, plane + 1)
        bx1 = pair_lanes(after(1, 0, 0) + after(1, 0, 1), 2) * 0.25
        u[k, pl.ds(0, R2), :] = by
        u[k, pl.ds(R2, PAD), :] = jnp.zeros((PAD, PZ), F32)
        _, inv2, _ = faces(al, bx, bx1, by, u[k, pl.ds(1, R2), :], bz, 4, 0.0625)
        return inv2 * rhs[plane + 1] * (1.0 / THETA), bx

    below, above = first(0, -1), first(1, 2)
    up = pack4([rhs[3], rhs[2], rhs[1], below[0]])
    down = pack4([rhs[0], rhs[1], rhs[2], above[0]])
    wide = jnp.broadcast_to(lax.axis_index("wide"), up.shape)
    ends = (lanes(R2) & 3) == 0
    down = jnp.where(wide == 0, jnp.where(ends, rhs[1], 0.0), down)
    up = jnp.where(wide == lax.axis_size("wide") - 1, jnp.where(ends, rhs[2], 0.0), up)
    edge[:R2] = jnp.where(jnp.broadcast_to(par, up.shape) == 0, down, up)
    edge[R2:] = above[1]
    for p in range(10):
        pre[p] = z[C0 - 3 + p, body, :]


def coarse_coefficients_kernel(s, two, its, w2, inv2, last, s2):
    par = parity()
    for c in range(2, 8):
        for i, v in enumerate(coarser(level2_load(s, c - 4), R2, 2)):
            s2[i, c, pl.ds(0, R2), :] = v
    for k in range(2):
        rows = pl.ds(R1 + R2 * k, R2)
        lower, upper = both_sides(par, two[rows, :], its[pl.ds(O_TWO + R1 + R2 * k, R2), :])
        for i in range(4):
            s2[i, k, pl.ds(0, R2), :] = unpack4(lower, i)
            s2[i, 8 + k, pl.ds(0, R2), :] = unpack4(upper, i)
    s2[2, :, R2:, :] = jnp.zeros((10, PAD, PZ), F32)
    body = pl.ds(0, R2)
    for c in range(9):
        _, inv, w6 = faces(
            s2[0, c, body, :], s2[1, c, body, :], s2[1, c + 1, body, :], s2[2, c, body, :], s2[2, c, pl.ds(1, R2), :],
            s2[3, c, body, :], 4, 0.0625,
        )
        for a, f in enumerate(w6):
            w2[a, c + 1] = f
        inv2[c + 1] = inv
    for i in range(4):
        last[i] = s2[i, 9]


def last_kernel(two2, its2, rhs, w2, inv2, last, pre1, w1, c1, pre0, sw, xs, w0, c0, out,
                wx, c2, x2, y2, z2, x1, y1, z1, x0, y0):
    par = parity()
    body = pl.ds(PAD, R2)
    lo, hi = both_sides(par, two2[:R2], its2[:R2])
    _, beyond = both_sides(par, two2[R2:], its2[R2:])
    clear_pads(x2, R2)
    clear_pads(y2, R2)
    clear_pads(z2, R2)
    _, inv, w6 = faces(
        last[0, :R2], last[1, :R2], beyond, last[2, :R2], last[2, pl.ds(1, R2), :], last[3, :R2], 4, 0.0625
    )
    for a, f in enumerate(w6):
        wx[a, 0] = f

    def start(j, b, dinv):
        v = dinv * b
        c2[j] = v
        x2[j, body, :] = v * (1.0 / THETA)

    for k in range(3):
        start(3 - k, unpack4(lo, k), inv2[3 - k])
        start(8 + k, unpack4(hi, k), inv2[8 + k] if k < 2 else inv)
    for c in range(4):
        start(c + 4, rhs[c], inv2[c + 4])
    x2[0, body, :] = unpack4(lo, 3)
    x2[11, body, :] = unpack4(hi, 3)
    rows = (0, R2)
    sweep(x2, None, c2, w2, 1, 10, rows, 4, 1, into(y2), R2, unroll=9)
    sweep(x2, None, c2, wx, 10, 11, rows, 4, 1, into(y2), R2, woff=-10)
    sweep(y2, x2, c2, w2, 2, 10, rows, 4, 2, into(z2), R2, unroll=8)
    sweep(z2, y2, c2, w2, 3, 9, rows, 4, 3, into(x2), R2, unroll=6)

    for q in range(8):
        v = x2[(q - 3) // 2 + M0 + par, body, :]
        z1[q, pl.ds(PAD, R2, 2), :] = v
        z1[q, pl.ds(PAD + 1, R2, 2), :] = v
        x1[q, pl.ds(PAD, R1), :] = pre1[q + 2 * par] + z1[q, pl.ds(PAD, R1), :]
    rows = (8, R1 - 8)
    off = C0 - 3 + 2 * par
    sweep(x1, None, c1, w1, 1, 7, rows, 2, 0, into(y1), 24, woff=off, coff=off, unroll=6)
    sweep(y1, x1, c1, w1, 2, 6, rows, 2, 1, into(z1), 24, woff=off, coff=off, unroll=4)

    clear_pads(x0, MID)
    clear_pads(y0, MID)
    near, far = 7 - 7 * par, 7 * par
    body = pl.ds(PAD, MID)
    for q in range(8):
        v = z1[(q - 2) // 2 + 3, pl.ds(PAD + 12, MID // 2), :]
        x0[q, pl.ds(PAD, MID // 2, 2), :] = v
        x0[q, pl.ds(PAD + 1, MID // 2, 2), :] = v
        if 0 < q < 7:
            x0[q, body, :] += pre0[q - 1]
    x0[near, body, :] += sw[pl.ds(O_EDGE, MID), :]
    x0[far, body, :] += xs[pl.ds(5 * R1, MID), :]
    off = Q0 - 2
    sweep(x0, None, c0, w0, 1, 7, (0, MID), 1, 0, into(y0), 40, woff=off, coff=off, wr=MID0, cr=MID0, unroll=6)

    def finish(q, r0, n, v):
        out[q - 2, pl.ds(r0 - 8, n), :] = v

    sweep(y0, x0, c0, w0, 2, 6, (8, 8 + PY), 1, 1, finish, 32, woff=off, coff=off, wr=MID0, cr=MID0, unroll=4)


def swap(v):
    return lax.ppermute(v, "wide", [(i, i ^ 1) for i in range(lax.axis_size("wide"))])


def across(v, chips, ends=()):
    count = lax.axis_size("wide")
    step = 2 * chips - 1
    pairs = [(i, i + step) for i in range(1, count, 2) if i + step < count]
    pairs += [(i, i - step) for i in range(0, count, 2) if i - step >= 0]
    return lax.ppermute(v, "wide", pairs + list(ends))


def from_beside(v):
    count = lax.axis_size("wide")
    pairs = [(i, i + 2) for i in range(0, count - 2, 2)] + [(i, i - 2) for i in range(3, count, 2)]
    return lax.ppermute(v, "wide", pairs)


def along_narrow(v, step):
    wide, narrow = lax.axis_size("wide"), lax.axis_size("narrow")
    pairs = []
    for i in range(wide):
        to = step if i % 2 == 0 else -step
        pairs += [(i * narrow + j, i * narrow + j + to) for j in range(narrow) if 0 <= j + to < narrow]
    return lax.ppermute(v, ("wide", "narrow"), pairs)


def shards(right_side, alpha_coef, beta_x, beta_y, beta_z):
    a, y1, y2 = call(
        pack_kernel, "pack", (shape(5, PX, PY, PZ), shape(5 * PX * HY, PZ), shape(5 * PX * HY, PZ)),
        (VMEM,) * 3, [ANY] * 5, [pltpu.SemaphoreType.DMA((5,))], SMALL,
    )(*[pltpu.with_memory_space_constraint(v, pltpu.HBM) for v in (right_side, alpha_coef, beta_x, beta_y, beta_z)])
    y1, y2 = along_narrow(y1, 1), along_narrow(y2, -1)
    ex, inner, own = call(
        inner_kernel, "inner_rows", (shape(EX_IN + 3 * INNER, PZ), shape(2, 3 * INNER, PZ), shape(RAW + 4 * R1, PZ)),
        (VMEM,) * 3, [VMEM],
        [scratch(3, PY + 2 * PAD, PZ)], LARGE,
    )(a)
    ex = across(ex, 1)
    own, sw, xs = call(
        corner_kernel, "corners", (shape(RAW + 4 * R1, PZ), shape(SRAW + 4 * R1, PZ), shape(XB + R1, PZ)),
        (VMEM,) * 3, [VMEM] * 4 + [ANY], [scratch(2, 3, EDGE + 8 + 2 * PAD, PZ), scratch(2, 6 * EDGE, PZ)], SMALL, aliases={0: 0},
    )(own, y1, y2, inner, first_to_arrive(y1, y2))
    xs = across(xs, 1)
    sw = swap(sw)

    send, send1, send2, edge0, pre0, w0, c0 = call(
        fine_kernel, "level0_pre",
        (shape(5 * R1 + MID, PZ), shape(5 * R1, PZ), shape(2 * R1, PZ), shape(MID, PZ), shape(6, MID, PZ),
         shape(6, 10, EY, PZ), shape(10, EY, PZ)),
        (VMEM,) * 7, [VMEM] * 4 + [ANY],
        [scratch(10, EY, PZ), scratch(10, EY, PZ)] + [scratch(10, EY + 2 * PAD, PZ)] * 3
        + [scratch(2, EY, PZ), scratch(4, 5, R1, PZ), scratch(R1 + PAD, PZ), scratch(8, EY, PZ)],
        LARGE,
    )(own, sw, xs, ex, first_to_arrive(xs, first_to_arrive(ex)))

    one = across(send, 1)
    beside = from_beside(send1)
    two = across(send2, 2)
    mine = call(join_kernel, "join", shape(O_END, PZ), VMEM, [VMEM] * 5, [], SMALL)(send, edge0, one, beside, two)
    its = swap(mine)
    w1_shapes = (shape(*S_SHAPE), shape(6, N1, R1, PZ), shape(N1, R1, PZ), shape(N1, R1, PZ))
    s1, w1, inv1, d1 = call(
        near_coefficients_kernel, "near_coefficients", w1_shapes, (VMEM,) * 4, [VMEM] * 4, [], LARGE,
    )(own[RAW:], sw[SRAW:], one, beside)

    edge, c1, pre1, rhs2, s1, w1, _, _ = call(
        middle_kernel, "level1_pre",
        (shape(2 * R2, PZ), shape(N1, R1, PZ), shape(10, R1, PZ), shape(4, R2, PZ)) + w1_shapes,
        (VMEM,) * 8, [VMEM] * 9,
        [scratch(N1, R1 + 2 * PAD, PZ)] * 3 + [scratch(4, R1, PZ), scratch(2, R2 + PAD, PZ)],
        LARGE, aliases={5: 4, 6: 5, 7: 6, 8: 7},
    )(send, one, beside, two, its, s1, w1, inv1, d1)

    w2, inv2, last2 = call(
        coarse_coefficients_kernel, "level2_coefficients",
        (shape(6, 12, R2, PZ), shape(12, R2, PZ), shape(4, R2 + PAD, PZ)),
        (VMEM,) * 3, [VMEM] * 3, [scratch(4, 10, R2 + PAD, PZ)], LARGE,
    )(s1, two, its)
    count = lax.axis_size("wide")
    two2 = across(edge, 2, ((0, 2), (count - 1, count - 3)))
    its2 = swap(two2)
    return call(
        last_kernel, "coarse_and_post", shape(PX, PY, PZ), VMEM, [VMEM] * 14,
        [scratch(6, 1, R2, PZ), scratch(12, R2, PZ)] + [scratch(12, R2 + 2 * PAD, PZ)] * 3
        + [scratch(8, R1 + 2 * PAD, PZ)] * 3 + [scratch(8, MID + 2 * PAD, PZ)] * 2,
        LARGE,
    )(two2, its2, rhs2, w2, inv2, last2, pre1, w1, c1, pre0, its, one, w0, c0)


def solution(mesh):
    spec = P("wide", "narrow", None)
    return jax.shard_map(shards, mesh=mesh, in_specs=(spec,) * 5, out_specs=spec, check_vma=False)
```

```python
import jax
import jax.numpy as jnp
from jax import lax
from jax.experimental import pallas as pl
from jax.experimental.pallas import tpu as pltpu
from jax.sharding import PartitionSpec as P

F32 = jnp.float32
THETA = (2.0 + 0.25) / 2.0
DELTA = (2.0 - 0.25) / 2.0
SIGMA = THETA / DELTA
RHO = [1.0 / SIGMA]
for _step in range(3):
    RHO.append(1.0 / (2.0 * SIGMA - RHO[-1]))
MOMENTUM = [0.0] + [RHO[k] * RHO[k - 1] for k in range(1, 4)]
GAIN = [1.0 / THETA] + [2.0 * RHO[k] / DELTA for k in range(1, 4)]

PX, PY, PZ = 4, 64, 128
HY = 32
EY = PY + 2 * HY
MID = PY + 16
MID0 = HY - 8
R1 = EY // 2
R2 = R1 // 2
RAW = 5 * PX * EY
SRAW = 8 * EY
XP = 5 * 2 * HY
INNER, EDGE = PY - 16, HY + 8
XB = XP + 3 * 2 * EDGE
EX_IN = 5 * PY
H1 = PY // 2
G1 = (R1 - H1) // 2
EX_RAW = EX_IN + 3 * INNER
A_EDGE = R1 + 8 * G1
PAD = 8
SMALL, LARGE = 1000, 2 * 10**10
B, ALPHA, BX, BY, BZ = range(5)
ANY = pl.BlockSpec(memory_space=pl.ANY)
VMEM = pl.BlockSpec(memory_space=pltpu.VMEM)
HBM = pl.BlockSpec(memory_space=pltpu.HBM)


def shape(*dims):
    return jax.ShapeDtypeStruct(dims, F32)


def scratch(*dims):
    return pltpu.VMEM(dims, F32)


def call(kernel, name, out_shape, out_specs, in_specs, scratch_shapes, flops, mib=24, aliases=None):
    return pl.pallas_call(
        kernel,
        out_shape=out_shape,
        in_specs=in_specs,
        out_specs=out_specs,
        scratch_shapes=scratch_shapes,
        compiler_params=pltpu.CompilerParams(vmem_limit_bytes=mib * 1024 * 1024),
        cost_estimate=pl.CostEstimate(flops=flops, bytes_accessed=0, transcendentals=0),
        input_output_aliases=aliases or {},
        name=name,
    )


def parity():
    return lax.rem(lax.axis_index("wide"), 2)


def lanes(rows):
    return lax.broadcasted_iota(jnp.int32, (rows, PZ), 1)


def moved(v, shift):
    return pltpu.roll(v, shift % PZ, 1)


def planes(lo, hi, each, unroll):
    if not unroll:
        each(lo)
        return
    steps = (hi - lo) // unroll

    def body(i, carry):
        for k in range(unroll):
            each(lo + i * unroll + k)
        return carry

    if steps > 1:
        lax.fori_loop(0, steps, body, 0)
    else:
        steps = 0
    for q in range(lo + steps * unroll, hi):
        each(q)


def defect(x_ref, c_ref, w_ref, q, r0, n, reach, cq, cr, wq, wr):
    rows = pl.ds(PAD + r0, n)
    here = pl.ds(wr + r0, n)
    x = x_ref[q, rows, :]
    total = c_ref[cq, pl.ds(cr + r0, n), :] - x
    total += w_ref[0, wq, here, :] * x_ref[q - 1, rows, :]
    total += w_ref[1, wq, here, :] * x_ref[q + 1, rows, :]
    total += w_ref[2, wq, here, :] * x_ref[q, pl.ds(PAD + r0 - 1, n), :]
    total += w_ref[3, wq, here, :] * x_ref[q, pl.ds(PAD + r0 + 1, n), :]
    total += w_ref[4, wq, here, :] * moved(x, reach)
    total += w_ref[5, wq, here, :] * moved(x, -reach)
    return x, total


def sweep(x_ref, prev_ref, c_ref, w_ref, lo, hi, rows, reach, k, store, chunk, woff=0, coff=0, wr=0, cr=0, unroll=8):
    def each(q):
        for r0 in range(rows[0], rows[1], chunk):
            n = min(chunk, rows[1] - r0)
            x, z = defect(x_ref, c_ref, w_ref, q, r0, n, reach, q + coff, cr, q + woff, wr)
            new = x + GAIN[k] * z
            if k > 0:
                gap = x if prev_ref is None else x - prev_ref[q, pl.ds(PAD + r0, n), :]
                new += MOMENTUM[k] * gap
            store(q, r0, n, new)

    planes(lo, hi, each, unroll)


def into(ref):
    def store(q, r0, n, v):
        ref[q, pl.ds(PAD + r0, n), :] = v

    return store


def inverse(d):
    inside = d > 0.0
    return jnp.where(inside, 1.0 / jnp.where(inside, d, 1.0), 0.0)


def faces(alpha, x0, x1, y0, y1, z0, reach, scale):
    z1 = moved(z0, -reach)
    d = alpha + scale * (x0 + x1 + y0 + y1 + z0 + z1)
    inv = inverse(d)
    si = scale * inv
    return d, inv, [si * f for f in (x0, x1, y0, y1, z0, z1)]


def next_rows(load, r0, n, rows):
    if r0 + n < rows:
        return load(r0 + 1, n)
    return pltpu.roll(load(r0, n), n - 1, 0)


def clear_pads(ref, rows):
    ref[:, :PAD, :] = jnp.zeros((ref.shape[0], PAD, PZ), F32)
    ref[:, PAD + rows :, :] = jnp.zeros((ref.shape[0], PAD, PZ), F32)


def pair_lanes(v, reach):
    low = (lanes(v.shape[0]) & reach) == 0
    return v + jnp.where(low, moved(v, -reach), moved(v, reach))


def low_lanes(v, reach):
    low = (lanes(v.shape[0]) & reach) == 0
    return jnp.where(low, v, moved(v, reach))


def pack2(v0, v1):
    return jnp.where((lanes(v0.shape[0]) & 1) == 0, v0, v1)


def unpack2(v):
    even = (lanes(v.shape[0]) & 1) == 0
    return jnp.where(even, v, moved(v, 1)), jnp.where(even, moved(v, -1), v)


def pack4(items):
    place = lanes(items[0].shape[0]) & 3
    out = items[0]
    for i, item in enumerate(items[1:], 1):
        out = jnp.where(place == i, item, out)
    return out


def unpack4(v, i):
    place = lanes(v.shape[0]) & 3
    out = v
    for m in range(4):
        if m != i:
            out = jnp.where(place == m, moved(v, m - i), out)
    return out


def coarser(load, rows, reach):
    def cell(i):
        return load(i, 0, 0) + load(i, 0, 1) + load(i, 1, 0) + load(i, 1, 1)

    al = pair_lanes(cell(0), reach) * 0.125
    bx = pair_lanes(load(1, 0, 0) + load(1, 0, 1), reach) * 0.25
    by = pair_lanes(load(2, 0, 0) + load(2, 1, 0), reach) * 0.25
    bz = low_lanes(cell(3), reach) * 0.25
    return al, bx, by, bz


def pack_kernel(b, al, bx, by, bz, a, one_out, two_out, sems):
    wide, narrow = lax.axis_index("wide"), lax.axis_index("narrow")
    par = lax.rem(wide, 2)
    copies = [pltpu.make_async_copy(ref, a.at[i], sems.at[i]) for i, ref in enumerate((b, al, bx, by, bz))]
    for c in copies:
        c.start()
    for c in copies:
        c.wait()
    row = lax.broadcasted_iota(jnp.int32, (PAD, PZ), 0)
    first_row = jnp.logical_and(row == 0, jnp.broadcast_to(narrow, (PAD, PZ)) == 0)
    a[BX, 0] = jnp.where(jnp.broadcast_to(wide, (PY, PZ)) == 0, 0.0, a[BX, 0])
    first_z = lanes(PY) == 0
    for p in range(PX):
        a[BY, p, :PAD] = jnp.where(first_row, 0.0, a[BY, p, :PAD])
        a[BZ, p] = jnp.where(first_z, 0.0, a[BZ, p])
    for i in range(5):
        for p in range(PX):
            here = pl.ds((PX * i + p) * HY, HY)
            one_out[here, :] = a[i, p, pl.ds(pl.multiple_of((1 - par) * (PY - HY), 8), HY), :]
            two_out[here, :] = a[i, p, pl.ds(pl.multiple_of(par * (PY - HY), 8), HY), :]


def plane(ref, k, r0=0, n=EY):
    start = k * EY + r0
    return ref[pl.ds(pl.multiple_of(start, 8) if r0 % 8 == 0 else start, n), :]


def second_planes(get, rows, x, keep):
    clear_pads(x, rows)
    body = pl.ds(PAD, rows)
    kept = []
    for p in range(3):
        by = get(BY, p)
        _, inv, w = faces(
            get(ALPHA, p), get(BX, p), get(BX, p + 1), by, pltpu.roll(by, rows - 1, 0), get(BZ, p), 1, 1.0
        )
        c0 = inv * get(B, p)
        x[p, body, :] = c0 * (1.0 / THETA)
        kept.append((w, c0))
    for up in range(2):
        second = 1 + up
        w, c0 = kept[second]
        here = x[second, body, :]
        z = c0 - here + w[0] * x[second - 1, body, :]
        if not up:
            z += w[1] * x[2, body, :]
        z += w[2] * x[second, pl.ds(PAD - 1, rows), :] + w[3] * x[second, pl.ds(PAD + 1, rows), :]
        z += w[4] * moved(here, 1) + w[5] * moved(here, -1)
        keep(up, 0, here)
        keep(up, 1, here + GAIN[1] * z + MOMENTUM[1] * here)
        keep(up, 2, w[1] if up else get(BX, second))


def inner_kernel(a, ex, v, own, x):
    par = parity()

    def keep(up, k, value):
        v[up, pl.ds(INNER * k, INNER), :] = value[8 : 8 + INNER]

    second_planes(lambda i, p: a[i, p], PY, x, keep)
    for i in range(5):
        ex[pl.ds(i * PY, PY), :] = a[i, 3 * par]
    ex[pl.ds(EX_IN, 3 * INNER), :] = v[par]
    for i in range(5):
        for p in range(PX):
            own[pl.ds((PX * i + p) * EY + HY, PY), :] = a[i, p]
    got = []
    for c in range(2):

        def load(i, k, row):
            return a[i + 1, 2 * c + k, pl.ds(row, H1, 2), :]

        got.append(coarser(load, H1, 1))
    for i in range(4):
        t = pack2(got[0][i], got[1][i])
        own[pl.ds(RAW + R1 * i + G1, H1), :] = t
        ex[pl.ds(EX_RAW + H1 * i, H1), :] = t


def corner_kernel(own_in, one, two, inner, _, own, sw, xs, x, v):
    par = parity()
    for i in range(5):
        for p in range(PX):
            k = PX * i + p
            here = pl.ds(k * HY, HY)
            own[pl.ds(pl.multiple_of(k * EY + par * (HY + PY), 8), HY), :] = one[here, :]
            own[pl.ds(pl.multiple_of(k * EY + (1 - par) * (HY + PY), 8), HY), :] = two[here, :]
    for r0, r1 in ((0, 0), (HY + PY, G1 + H1)):
        got = []
        for c in range(2):

            def load(i, k, row):
                return own[pl.ds((PX * (i + 1) + 2 * c + k) * EY + r0 + row, G1, 2), :]

            got.append(coarser(load, G1, 1))
        for i in range(4):
            own[pl.ds(RAW + R1 * i + r1, G1), :] = pack2(got[0][i], got[1][i])
    sw[pl.ds(SRAW, 4 * R1), :] = own[pl.ds(RAW, 4 * R1), :]
    xs[pl.ds(XB, R1), :] = own[pl.ds(RAW + R1, R1), :]
    for i in range(5):
        xs[pl.ds(2 * HY * i, HY), :] = plane(own, PX * i + 3 * par, 0, HY)
        xs[pl.ds(2 * HY * i + HY, HY), :] = plane(own, PX * i + 3 * par, HY + PY, HY)
        sw[pl.ds(i * EY, EY), :] = plane(own, PX * i + 3 - 3 * par)
    span = EDGE + 8
    for side, r0 in ((0, 0), (1, EY - span)):

        def keep(up, k, value):
            v[up, pl.ds((2 * k + side) * EDGE, EDGE), :] = value[8 * side : 8 * side + EDGE]

        second_planes(lambda i, p: plane(own, PX * i + p, r0, span), span, x.at[side], keep)
    xs[pl.ds(XP, 6 * EDGE), :] = v[par]
    for k in range(3):
        base = (5 + k) * EY
        sw[pl.ds(base, EDGE), :] = v[1 - par, pl.ds(2 * k * EDGE, EDGE), :]
        sw[pl.ds(base + EDGE, INNER), :] = inner[1 - par, pl.ds(k * INNER, INNER), :]
        sw[pl.ds(base + EDGE + INNER, EDGE), :] = v[1 - par, pl.ds((2 * k + 1) * EDGE, EDGE), :]


Q0 = 3


def fine_kernel(own, sw, xs, ex, _, send, send1, send2, edge, pre, w, cc, sx, d, x, y, z, t, s, u, sf):
    par = parity()
    for i in range(5):
        sf[i, :HY] = xs[pl.ds(2 * HY * i, HY), :]
        sf[i, HY : HY + PY] = ex[pl.ds(PY * i, PY), :]
        sf[i, HY + PY :] = xs[pl.ds(2 * HY * i + HY, HY), :]

    for k in range(3):
        sf[5 + k, :EDGE] = xs[pl.ds(XP + 2 * k * EDGE, EDGE), :]
        sf[5 + k, EDGE : EDGE + INNER] = ex[pl.ds(EX_IN + k * INNER, INNER), :]
        sf[5 + k, EDGE + INNER :] = xs[pl.ds(XP + (2 * k + 1) * EDGE, EDGE), :]

    def far(i, r, n):
        return sf[i, pl.ds(r, n), :]

    def near(i, r, n):
        return plane(sw, i, r, n)

    sides2 = ((far, par), (near, 1 - par))
    for i in range(4):
        for p, ref, base in ((par, own, RAW), (1 - par, sw, SRAW)):
            v0, v1 = unpack2(ref[pl.ds(base + R1 * i, R1), :])
            s[i, 2 * p] = v0
            s[i, 2 * p + 1] = v1
    s[1, 4] = unpack2(xs[pl.ds(XB, R1), :])[0]
    for p in range(PX):
        sx[Q0 + p] = plane(own, PX * BX + p)
    for get, above in sides2:
        sx[2 + 5 * above] = get(BX, 0, EY)
        sx[9 - above] = get(7, 0, EY)
    clear_pads(x, EY)
    clear_pads(y, EY)
    chunk = 32

    def prepare(q, get):
        for r0 in range(0, EY, chunk):
            here = pl.ds(r0, chunk)

            def load(i):
                return lambda r, n: get(i, r, n)

            dd, inv, w6 = faces(
                load(ALPHA)(r0, chunk), sx[q, here, :], sx[q + 1, here, :], load(BY)(r0, chunk),
                next_rows(load(BY), r0, chunk, EY), load(BZ)(r0, chunk), 1, 1.0,
            )
            for a, f in enumerate(w6):
                w[a, q, here, :] = f
            c0 = inv * load(B)(r0, chunk)
            cc[q, here, :] = c0
            x[q, pl.ds(PAD + r0, chunk), :] = c0 * (1.0 / THETA)
            d[q, here, :] = dd

    for p in range(PX):
        prepare(Q0 + p, lambda i, r, n: plane(own, PX * i + p, r, n))
    body = pl.ds(PAD, EY)
    for get, above in sides2:
        q = 2 + 5 * above
        prepare(q, get)
        x[1 + 7 * above, body, :] = get(5, 0, EY)
        missing = GAIN[1] * get(7, 0, EY) * x[q, body, :]
        below = jnp.broadcast_to(above, missing.shape) == 0
        y[1 + 7 * above, body, :] = get(6, 0, EY) + jnp.where(below, missing, 0.0)

    rows = (0, EY)
    sweep(x, None, cc, w, 2, 8, rows, 1, 1, into(y), chunk)
    sweep(y, x, cc, w, 2, 8, rows, 1, 2, into(z), chunk)
    got = []
    for c in range(2):
        for r0 in range(0, EY, chunk):
            v = 0.0
            for q in (Q0 + 2 * c, Q0 + 2 * c + 1):
                _, zz = defect(z, cc, w, q, r0, chunk, 1, q, 0, q, 0)
                v = v + d[q, pl.ds(r0, chunk), :] * zz
            t[c, pl.ds(r0, chunk), :] = v
        got.append(pair_lanes(t[c, pl.ds(0, R1, 2), :] + t[c, pl.ds(1, R1, 2), :], 1) * 0.125)
    mid = pl.ds(PAD + MID0, MID)
    rhs = pack2(got[0], got[1])
    send[:R1] = rhs
    send1[:R1] = rhs
    send1[pl.ds(R1, 4 * R1), :] = own[pl.ds(RAW, 4 * R1), :]
    for i in range(4):
        send[pl.ds(R1 + 2 * G1 * i, G1), :] = own[pl.ds(RAW + R1 * i, G1), :]
        send[pl.ds(R1 + 2 * G1 * i + G1, G1), :] = own[pl.ds(RAW + R1 * i + G1 + H1, G1), :]
    edge[...] = z[Q0 + 2 - par, mid, :]
    send[pl.ds(A_EDGE, MID), :] = z[Q0 + 1 + par, mid, :]
    q = 3 * par
    u[:R1] = s[2, q]
    u[R1:] = jnp.zeros((PAD, PZ), F32)
    _, inv, _ = faces(s[0, q], s[1, q], s[1, q + 1], u[:R1], u[pl.ds(1, R1), :], s[3, q], 2, 0.25)
    x1 = inv * jnp.where(jnp.broadcast_to(par, rhs.shape) == 0, *unpack2(rhs)) * (1.0 / THETA)
    send2[:R1] = pack2(x1, s[1, q])
    for c in range(2):

        def load(i, k, row):
            return s[i, 2 * c + k, pl.ds(row, R2, 2), :]

        send2[pl.ds(R1 + R2 * c, R2), :] = pack4(coarser(load, R2, 2))
    for p in range(6):
        pre[p] = z[Q0 - 1 + p, mid, :]


C0 = 5
N1 = 14
M0 = 5
S_SHAPE = (4, N1, R1 + 2 * PAD, PZ)
O_EDGE = R1
O_ONE = O_EDGE + MID
O_BESIDE = O_ONE + R1
O_TWO = O_BESIDE + R1
O_RAW = O_TWO + 2 * R1
O_END = O_RAW + 8 * R1


def place_coefficients(s, i, e, v):
    v0, v1 = unpack2(v)
    s[i, 1 + 2 * e, pl.ds(PAD, R1), :] = v0
    s[i, 2 + 2 * e, pl.ds(PAD, R1), :] = v1


def middle_faces(s, w1, inv1, d1, q):
    for r0 in range(0, R1, 32):
        here, up, out = pl.ds(PAD + r0, 32), pl.ds(PAD + r0 + 1, 32), pl.ds(r0, 32)
        dd, inv, w6 = faces(
            s[0, q, here, :], s[1, q, here, :], s[1, q + 1, here, :], s[2, q, here, :], s[2, q, up, :],
            s[3, q, here, :], 2, 0.25,
        )
        for a, f in enumerate(w6):
            w1[a, q, out, :] = f
        inv1[q, out, :] = inv
        d1[q, out, :] = dd


def sides(par, k):
    lower, upper = 1 - k, 4 + k
    return jnp.where(par == 0, lower, upper), jnp.where(par == 0, upper, lower)


def level2_load(s, plane):
    def load(i, k, row):
        return s[i, 2 * plane + C0 + k, pl.ds(PAD + row, R2, 2), :]

    return load


def across_coefficients(one, ex, i):
    base = R1 + 2 * G1 * i
    return jnp.concatenate([one[pl.ds(base, G1), :], ex[pl.ds(EX_RAW + H1 * i, H1), :], one[pl.ds(base + G1, G1), :]], 0)


def near_coefficients_kernel(own, other, one, ex, beside, s, w1, inv1, d1):
    par = parity()
    for i in range(4):
        s[i, :, PAD + R1 :, :] = jnp.zeros((N1, PAD, PZ), F32)
        rows = pl.ds(R1 * i, R1)
        sent = pl.ds(R1 * (1 + i), R1)
        place_coefficients(s, i, 2 + par, own[rows, :])
        place_coefficients(s, i, 3 - par, other[rows, :])
        place_coefficients(s, i, sides(par, 0)[0], across_coefficients(one, ex, i))
        place_coefficients(s, i, sides(par, 1)[0], beside[sent, :])
    for k in range(7):
        middle_faces(s, w1, inv1, d1, 1 + 4 * par + k)


def join_kernel(own, edge, one, ex, beside, two, out):
    out[:R1] = own[:R1]
    out[pl.ds(O_EDGE, MID), :] = edge[...]
    out[pl.ds(O_ONE, R1), :] = one[:R1]
    out[pl.ds(O_BESIDE, R1), :] = beside[:R1]
    out[pl.ds(O_TWO, 2 * R1), :] = two[...]
    for i in range(4):
        out[pl.ds(O_RAW + R1 * i, R1), :] = across_coefficients(one, ex, i)
    out[pl.ds(O_RAW + 4 * R1, 4 * R1), :] = beside[pl.ds(R1, 4 * R1), :]


def tick_kernel(*refs):
    refs[-1][...] = jnp.zeros(refs[-1].shape, F32)


def first_to_arrive(*values):
    return call(tick_kernel, "tick", shape(PAD, PZ), VMEM, [ANY] * len(values), [], LARGE)(*values)


def both_sides(par, mine, its):
    upper = jnp.broadcast_to(par, mine.shape) == 1
    return jnp.where(upper, its, mine), jnp.where(upper, mine, its)


def middle_kernel(own, one, beside, two, its, s_in, w_in, inv_in, d_in, edge, cc, pre, rhs, s, w, inv, d,
                  x, y, z, t, u):
    par = parity()
    clear_pads(x, R1)
    clear_pads(y, R1)
    body = pl.ds(PAD, R1)
    lower, upper = both_sides(par, two[:R1], its[pl.ds(O_TWO, R1), :])
    x[0, body, :] = unpack2(lower)[0]
    x1, bx = unpack2(upper)
    x[N1 - 1, body, :] = x1
    s[1, N1 - 1, body, :] = bx
    for k in range(2):
        e = sides(par, k)[1]
        for i in range(4):
            place_coefficients(s, i, e, its[pl.ds(O_RAW + (4 * k + i) * R1, R1), :])
    for k in range(5):
        middle_faces(s, w, inv, d, jnp.where(par == 0, 8 + k, 1 + k if k < 4 else 12))

    def place(e, v):
        for k, b in enumerate(unpack2(v)):
            q = 1 + 2 * e + k
            c0 = inv[q] * b
            cc[q] = c0
            x[q, body, :] = c0 * (1.0 / THETA)

    place(2 + par, own[:R1])
    place(3 - par, its[:R1])
    for k, ref, row in ((0, one, O_ONE), (1, beside, O_BESIDE)):
        e, f = sides(par, k)
        place(e, ref[:R1])
        place(f, its[pl.ds(row, R1), :])

    rows = (0, R1)
    sweep(x, None, cc, w, 1, 13, rows, 2, 1, into(y), 32, unroll=12)
    sweep(y, x, cc, w, 2, 12, rows, 2, 2, into(z), 32, unroll=10)

    for c in range(4):
        for r0 in range(0, R1, 32):
            v = 0.0
            for k in range(2):
                q = C0 - 2 + 2 * c + k
                _, zz = defect(z, cc, w, q, r0, 32, 2, q, 0, q, 0)
                v = v + d[q, pl.ds(r0, 32), :] * zz
            t[c, pl.ds(r0, 32), :] = v
        rhs[c] = pair_lanes(t[c, pl.ds(0, R2, 2), :] + t[c, pl.ds(1, R2, 2), :], 2) * 0.125

    def first(k, plane):
        al, bx, by, bz = coarser(level2_load(s, plane), R2, 2)
        after = level2_load(s, plane + 1)
        bx1 = pair_lanes(after(1, 0, 0) + after(1, 0, 1), 2) * 0.25
        u[k, pl.ds(0, R2), :] = by
        u[k, pl.ds(R2, PAD), :] = jnp.zeros((PAD, PZ), F32)
        _, inv2, _ = faces(al, bx, bx1, by, u[k, pl.ds(1, R2), :], bz, 4, 0.0625)
        return inv2 * rhs[plane + 1] * (1.0 / THETA), bx

    below, above = first(0, -1), first(1, 2)
    up = pack4([rhs[3], rhs[2], rhs[1], below[0]])
    down = pack4([rhs[0], rhs[1], rhs[2], above[0]])
    wide = jnp.broadcast_to(lax.axis_index("wide"), up.shape)
    ends = (lanes(R2) & 3) == 0
    down = jnp.where(wide == 0, jnp.where(ends, rhs[1], 0.0), down)
    up = jnp.where(wide == lax.axis_size("wide") - 1, jnp.where(ends, rhs[2], 0.0), up)
    edge[:R2] = jnp.where(jnp.broadcast_to(par, up.shape) == 0, down, up)
    edge[R2:] = above[1]
    for p in range(10):
        pre[p] = z[C0 - 3 + p, body, :]


def coarse_coefficients_kernel(s, two, its, w2, inv2, last, s2):
    par = parity()
    for c in range(2, 8):
        for i, v in enumerate(coarser(level2_load(s, c - 4), R2, 2)):
            s2[i, c, pl.ds(0, R2), :] = v
    for k in range(2):
        rows = pl.ds(R1 + R2 * k, R2)
        lower, upper = both_sides(par, two[rows, :], its[pl.ds(O_TWO + R1 + R2 * k, R2), :])
        for i in range(4):
            s2[i, k, pl.ds(0, R2), :] = unpack4(lower, i)
            s2[i, 8 + k, pl.ds(0, R2), :] = unpack4(upper, i)
    s2[2, :, R2:, :] = jnp.zeros((10, PAD, PZ), F32)
    body = pl.ds(0, R2)
    for c in range(9):
        _, inv, w6 = faces(
            s2[0, c, body, :], s2[1, c, body, :], s2[1, c + 1, body, :], s2[2, c, body, :], s2[2, c, pl.ds(1, R2), :],
            s2[3, c, body, :], 4, 0.0625,
        )
        for a, f in enumerate(w6):
            w2[a, c + 1] = f
        inv2[c + 1] = inv
    for i in range(4):
        last[i] = s2[i, 9]


def last_kernel(two2, its2, rhs, w2, inv2, last, pre1, w1, c1, pre0, sw, xs, w0, c0, out,
                wx, c2, x2, y2, z2, x1, y1, z1, x0, y0):
    par = parity()
    body = pl.ds(PAD, R2)
    lo, hi = both_sides(par, two2[:R2], its2[:R2])
    _, beyond = both_sides(par, two2[R2:], its2[R2:])
    clear_pads(x2, R2)
    clear_pads(y2, R2)
    clear_pads(z2, R2)
    _, inv, w6 = faces(
        last[0, :R2], last[1, :R2], beyond, last[2, :R2], last[2, pl.ds(1, R2), :], last[3, :R2], 4, 0.0625
    )
    for a, f in enumerate(w6):
        wx[a, 0] = f

    def start(j, b, dinv):
        v = dinv * b
        c2[j] = v
        x2[j, body, :] = v * (1.0 / THETA)

    for k in range(3):
        start(3 - k, unpack4(lo, k), inv2[3 - k])
        start(8 + k, unpack4(hi, k), inv2[8 + k] if k < 2 else inv)
    for c in range(4):
        start(c + 4, rhs[c], inv2[c + 4])
    x2[0, body, :] = unpack4(lo, 3)
    x2[11, body, :] = unpack4(hi, 3)
    rows = (0, R2)
    sweep(x2, None, c2, w2, 1, 10, rows, 4, 1, into(y2), R2, unroll=9)
    sweep(x2, None, c2, wx, 10, 11, rows, 4, 1, into(y2), R2, woff=-10)
    sweep(y2, x2, c2, w2, 2, 10, rows, 4, 2, into(z2), R2, unroll=8)
    sweep(z2, y2, c2, w2, 3, 9, rows, 4, 3, into(x2), R2, unroll=6)

    for q in range(8):
        v = x2[(q - 3) // 2 + M0 + par, body, :]
        z1[q, pl.ds(PAD, R2, 2), :] = v
        z1[q, pl.ds(PAD + 1, R2, 2), :] = v
        x1[q, pl.ds(PAD, R1), :] = pre1[q + 2 * par] + z1[q, pl.ds(PAD, R1), :]
    rows = (8, R1 - 8)
    off = C0 - 3 + 2 * par
    sweep(x1, None, c1, w1, 1, 7, rows, 2, 0, into(y1), 24, woff=off, coff=off, unroll=6)
    sweep(y1, x1, c1, w1, 2, 6, rows, 2, 1, into(z1), 24, woff=off, coff=off, unroll=4)

    clear_pads(x0, MID)
    clear_pads(y0, MID)
    near, far = 7 - 7 * par, 7 * par
    body = pl.ds(PAD, MID)
    for q in range(8):
        v = z1[(q - 2) // 2 + 3, pl.ds(PAD + 12, MID // 2), :]
        x0[q, pl.ds(PAD, MID // 2, 2), :] = v
        x0[q, pl.ds(PAD + 1, MID // 2, 2), :] = v
        if 0 < q < 7:
            x0[q, body, :] += pre0[q - 1]
    x0[near, body, :] += sw[pl.ds(O_EDGE, MID), :]
    x0[far, body, :] += xs[pl.ds(A_EDGE, MID), :]
    off = Q0 - 2
    sweep(x0, None, c0, w0, 1, 7, (0, MID), 1, 0, into(y0), 40, woff=off, coff=off, wr=MID0, cr=MID0, unroll=6)

    def finish(q, r0, n, v):
        out[q - 2, pl.ds(r0 - 8, n), :] = v

    sweep(y0, x0, c0, w0, 2, 6, (8, 8 + PY), 1, 1, finish, 32, woff=off, coff=off, wr=MID0, cr=MID0, unroll=4)


def swap(v):
    return lax.ppermute(v, "wide", [(i, i ^ 1) for i in range(lax.axis_size("wide"))])


def across(v, chips, ends=()):
    count = lax.axis_size("wide")
    step = 2 * chips - 1
    pairs = [(i, i + step) for i in range(1, count, 2) if i + step < count]
    pairs += [(i, i - step) for i in range(0, count, 2) if i - step >= 0]
    return lax.ppermute(v, "wide", pairs + list(ends))


def from_beside(v):
    count = lax.axis_size("wide")
    pairs = [(i, i + 2) for i in range(0, count - 2, 2)] + [(i, i - 2) for i in range(3, count, 2)]
    return lax.ppermute(v, "wide", pairs)


def along_narrow(v, step):
    wide, narrow = lax.axis_size("wide"), lax.axis_size("narrow")
    pairs = []
    for i in range(wide):
        to = step if i % 2 == 0 else -step
        pairs += [(i * narrow + j, i * narrow + j + to) for j in range(narrow) if 0 <= j + to < narrow]
    return lax.ppermute(v, ("wide", "narrow"), pairs)


def shards(right_side, alpha_coef, beta_x, beta_y, beta_z):
    a, y1, y2 = call(
        pack_kernel, "pack", (shape(5, PX, PY, PZ), shape(5 * PX * HY, PZ), shape(5 * PX * HY, PZ)),
        (VMEM,) * 3, [ANY] * 5, [pltpu.SemaphoreType.DMA((5,))], SMALL,
    )(*[pltpu.with_memory_space_constraint(v, pltpu.HBM) for v in (right_side, alpha_coef, beta_x, beta_y, beta_z)])
    y1, y2 = along_narrow(y1, 1), along_narrow(y2, -1)
    ex, inner, own = call(
        inner_kernel, "inner_rows", (shape(EX_RAW + 4 * H1, PZ), shape(2, 3 * INNER, PZ), shape(RAW + 4 * R1, PZ)),
        (VMEM,) * 3, [VMEM],
        [scratch(3, PY + 2 * PAD, PZ)], LARGE,
    )(a)
    ex = across(ex, 1)
    own, sw, xs = call(
        corner_kernel, "corners", (shape(RAW + 4 * R1, PZ), shape(SRAW + 4 * R1, PZ), shape(XB + R1, PZ)),
        (VMEM,) * 3, [VMEM] * 4 + [ANY], [scratch(2, 3, EDGE + 8 + 2 * PAD, PZ), scratch(2, 6 * EDGE, PZ)], SMALL, aliases={0: 0},
    )(own, y1, y2, inner, first_to_arrive(y1, y2))
    xs = across(xs, 1)
    sw = swap(sw)

    send, send1, send2, edge0, pre0, w0, c0 = call(
        fine_kernel, "level0_pre",
        (shape(A_EDGE + MID, PZ), shape(5 * R1, PZ), shape(2 * R1, PZ), shape(MID, PZ), shape(6, MID, PZ),
         shape(6, 10, EY, PZ), shape(10, EY, PZ)),
        (VMEM,) * 7, [VMEM] * 4 + [ANY],
        [scratch(10, EY, PZ), scratch(10, EY, PZ)] + [scratch(10, EY + 2 * PAD, PZ)] * 3
        + [scratch(2, EY, PZ), scratch(4, 5, R1, PZ), scratch(R1 + PAD, PZ), scratch(8, EY, PZ)],
        LARGE,
    )(own, sw, xs, ex, first_to_arrive(xs, first_to_arrive(ex)))

    one = across(send, 1)
    beside = from_beside(send1)
    two = across(send2, 2)
    mine = call(join_kernel, "join", shape(O_END, PZ), VMEM, [VMEM] * 6, [], SMALL)(
        send, edge0, one, ex, beside, two
    )
    its = swap(mine)
    w1_shapes = (shape(*S_SHAPE), shape(6, N1, R1, PZ), shape(N1, R1, PZ), shape(N1, R1, PZ))
    s1, w1, inv1, d1 = call(
        near_coefficients_kernel, "near_coefficients", w1_shapes, (VMEM,) * 4, [VMEM] * 5, [], LARGE,
    )(own[RAW:], sw[SRAW:], one, ex, beside)

    edge, c1, pre1, rhs2, s1, w1, _, _ = call(
        middle_kernel, "level1_pre",
        (shape(2 * R2, PZ), shape(N1, R1, PZ), shape(10, R1, PZ), shape(4, R2, PZ)) + w1_shapes,
        (VMEM,) * 8, [VMEM] * 9,
        [scratch(N1, R1 + 2 * PAD, PZ)] * 3 + [scratch(4, R1, PZ), scratch(2, R2 + PAD, PZ)],
        LARGE, aliases={5: 4, 6: 5, 7: 6, 8: 7},
    )(send, one, beside, two, its, s1, w1, inv1, d1)

    w2, inv2, last2 = call(
        coarse_coefficients_kernel, "level2_coefficients",
        (shape(6, 12, R2, PZ), shape(12, R2, PZ), shape(4, R2 + PAD, PZ)),
        (VMEM,) * 3, [VMEM] * 3, [scratch(4, 10, R2 + PAD, PZ)], LARGE,
    )(s1, two, its)
    count = lax.axis_size("wide")
    two2 = across(edge, 2, ((0, 2), (count - 1, count - 3)))
    its2 = swap(two2)
    return call(
        last_kernel, "coarse_and_post", shape(PX, PY, PZ), VMEM, [VMEM] * 14,
        [scratch(6, 1, R2, PZ), scratch(12, R2, PZ)] + [scratch(12, R2 + 2 * PAD, PZ)] * 3
        + [scratch(8, R1 + 2 * PAD, PZ)] * 3 + [scratch(8, MID + 2 * PAD, PZ)] * 2,
        LARGE,
    )(two2, its2, rhs2, w2, inv2, last2, pre1, w1, c1, pre0, its, one, w0, c0)


def solution(mesh):
    spec = P("wide", "narrow", None)
    return jax.shard_map(shards, mesh=mesh, in_specs=(spec,) * 5, out_specs=spec, check_vma=False)
```
